512 devices in a mesh: tm: 16 (over y_hi, z), space: 8 (over x, core), dp: 4 (over y_lo).
Axes of the slice: x: 4, y: 8 (y_hi: 2, y_lo: 4; y = y_hi * 4 + y_lo), z: 8, core: 2. Of those that a mesh axis runs over, the one named last changes fastest.
Arguments:
- time_query: bfloat16 [4, 128, 128, 768], P('dp', 'tm', 'space'), may hold values from -36 to 36
- time_key: bfloat16 [4, 128, 128, 768], P('dp', 'tm', 'space'), may hold values from -37 to 37
- time_value: bfloat16 [4, 128, 128, 768], P('dp', 'tm', 'space'), may hold values from -6 to 6
- residual_in: bfloat16 [4, 128, 128, 1024], P('dp', 'tm', 'space'), may hold values from -6 to 6
- fc_weight: bfloat16 [768, 1024], P(('tm', 'space')), may hold values from -0.21875 to 0.21875
- norm_gain: float32 [1024], replicated, may hold values from 0.25 to 1.75
- qkv_weight: bfloat16 [1024, 2304], P(('tm', 'space')), may hold values from -0.640625 to 0.640625
- out_weight: bfloat16 [768, 1024], P(('tm', 'space')), may hold values from -0.21875 to 0.21875
- bias_slope: float32 [12], replicated, may hold values from 0.01 to 0.3
- visible: int32 [4, 128], P('dp'), may hold values from 0 to 1023, as said below
- cotangent: bfloat16 [4, 128, 128, 1024], P('dp', 'tm', 'space'), may hold values from -6 to 6
Outputs:
- grad_residual: bfloat16 [4, 128, 128, 1024], P('dp', 'tm', 'space')
- grad_query: bfloat16 [4, 128, 128, 768], P('dp', 'tm', 'space')
- grad_key: bfloat16 [4, 128, 128, 768], P('dp', 'tm', 'space')
- grad_value: bfloat16 [4, 128, 128, 768], P('dp', 'tm', 'space')
The draws below stay inside these ranges and needn't reach their ends.
Inputs may be any that keep to these rules, and one draw needn't show every extreme that they name: `visible`: each clip's 128 entries are distinct positions of a 32 x 32 grid; the same for all time steps.
All inputs are finite; a program needn't handle non-finite values.
Results may differ from the reference program's by a relative error of at most 0.018.
Values may be sent and summed in bfloat16 or wider, within the bound.
No kernel may reach another device: no remote copies, remote signals or barrier semaphores. Data moves between devices by JAX's collectives and lax.ppermute only.
A program may use at most 64 MiB of HBM per device.

```python
import math
import jax
import jax.numpy as jnp
from jax import lax

D = 1024
HEADS = 12
HD = 64
INNER = 768
GRID = 32
T_SIZE = 128
S = 128
CLIPS = 4


def draw_time_query(key, part):
    key = jax.random.fold_in(key, 11)
    shape = (CLIPS, T_SIZE, S, INNER)
    entries = jnp.clip(jax.random.normal(key, shape, jnp.float32), -6.0, 6.0)
    return entries.astype(jnp.bfloat16)


def draw_time_key(key, part):
    key = jax.random.fold_in(key, 12)
    shape = (CLIPS, T_SIZE, S, INNER)
    entries = jnp.clip(jax.random.normal(key, shape, jnp.float32), -6.0, 6.0)
    return entries.astype(jnp.bfloat16)


def draw_qkv_weight(key, part):
    key = jax.random.fold_in(key, 13)
    shape = (D, 3 * INNER)
    entries = jnp.clip(jax.random.normal(key, shape, jnp.float32), -6.0, 6.0) / D ** 0.5
    return entries.astype(jnp.bfloat16)


def draw_visible(key, part):
    key = jax.random.fold_in(key, 21)
    middle = GRID * GRID - 2

    def one_clip(clip_key):
        order = jax.random.permutation(clip_key, middle).astype(jnp.int32) + 1
        ends = jnp.array([0, GRID * GRID - 1], jnp.int32)
        chosen = jnp.concatenate([ends, order[:S - 2]])
        return jax.random.permutation(jax.random.fold_in(clip_key, 5), chosen)
    clip_keys = jax.random.split(key, CLIPS)
    return jax.vmap(one_clip)(clip_keys).astype(jnp.int32)


def block_levels(own_key, shape, cuts, least, high):
    def one(axis_at, blocks):
        draws = jax.random.uniform(jax.random.fold_in(jax.random.fold_in(own_key, 6), axis_at), (blocks,), jnp.float32, least / len(cuts), high / len(cuts))
        return jnp.repeat(jnp.exp(draws), shape[axis_at] // blocks).reshape((-1,) + (1,) * (len(shape) - axis_at - 1))

    gain = one(*cuts[0])
    for cut in cuts[1:]:
        gain = gain * one(*cut)
    return gain


def scatter_about(own_key, extent, deviation, bound, cuts=(), dtype=jnp.bfloat16):
    values = deviation * jax.random.normal(own_key, extent, jnp.float32)
    if cuts:
        values = values * block_levels(own_key, extent, cuts, -0.22, 0.18)
    return jnp.clip(values, -bound, bound).astype(dtype)


def setup_inputs(seed: int = 0) -> dict:
    seeds = jax.random.split(jax.random.key(seed), 12)
    time_query = draw_time_query(jax.random.fold_in(seeds[11], 71), 0)
    time_key = draw_time_key(jax.random.fold_in(seeds[11], 71), 0)
    time_value = scatter_about(seeds[2], (CLIPS, T_SIZE, S, INNER), 1.0, 6.0, ((0, 4), (1, 16), (2, 8)))
    residual_in = scatter_about(seeds[3], (CLIPS, T_SIZE, S, D), 1.0, 6.0, ((0, 4), (1, 16), (2, 8)))
    fc_weight = scatter_about(seeds[4], (INNER, D), INNER ** -0.5, 0.21875, ((0, 128),))
    norm_gain = jnp.clip(1.0 + 0.15 * jax.random.normal(seeds[5], (D,), jnp.float32), 0.25, 1.75)
    qkv_weight = draw_qkv_weight(jax.random.fold_in(seeds[11], 71), 0)
    out_weight = scatter_about(seeds[7], (INNER, D), INNER ** -0.5, 0.21875, ((0, 128),))
    bias_slope = jnp.clip(jnp.exp(jax.random.uniform(seeds[8], (HEADS,), jnp.float32, math.log(0.01), math.log(0.3))), 0.01, 0.3)
    visible = draw_visible(jax.random.fold_in(seeds[11], 71), 0)
    cotangent = scatter_about(seeds[10], (CLIPS, T_SIZE, S, D), 1.0, 6.0, ((0, 4), (1, 16), (2, 8)))
    return dict(time_query=time_query, time_key=time_key, time_value=time_value, residual_in=residual_in, fc_weight=fc_weight, norm_gain=norm_gain, qkv_weight=qkv_weight, out_weight=out_weight, bias_slope=bias_slope, visible=visible, cotangent=cotangent)


epsilon = 1e-05

def rounded(values):
    return lax.optimization_barrier(values.astype(jnp.bfloat16)).astype(jnp.float32)

def split_heads(block):
    return block.reshape(block.shape[:-1] + (HEADS, HD)).astype(jnp.float32)

def softmax_rows(scores):
    row_top = lax.optimization_barrier(jnp.max(scores, axis=-1, keepdims=True))
    exponent = jnp.exp(scores - row_top)
    return exponent / lax.optimization_barrier(jnp.sum(exponent, axis=-1, keepdims=True))

def temporal_probs(queries, key_rows):
    scores = jnp.einsum('tshd,ushd->shtu', split_heads(queries), split_heads(key_rows)) * HD ** (-0.5)
    return softmax_rows(scores)

def temporal_forward(queries, key_rows, value_rows):
    attend = temporal_probs(queries, key_rows)
    mixed_out = jnp.einsum('shtu,ushd->tshd', rounded(attend), split_heads(value_rows))
    return mixed_out.reshape(queries.shape).astype(jnp.bfloat16)

def temporal_backward(queries, key_rows, value_rows, grad_out):
    attend = temporal_probs(queries, key_rows)
    grad_attend = jnp.einsum('tshd,ushd->shtu', split_heads(grad_out), split_heads(value_rows))
    inner_sum = lax.optimization_barrier(jnp.sum(attend * grad_attend, axis=-1, keepdims=True))
    grad_scores = rounded(attend * (grad_attend - inner_sum))
    score_scale = HD ** (-0.5)
    grad_q = jnp.einsum('shtu,ushd->tshd', grad_scores, split_heads(key_rows)) * score_scale
    grad_k = jnp.einsum('shtu,tshd->ushd', grad_scores, split_heads(queries)) * score_scale
    grad_v = jnp.einsum('shtu,tshd->ushd', rounded(attend), split_heads(grad_out))
    return (grad_q.reshape(queries.shape).astype(jnp.bfloat16), grad_k.reshape(queries.shape).astype(jnp.bfloat16), grad_v.reshape(queries.shape).astype(jnp.bfloat16))

def distance_bias(tube_ids, bias_slope):
    tube_rows = tube_ids // GRID
    tube_cols = tube_ids % GRID
    distance = jnp.abs(tube_rows[:, None] - tube_rows[None, :]) + jnp.abs(tube_cols[:, None] - tube_cols[None, :])
    return -bias_slope[:, None, None] * distance.astype(jnp.float32)[None]

def spatial_backward(queries, key_rows, value_rows, grad_out, pair_bias):
    score_scale = HD ** (-0.5)
    scores = jnp.einsum('tihd,tjhd->thij', split_heads(queries), split_heads(key_rows)) * score_scale
    attend = softmax_rows(scores + pair_bias[None])
    grad_attend = jnp.einsum('tihd,tjhd->thij', split_heads(grad_out), split_heads(value_rows))
    inner_sum = lax.optimization_barrier(jnp.sum(attend * grad_attend, axis=-1, keepdims=True))
    grad_scores = rounded(attend * (grad_attend - inner_sum))
    grad_q = jnp.einsum('thij,tjhd->tihd', grad_scores, split_heads(key_rows)) * score_scale
    grad_k = jnp.einsum('thij,tihd->tjhd', grad_scores, split_heads(queries)) * score_scale
    grad_v = jnp.einsum('thij,tihd->tjhd', rounded(attend), split_heads(grad_out))
    return (grad_q.reshape(queries.shape).astype(jnp.bfloat16), grad_k.reshape(queries.shape).astype(jnp.bfloat16), grad_v.reshape(queries.shape).astype(jnp.bfloat16))

def normalize(hidden):
    row_mean = lax.optimization_barrier(jnp.mean(hidden, axis=-1, keepdims=True))
    centred = hidden - row_mean
    row_var = lax.optimization_barrier(jnp.mean(centred * centred, axis=-1, keepdims=True))
    inv_std = lax.rsqrt(row_var + epsilon)
    return (centred * inv_std, inv_std)

def norm_backward(grad_normed, normed, inv_std, norm_gain, cot_rows):
    scaled_grad = grad_normed.astype(jnp.float32) * norm_gain
    first_mean = lax.optimization_barrier(jnp.mean(scaled_grad, axis=-1, keepdims=True))
    second_mean = lax.optimization_barrier(jnp.mean(scaled_grad * normed, axis=-1, keepdims=True))
    term = inv_std * (scaled_grad - first_mean - normed * second_mean)
    return (cot_rows.astype(jnp.float32) + term).astype(jnp.bfloat16)

def reference(time_query, time_key, time_value, residual_in, fc_weight, norm_gain, qkv_weight, out_weight, bias_slope, visible, cotangent):

    def one_clip(pieces):
        query_rows, key_rows, value_rows, resid_rows, tube_ids, cot_rows = pieces
        step_count, tube_count, inner_width = query_rows.shape
        model_width = resid_rows.shape[-1]
        shape_three = (step_count, tube_count, inner_width)
        mixed_out = temporal_forward(query_rows, key_rows, value_rows)
        hidden = resid_rows.reshape(-1, model_width).astype(jnp.float32) + jnp.dot(mixed_out.reshape(-1, inner_width), fc_weight, preferred_element_type=jnp.float32)
        normed, inv_std = normalize(hidden)
        normed_in = (normed * norm_gain).astype(jnp.bfloat16)
        projected = jnp.dot(normed_in, qkv_weight, preferred_element_type=jnp.float32).astype(jnp.bfloat16)
        flat_cot = cot_rows.reshape(-1, model_width)
        grad_mixed = jnp.dot(flat_cot, out_weight.T, preferred_element_type=jnp.float32).astype(jnp.bfloat16)
        pair_bias = distance_bias(tube_ids, bias_slope)
        grad_list = spatial_backward(projected[:, :inner_width].reshape(shape_three), projected[:, inner_width:2 * inner_width].reshape(shape_three), projected[:, 2 * inner_width:].reshape(shape_three), grad_mixed.reshape(shape_three), pair_bias)
        joined = jnp.concatenate([gradient.reshape(-1, inner_width) for gradient in grad_list], axis=-1)
        grad_normed = jnp.dot(joined, qkv_weight.T, preferred_element_type=jnp.float32).astype(jnp.bfloat16)
        grad_resid = norm_backward(grad_normed, normed, inv_std, norm_gain, flat_cot)
        grad_time = jnp.dot(grad_resid, fc_weight.T, preferred_element_type=jnp.float32).astype(jnp.bfloat16)
        grad_q, grad_k, grad_v = temporal_backward(query_rows, key_rows, value_rows, grad_time.reshape(shape_three))
        return (grad_resid.reshape(resid_rows.shape), grad_q, grad_k, grad_v)
    outputs = lax.map(one_clip, (time_query, time_key, time_value, residual_in, visible, cotangent))
    return (outputs[0], outputs[1], outputs[2], outputs[3])
```

```python
import jax
import jax.numpy as jnp
from jax import lax
from jax.sharding import PartitionSpec as P

HEADS = 12
HD = 64
GRID = 32


epsilon = 1e-05


def rounded(values):
    return lax.optimization_barrier(values.astype(jnp.bfloat16)).astype(jnp.float32)


def split_heads(block):
    return block.reshape(block.shape[:-1] + (HEADS, HD)).astype(jnp.float32)


def softmax_rows(scores):
    row_top = jnp.max(scores, axis=-1, keepdims=True)
    exponent = jnp.exp(scores - row_top)
    return exponent / jnp.sum(exponent, axis=-1, keepdims=True)


def probs_of(queries, key_rows, pair_bias=None):
    scores = jnp.einsum("thd,uhd->htu", split_heads(queries), split_heads(key_rows)) * HD ** (-0.5)
    if pair_bias is not None:
        scores = scores + pair_bias
    return softmax_rows(scores)


def attention_forward(queries, key_rows, value_rows):
    attend = probs_of(queries, key_rows)
    mixed_out = jnp.einsum("htu,uhd->thd", rounded(attend), split_heads(value_rows))
    return mixed_out.reshape(queries.shape).astype(jnp.bfloat16)


def attention_backward(queries, key_rows, value_rows, grad_out, pair_bias=None):
    attend = probs_of(queries, key_rows, pair_bias)
    grad_attend = jnp.einsum("thd,uhd->htu", split_heads(grad_out), split_heads(value_rows))
    inner_sum = jnp.sum(attend * grad_attend, axis=-1, keepdims=True)
    grad_scores = rounded(attend * (grad_attend - inner_sum))
    score_scale = HD ** (-0.5)
    grad_q = jnp.einsum("htu,uhd->thd", grad_scores, split_heads(key_rows)) * score_scale
    grad_k = jnp.einsum("htu,thd->uhd", grad_scores, split_heads(queries)) * score_scale
    grad_v = jnp.einsum("htu,thd->uhd", rounded(attend), split_heads(grad_out))
    return tuple(g.reshape(queries.shape).astype(jnp.bfloat16) for g in (grad_q, grad_k, grad_v))


def distance_bias(tube_ids, bias_slope):
    tube_rows = tube_ids // GRID
    tube_cols = tube_ids % GRID
    distance = jnp.abs(tube_rows[:, None] - tube_rows[None, :]) + jnp.abs(
        tube_cols[:, None] - tube_cols[None, :]
    )
    return -bias_slope[:, None, None] * distance.astype(jnp.float32)[None]


def normalize(hidden):
    row_mean = jnp.mean(hidden, axis=-1, keepdims=True)
    centred = hidden - row_mean
    row_var = jnp.mean(centred * centred, axis=-1, keepdims=True)
    inv_std = lax.rsqrt(row_var + epsilon)
    return (centred * inv_std, inv_std)


def norm_backward(grad_normed, normed, inv_std, norm_gain, cot_rows):
    scaled_grad = grad_normed.astype(jnp.float32) * norm_gain
    first_mean = jnp.mean(scaled_grad, axis=-1, keepdims=True)
    second_mean = jnp.mean(scaled_grad * normed, axis=-1, keepdims=True)
    term = inv_std * (scaled_grad - first_mean - normed * second_mean)
    return (cot_rows.astype(jnp.float32) + term).astype(jnp.bfloat16)


def middle(mixed, resid, cot, fc_full, qkv_full, out_full, norm_gain, pair_bias):
    inner = mixed.shape[-1]
    f32 = jnp.float32
    hidden = resid.astype(f32) + jnp.dot(mixed, fc_full, preferred_element_type=f32)
    normed, inv_std = normalize(hidden)
    normed_in = (normed * norm_gain).astype(jnp.bfloat16)
    grad_mixed = jnp.dot(cot, out_full.T, preferred_element_type=f32).astype(jnp.bfloat16)
    projected = jnp.dot(normed_in, qkv_full, preferred_element_type=f32).astype(jnp.bfloat16)
    grads = attention_backward(
        projected[:, :inner],
        projected[:, inner : 2 * inner],
        projected[:, 2 * inner :],
        grad_mixed,
        pair_bias,
    )
    joined = jnp.concatenate(grads, axis=-1)
    grad_normed = jnp.dot(joined, qkv_full.T, preferred_element_type=f32).astype(jnp.bfloat16)
    grad_resid = norm_backward(grad_normed, normed, inv_std, norm_gain, cot)
    grad_time = jnp.dot(grad_resid, fc_full.T, preferred_element_type=f32).astype(jnp.bfloat16)
    return grad_resid, grad_time


def body(
    time_query,
    time_key,
    time_value,
    residual_in,
    fc_weight,
    norm_gain,
    qkv_weight,
    out_weight,
    bias_slope,
    visible,
    cotangent,
):
    tm, sp = lax.axis_size("tm"), lax.axis_size("space")
    steps, tubes, inner = time_query.shape[1:]
    width = residual_in.shape[-1]
    fc_rows, qkv_rows = fc_weight.shape[0], qkv_weight.shape[0]
    total = tm * steps
    both = ("tm", "space")

    pieces = [x[0].transpose(1, 0, 2) for x in (time_query, time_key, time_value)]
    shard = jnp.concatenate(
        [qkv_weight.reshape(-1, inner), fc_weight.reshape(-1, inner), out_weight.reshape(-1, inner)]
    )
    send = jnp.concatenate(
        pieces + [jnp.broadcast_to(shard[None], (tm,) + shard.shape)], axis=1
    )
    got = lax.all_to_all(send, "tm", split_axis=0, concat_axis=0, tiled=True)
    queries, keys, values = (
        got[:, i * steps : (i + 1) * steps].reshape(total, inner) for i in range(3)
    )
    at = 3 * steps
    cut = at + qkv_weight.size // inner
    mid = cut + fc_weight.size // inner
    qkv_part = got[:, at:cut].reshape(tm * qkv_rows, 3 * inner)
    fc_part = got[:, cut:mid].reshape(tm * fc_rows, width)
    out_part = got[:, mid:].reshape(tm * fc_rows, width)
    qkv_all = lax.all_gather(qkv_part, "space", axis=0)
    fo_all = lax.all_gather(jnp.concatenate([fc_part, out_part]), "space", axis=0)

    def natural(block, rows):
        block = block.reshape((sp, tm, rows) + block.shape[-1:])
        return block.transpose(1, 0, 2, 3).reshape(sp * tm * rows, -1)

    mixed = attention_forward(queries, keys, values)
    mixed = lax.all_to_all(mixed, both, split_axis=0, concat_axis=0, tiled=True)

    rest = jnp.concatenate([residual_in[0], cotangent[0]], axis=-1)
    rest, mixed = lax.optimization_barrier((rest, mixed))
    rest = lax.all_to_all(rest, "space", split_axis=0, concat_axis=0, tiled=True)
    rest = rest.reshape(sp, tm, 2 * width).transpose(1, 0, 2).reshape(sp * tm, 2 * width)
    tube_ids = visible[0].reshape(sp, tm).T.reshape(-1)
    pair_bias = distance_bias(tube_ids, bias_slope)

    qkv_full = natural(qkv_all, qkv_rows)
    fc_full = natural(fo_all[:, : tm * fc_rows], fc_rows)
    out_full = natural(fo_all[:, tm * fc_rows :], fc_rows)
    grad_resid, grad_time = middle(
        mixed, rest[:, :width], rest[:, width:], fc_full, qkv_full, out_full, norm_gain, pair_bias
    )
    grad_time = lax.all_to_all(grad_time, both, split_axis=0, concat_axis=0, tiled=True)
    grad_resid, grad_time = lax.optimization_barrier((grad_resid, grad_time))
    grad_resid = grad_resid.reshape(tm, sp, width).transpose(1, 0, 2)
    grad_resid = lax.all_to_all(grad_resid, "space", split_axis=0, concat_axis=0, tiled=True)

    grads = attention_backward(queries, keys, values, grad_time)
    back = jnp.concatenate([g.reshape(tm, steps, inner) for g in grads], axis=1)
    back = lax.all_to_all(back, "tm", split_axis=0, concat_axis=0, tiled=True)
    outs = [
        back[:, i * steps : (i + 1) * steps].transpose(1, 0, 2)[None] for i in range(3)
    ]
    return (grad_resid.reshape(residual_in.shape), *outs)


def solution(mesh):
    token = P("dp", "tm", "space", None)
    row = P(("tm", "space"), None)
    in_specs = (token, token, token, token, row, P(), row, row, P(), P("dp", None), token)
    return jax.shard_map(
        body, mesh=mesh, in_specs=in_specs, out_specs=(token,) * 4, check_vma=False
    )
```

```python
import numpy as np
import jax
import jax.numpy as jnp
from jax import lax
from jax.experimental import pallas as pl
from jax.experimental.pallas import tpu as pltpu
from jax.sharding import PartitionSpec as P

HEADS = 12
HD = 64
GRID = 32
SCALE = HD ** (-0.5)
EPSILON = 1e-05
F32 = jnp.float32
BF16 = jnp.bfloat16
VMEM = pl.BlockSpec(memory_space=pltpu.VMEM)
SMEM = pl.BlockSpec(memory_space=pltpu.SMEM)
ANY = pl.BlockSpec(memory_space=pl.ANY)


def params(mib):
    return pltpu.CompilerParams(vmem_limit_bytes=mib * 2**20)


def nn(a, b):
    return jnp.dot(a, b, preferred_element_type=F32)


def nt(a, b):
    return lax.dot_general(a, b, (((1,), (1,)), ((), ())), preferred_element_type=F32)


def tn(a, b):
    return lax.dot_general(a, b, (((0,), (0,)), ((), ())), preferred_element_type=F32)


def transposed_rows(outer, inner):
    m = np.zeros((outer * inner, outer * inner), np.float32)
    i, j = np.meshgrid(np.arange(outer), np.arange(inner), indexing="ij")
    m[(j * outer + i).ravel(), (i * inner + j).ravel()] = 1
    return m.astype(BF16)


def gathered_order(tm, sp, rows):
    size = tm * sp * rows
    m = np.zeros((size, size), np.float32)
    a, b, r = (v.ravel() for v in np.meshgrid(*map(np.arange, (tm, sp, rows)), indexing="ij"))
    m[(a * sp + b) * rows + r, (b * tm + a) * rows + r] = 1
    return m.astype(BF16)


def shard_order(tm):
    main = np.zeros((12 * tm, 16 * tm), np.float32)
    rest = np.zeros((3, 3, 4 * tm, 16 * tm), np.float32)
    third = 2 * tm
    for which in range(2):
        for n in range(6 * tm):
            a, r = divmod(n, 6)
            g = which * 6 + r
            main[which * 6 * tm + n, a * 16 + g] = 1
            rest[n // third, g // 4, which * third + n % third, a * 16 + 12 + g % 4] = 1
    return main.astype(BF16), rest.astype(BF16)


def weights_pack_kernel(fc_ref, out_ref, qkv_ref, o_ref):
    both = jnp.concatenate([fc_ref[...].astype(F32), out_ref[...].astype(F32)], axis=0)
    tail = both[:, 768:]
    tail = jnp.concatenate([tail[0:4], tail[4:8], tail[8:12]], axis=1)
    qkv = qkv_ref[...].astype(F32)
    block = jnp.concatenate(
        [both[:, :768], tail, qkv[:, :768], qkv[:, 768:1536], qkv[:, 1536:]], axis=0
    )
    o_ref[...] = jnp.broadcast_to(block[None], o_ref.shape).astype(BF16)


def weights_unpack_kernel(x_ref, main_ref, rest_ref, o_ref):
    tm = x_ref.shape[0]
    x = x_ref[...].astype(F32)
    fo = x[:, 0:16].reshape(16 * tm, 768).astype(BF16)
    n = 8 * tm
    for j in range(3):
        o_ref[pl.ds(j * n, n), :] = x[:, 16 + 8 * j : 24 + 8 * j].reshape(n, 768).astype(BF16)
    o_ref[pl.ds(3 * n, 12 * tm), :] = nn(main_ref[...], fo).astype(BF16)
    for j in range(3):
        part = nn(rest_ref[j, 0], fo[:, :256])
        part += nn(rest_ref[j, 1], fo[:, 256:512])
        part += nn(rest_ref[j, 2], fo[:, 512:])
        o_ref[pl.ds(3 * n + 12 * tm, 4 * tm), pl.ds(j * 256, 256)] = part.astype(BF16)


def pack_kernel(q_ref, k_ref, v_ref, res_ref, cot_ref, turn_ref, o_ref, rest_ref):
    steps, tubes, inner = q_ref.shape[1:]
    rows = steps * tubes
    parts = [
        nn(turn_ref[...], ref[0].reshape(rows, inner)).reshape(tubes, steps, inner)
        for ref in (q_ref, k_ref, v_ref)
    ]
    o_ref[...] = jnp.concatenate(parts, axis=1).astype(BF16)
    rest_ref[...] = jnp.concatenate([res_ref[0], cot_ref[0]], axis=-1)


def unpack_kernel(x_ref, turn_ref, *outs):
    x = x_ref[...].astype(F32)
    tubes, steps = x.shape[0], x.shape[1] // 3
    for j, o_ref in enumerate(outs):
        part = x[:, j * steps : (j + 1) * steps].reshape(tubes * steps, -1).astype(BF16)
        o_ref[0] = nn(turn_ref[...], part).astype(BF16).reshape(steps, tubes, -1)


def lane_masks(rows):
    lane = lax.broadcasted_iota(jnp.int32, (rows, 2 * HD), 1)
    return lane < HD


def stacked(block, first):
    zero = jnp.zeros_like(block)
    return jnp.concatenate([jnp.where(first, block, zero), jnp.where(first, zero, block)], axis=0)


def softmax(scores):
    exponent = jnp.exp(scores - jnp.max(scores, axis=-1, keepdims=True))
    return exponent / jnp.sum(exponent, axis=-1, keepdims=True)


def pair_probs(q, k2, bias0=None, bias1=None):
    n = q.shape[0]
    scores = nt(q, k2) * SCALE
    s0, s1 = scores[:, :n], scores[:, n:]
    if bias0 is not None:
        s0, s1 = s0 + bias0, s1 + bias1
    return softmax(s0), softmax(s1)


def pair_backward(p0, p1, q, k, v, g, first):
    n = q.shape[0]
    k2, v2, q2, g2 = (stacked(x, first) for x in (k, v, q, g))
    gp = nt(g, v2)
    g0, g1 = gp[:, :n], gp[:, n:]
    d0 = (p0 * (g0 - jnp.sum(p0 * g0, axis=-1, keepdims=True))).astype(BF16)
    d1 = (p1 * (g1 - jnp.sum(p1 * g1, axis=-1, keepdims=True))).astype(BF16)
    grad_q = nn(jnp.concatenate([d0, d1], axis=1), k2)
    grad_k = tn(jnp.concatenate([d0, d1], axis=0), q2)
    grad_v = tn(jnp.concatenate([p0.astype(BF16), p1.astype(BF16)], axis=0), g2)
    return grad_q * SCALE, grad_k * SCALE, grad_v


def qkv_of(x, steps):
    return [
        x[:, j * steps : (j + 1) * steps].reshape(x.shape[0] * steps, -1).astype(BF16)
        for j in range(3)
    ]


def forward_kernel(x_ref, o_ref, p_ref, turned):
    x = x_ref[...].astype(F32)
    q, k, v = qkv_of(x, x.shape[1] // 3)
    n = q.shape[0]
    first = lane_masks(n)
    for h in range(HEADS // 2):
        at = slice(h * 128, (h + 1) * 128)
        p0, p1 = pair_probs(q[:, at], stacked(k[:, at], first))
        p_ref[h, :, 0:n] = p0
        p_ref[h, :, n : 2 * n] = p1
        both = jnp.concatenate([p0.astype(BF16), p1.astype(BF16)], axis=1)
        turned[:, h, :] = nn(both, stacked(v[:, at], first))
    o_ref[...] = turned[...].astype(BF16)


def backward_kernel(x_ref, p_ref, g_ref, o_ref, turned):
    x = x_ref[...].astype(F32)
    steps = x.shape[1] // 3
    q, k, v = qkv_of(x, steps)
    n = q.shape[0]
    turned[...] = g_ref[...].astype(F32)
    first = lane_masks(n)
    for h in range(HEADS // 2):
        at = slice(h * 128, (h + 1) * 128)
        grads = pair_backward(
            p_ref[h, :, 0:n],
            p_ref[h, :, n : 2 * n],
            q[:, at],
            k[:, at],
            v[:, at],
            turned[:, h, :].astype(BF16),
            first,
        )
        joined = jnp.concatenate([d.reshape(n // steps, steps, 128) for d in grads], axis=1)
        o_ref[:, :, at] = joined.astype(BF16)


def middle_kernel(
    w_hbm, x_ref, rest_ref, gain_ref, slope_ref, row_ref, col_ref, turn_ref, inner_ref, width_ref,
    gr_ref, gt_ref, qkv_v, fc_v, out_v, turned, proj, joined, sem,
):
    sp = w_hbm.shape[0]
    tm = w_hbm.shape[1] // 40
    n, third = 8 * tm, 2 * tm
    copies = []

    def load(src, dst):
        copies.append(pltpu.make_async_copy(src, dst, sem.at[len(copies)]))
        copies[-1].start()

    at = 3 * n
    for dst, base, tail in (
        (fc_v, at, at + 12 * tm),
        (out_v, at + 6 * tm, at + 12 * tm + third),
    ):
        load(w_hbm.at[:, pl.ds(base, 6 * tm), :], dst.at[:, :, pl.ds(0, 768)])
        for j in range(3):
            load(
                w_hbm.at[:, pl.ds(tail, third), pl.ds(j * 256, 256)],
                dst.at[:, pl.ds(j * third, third), pl.ds(768, 256)],
            )
    for j in range(3):
        load(w_hbm.at[:, pl.ds(j * n, n), :], qkv_v.at[:, :, pl.ds(j * 768, 768)])

    tokens = x_ref.shape[0]
    width = gain_ref.shape[1]
    inner = 768
    rows, cols = row_ref[...], col_ref[...]
    distance = jnp.abs((rows >> 5) - (cols >> 5)) + jnp.abs((rows & 31) - (cols & 31))
    distance = distance.astype(F32)
    gain = gain_ref[...]
    turn = turn_ref[...]
    turned[...] = x_ref[...].astype(F32)
    mixed = jnp.concatenate([turned[:, h, :] for h in range(6)], axis=1).astype(BF16)
    mixed = nn(turn, mixed).astype(BF16)
    mixed = nn(mixed, inner_ref[...]).astype(BF16)
    cot = rest_ref[:, width:]

    for c in copies[:4]:
        c.wait()
    fc = fc_v[...].reshape(inner, width)
    hidden = rest_ref[:, :width].astype(F32) + nn(mixed, fc)
    centred = hidden - jnp.mean(hidden, axis=-1, keepdims=True)
    inv_std = lax.rsqrt(jnp.mean(centred * centred, axis=-1, keepdims=True) + EPSILON)
    normed = centred * inv_std
    normed_in = (normed * gain).astype(BF16)
    normed_in = nn(normed_in, width_ref[...]).astype(BF16)

    for c in copies[4:8]:
        c.wait()
    grad_mixed = nt(cot, out_v[...].reshape(inner, width)).astype(BF16)
    grad_mixed = nt(grad_mixed, inner_ref[...]).astype(BF16)

    for c in copies[8:]:
        c.wait()
    qkv = qkv_v[...].reshape(width, 3 * inner)
    proj[...] = nn(normed_in, qkv).astype(BF16)

    first = lane_masks(tokens)
    for h in range(HEADS // 2):
        q, k, v = (proj[:, j * inner + h * 128 : j * inner + (h + 1) * 128] for j in range(3))
        g = grad_mixed[:, h * 128 : (h + 1) * 128]
        p0, p1 = pair_probs(
            q, stacked(k, first), -slope_ref[2 * h] * distance, -slope_ref[2 * h + 1] * distance
        )
        for j, d in enumerate(pair_backward(p0, p1, q, k, v, g, first)):
            joined[:, j * inner + h * 128 : j * inner + (h + 1) * 128] = d.astype(BF16)

    grad_normed = nt(joined[...], qkv).astype(BF16)
    grad_normed = nt(grad_normed, width_ref[...])
    scaled = grad_normed * gain
    first_mean = jnp.mean(scaled, axis=-1, keepdims=True)
    second_mean = jnp.mean(scaled * normed, axis=-1, keepdims=True)
    term = inv_std * (scaled - first_mean - normed * second_mean)
    grad_resid = (cot.astype(F32) + term).astype(BF16)
    gr_ref[...] = grad_resid
    grad_time = nt(grad_resid, fc).astype(BF16)
    grad_time = nt(grad_time, inner_ref[...]).astype(BF16)
    grad_time = tn(turn, grad_time)
    for h in range(6):
        turned[:, h, :] = grad_time[:, h * 128 : (h + 1) * 128]
    gt_ref[...] = turned[...].astype(BF16)


def body(
    time_query,
    time_key,
    time_value,
    residual_in,
    fc_weight,
    norm_gain,
    qkv_weight,
    out_weight,
    bias_slope,
    visible,
    cotangent,
):
    tm, sp = lax.axis_size("tm"), lax.axis_size("space")
    steps, tubes, inner = time_query.shape[1:]
    width = residual_in.shape[-1]
    total = tm * steps
    both = ("tm", "space")
    shape = jax.ShapeDtypeStruct

    def exchange(x, axes):
        return lax.all_to_all(x, axes, split_axis=0, concat_axis=0, tiled=True)

    to_tubes = jnp.asarray(transposed_rows(steps, tubes))
    to_steps = jnp.asarray(transposed_rows(tubes, steps))
    to_order = jnp.asarray(transposed_rows(tm, sp))
    main_map, rest_map = map(jnp.asarray, shard_order(tm))
    inner_map = jnp.asarray(gathered_order(tm, sp, fc_weight.shape[0]))
    width_map = jnp.asarray(gathered_order(tm, sp, qkv_weight.shape[0]))

    shards = pl.pallas_call(
        weights_pack_kernel,
        out_shape=shape((tm, 40, inner), BF16),
        in_specs=[VMEM] * 3,
        out_specs=VMEM,
        compiler_params=params(16),
        name="weights_pack",
    )(fc_weight, out_weight, qkv_weight)
    shards = exchange(shards, "tm")

    send, rest = pl.pallas_call(
        pack_kernel,
        out_shape=(shape((tubes, 3 * steps, inner), BF16), shape((steps, tubes, 2 * width), BF16)),
        in_specs=[VMEM] * 6,
        out_specs=(VMEM, VMEM),
        compiler_params=params(16),
        name="pack",
    )(time_query, time_key, time_value, residual_in, cotangent, to_tubes)

    shards = pl.pallas_call(
        weights_unpack_kernel,
        out_shape=shape((40 * tm, inner), BF16),
        in_specs=[VMEM] * 3,
        out_specs=VMEM,
        compiler_params=params(24),
        name="weights_unpack",
    )(shards, main_map, rest_map)
    weights = lax.all_gather(shards, "space", axis=0)

    send, shards = lax.optimization_barrier((send, shards))
    got = exchange(send, "tm")
    rest, got = lax.optimization_barrier((rest, got))
    rest = exchange(rest, "space").reshape(total, 2 * width)

    mixed, probs = pl.pallas_call(
        forward_kernel,
        out_shape=(shape((total, 6, 128), BF16), shape((HEADS // 2, total, 2 * total), F32)),
        in_specs=[VMEM],
        out_specs=(VMEM, VMEM),
        scratch_shapes=[pltpu.VMEM((total, 6, 128), F32)],
        compiler_params=params(24),
        cost_estimate=pl.CostEstimate(flops=10**8, bytes_accessed=2 * 10**6, transcendentals=2 * 10**5),
        name="temporal_forward",
    )(got)
    mixed, rest = lax.optimization_barrier((mixed, rest))
    mixed = exchange(mixed, both)

    grad_resid, grad_time = pl.pallas_call(
        middle_kernel,
        out_shape=(shape((total, width), BF16), shape((total, 6, 128), BF16)),
        in_specs=[ANY, VMEM, VMEM, VMEM, SMEM, VMEM, VMEM, VMEM, VMEM, VMEM],
        out_specs=(VMEM, VMEM),
        scratch_shapes=[
            pltpu.VMEM((sp, 8 * tm, 3 * inner), BF16),
            pltpu.VMEM((sp, 6 * tm, width), BF16),
            pltpu.VMEM((sp, 6 * tm, width), BF16),
            pltpu.VMEM((total, 6, 128), F32),
            pltpu.VMEM((total, 3 * inner), BF16),
            pltpu.VMEM((total, 3 * inner), BF16),
            pltpu.SemaphoreType.DMA((11,)),
        ],
        compiler_params=params(48),
        cost_estimate=pl.CostEstimate(flops=4 * 10**9, bytes_accessed=10**7, transcendentals=2 * 10**5),
        name="middle",
    )(
        weights,
        mixed,
        rest,
        norm_gain.reshape(1, width),
        bias_slope,
        visible.reshape(total, 1),
        visible.reshape(1, total),
        to_order,
        inner_map,
        width_map,
    )
    grad_time = exchange(grad_time, both)
    grad_resid, grad_time = lax.optimization_barrier((grad_resid, grad_time))
    grad_resid = exchange(grad_resid.reshape(steps, tubes, width), "space")

    back = pl.pallas_call(
        backward_kernel,
        out_shape=shape((tm, 3 * steps, inner), BF16),
        in_specs=[VMEM] * 3,
        out_specs=VMEM,
        scratch_shapes=[pltpu.VMEM((total, 6, 128), F32)],
        compiler_params=params(24),
        cost_estimate=pl.CostEstimate(flops=3 * 10**8, bytes_accessed=2 * 10**6, transcendentals=0),
        name="temporal_backward",
    )(got, probs, grad_time)
    back, grad_resid = lax.optimization_barrier((back, grad_resid))
    back = exchange(back, "tm")
    outs = pl.pallas_call(
        unpack_kernel,
        out_shape=(shape(time_query.shape, BF16),) * 3,
        in_specs=[VMEM] * 2,
        out_specs=(VMEM,) * 3,
        compiler_params=params(16),
        name="unpack",
    )(back, to_steps)
    return (grad_resid.reshape(residual_in.shape), *outs)


def solution(mesh):
    token = P("dp", "tm", "space", None)
    row = P(("tm", "space"), None)
    in_specs = (token, token, token, token, row, P(), row, row, P(), P("dp", None), token)
    return jax.shard_map(
        body, mesh=mesh, in_specs=in_specs, out_specs=(token,) * 4, check_vma=False
    )
```

```python
import numpy as np
import jax
import jax.numpy as jnp
from jax import lax
from jax.experimental import pallas as pl
from jax.experimental.pallas import tpu as pltpu
from jax.sharding import PartitionSpec as P

HEADS = 12
HD = 64
GRID = 32
SCALE = HD ** (-0.5)
EPSILON = 1e-05
F32 = jnp.float32
BF16 = jnp.bfloat16
VMEM = pl.BlockSpec(memory_space=pltpu.VMEM)
SMEM = pl.BlockSpec(memory_space=pltpu.SMEM)
HBM = pl.BlockSpec(memory_space=pltpu.HBM)


def params(mib):
    return pltpu.CompilerParams(vmem_limit_bytes=mib * 2**20)


def nn(a, b):
    return jnp.dot(a, b, preferred_element_type=F32)


def nt(a, b):
    return lax.dot_general(a, b, (((1,), (1,)), ((), ())), preferred_element_type=F32)


def tn(a, b):
    return lax.dot_general(a, b, (((0,), (0,)), ((), ())), preferred_element_type=F32)


def transposed_rows(outer, inner):
    m = np.zeros((outer * inner, outer * inner), np.float32)
    i, j = np.meshgrid(np.arange(outer), np.arange(inner), indexing="ij")
    m[(j * outer + i).ravel(), (i * inner + j).ravel()] = 1
    return m.astype(BF16)


def gathered_order(tm, sp, rows):
    size = tm * sp * rows
    m = np.zeros((size, size), np.float32)
    a, b, r = (v.ravel() for v in np.meshgrid(*map(np.arange, (tm, sp, rows)), indexing="ij"))
    m[(a * sp + b) * rows + r, (b * tm + a) * rows + r] = 1
    return m.astype(BF16)


def shard_order(tm):
    main = np.zeros((12 * tm, 16 * tm), np.float32)
    rest = np.zeros((3, 3, 4 * tm, 16 * tm), np.float32)
    third = 2 * tm
    for which in range(2):
        for n in range(6 * tm):
            a, r = divmod(n, 6)
            g = which * 6 + r
            main[which * 6 * tm + n, a * 16 + g] = 1
            rest[n // third, g // 4, which * third + n % third, a * 16 + 12 + g % 4] = 1
    return main.astype(BF16), rest.astype(BF16)


def first_kernel(fc_hbm, out_hbm, qkv_hbm, res_hbm, cot_hbm, o_ref, rest_hbm, fc_ref, out_ref, qkv_ref, sem):
    width = res_hbm.shape[-1]
    copies = [
        pltpu.make_async_copy(res_hbm.at[0], rest_hbm.at[:, :, pl.ds(0, width)], sem.at[0]),
        pltpu.make_async_copy(cot_hbm.at[0], rest_hbm.at[:, :, pl.ds(width, width)], sem.at[1]),
        pltpu.make_async_copy(fc_hbm, fc_ref, sem.at[2]),
        pltpu.make_async_copy(out_hbm, out_ref, sem.at[3]),
        pltpu.make_async_copy(qkv_hbm, qkv_ref, sem.at[4]),
    ]
    for c in copies:
        c.start()
    for c in copies[2:]:
        c.wait()
    both = jnp.concatenate([fc_ref[...].astype(F32), out_ref[...].astype(F32)], axis=0)
    tail = both[:, 768:]
    tail = jnp.concatenate([tail[0:4], tail[4:8], tail[8:12]], axis=1)
    qkv = qkv_ref[...].astype(F32)
    block = jnp.concatenate(
        [both[:, :768], tail, qkv[:, :768], qkv[:, 768:1536], qkv[:, 1536:]], axis=0
    )
    o_ref[...] = jnp.broadcast_to(block[None], o_ref.shape).astype(BF16)
    for c in copies[:2]:
        c.wait()


def weights_unpack_kernel(x_ref, main_ref, rest_ref, o_ref):
    tm = x_ref.shape[0]
    x = x_ref[...].astype(F32)
    fo = x[:, 0:16].reshape(16 * tm, 768).astype(BF16)
    n = 8 * tm
    for j in range(3):
        o_ref[pl.ds(j * n, n), :] = x[:, 16 + 8 * j : 24 + 8 * j].reshape(n, 768).astype(BF16)
    o_ref[pl.ds(3 * n, 12 * tm), :] = nn(main_ref[...], fo).astype(BF16)
    for j in range(3):
        part = nn(rest_ref[j, 0], fo[:, :256])
        part += nn(rest_ref[j, 1], fo[:, 256:512])
        part += nn(rest_ref[j, 2], fo[:, 512:])
        o_ref[pl.ds(3 * n + 12 * tm, 4 * tm), pl.ds(j * 256, 256)] = part.astype(BF16)


def pack_kernel(q_ref, k_ref, v_ref, turn_ref, o_ref):
    steps, tubes, inner = q_ref.shape[1:]
    rows = steps * tubes
    parts = [
        nn(turn_ref[...], ref[0].reshape(rows, inner)).reshape(tubes, steps, inner)
        for ref in (q_ref, k_ref, v_ref)
    ]
    o_ref[...] = jnp.concatenate(parts, axis=1).astype(BF16)


def unpack_kernel(me_ref, x_ref, turn_ref, gr_hbm, *refs):
    outs, gr_out, sem = refs[:3], refs[3], refs[4]
    mine = outs[0].shape[2]
    at = pl.multiple_of(me_ref[0] * mine, mine)
    copy = pltpu.make_async_copy(gr_hbm.at[:, pl.ds(at, mine), :], gr_out.at[0], sem)
    copy.start()
    x = x_ref[...].astype(F32)
    tubes, steps = x.shape[0], x.shape[1] // 3
    for j, o_ref in enumerate(outs):
        part = x[:, j * steps : (j + 1) * steps].reshape(tubes * steps, -1).astype(BF16)
        o_ref[0] = nn(turn_ref[...], part).astype(BF16).reshape(steps, tubes, -1)
    copy.wait()


def lane_masks(rows):
    lane = lax.broadcasted_iota(jnp.int32, (rows, 2 * HD), 1)
    return lane < HD


def stacked(block, first):
    zero = jnp.zeros_like(block)
    return jnp.concatenate([jnp.where(first, block, zero), jnp.where(first, zero, block)], axis=0)


def softmax(scores):
    exponent = jnp.exp(scores - jnp.max(scores, axis=-1, keepdims=True))
    return exponent / jnp.sum(exponent, axis=-1, keepdims=True)


def pair_probs(q, k2, bias0=None, bias1=None):
    n = q.shape[0]
    scores = nt(q, k2) * SCALE
    s0, s1 = scores[:, :n], scores[:, n:]
    if bias0 is not None:
        s0, s1 = s0 + bias0, s1 + bias1
    return softmax(s0), softmax(s1)


def pair_backward(p0, p1, q, k, v, g, first):
    n = q.shape[0]
    k2, v2, q2, g2 = (stacked(x, first) for x in (k, v, q, g))
    gp = nt(g, v2)
    g0, g1 = gp[:, :n], gp[:, n:]
    d0 = (p0 * (g0 - jnp.sum(p0 * g0, axis=-1, keepdims=True))).astype(BF16)
    d1 = (p1 * (g1 - jnp.sum(p1 * g1, axis=-1, keepdims=True))).astype(BF16)
    grad_q = nn(jnp.concatenate([d0, d1], axis=1), k2)
    grad_k = tn(jnp.concatenate([d0, d1], axis=0), q2)
    grad_v = tn(jnp.concatenate([p0.astype(BF16), p1.astype(BF16)], axis=0), g2)
    return grad_q * SCALE, grad_k * SCALE, grad_v


def qkv_of(x, steps):
    return [
        x[:, j * steps : (j + 1) * steps].reshape(x.shape[0] * steps, -1).astype(BF16)
        for j in range(3)
    ]


def forward_kernel(x_ref, o_ref, p_ref, turned):
    x = x_ref[...].astype(F32)
    q, k, v = qkv_of(x, x.shape[1] // 3)
    n = q.shape[0]
    first = lane_masks(n)
    for h in range(HEADS // 2):
        at = slice(h * 128, (h + 1) * 128)
        p0, p1 = pair_probs(q[:, at], stacked(k[:, at], first))
        p_ref[h, :, 0:n] = p0
        p_ref[h, :, n : 2 * n] = p1
        both = jnp.concatenate([p0.astype(BF16), p1.astype(BF16)], axis=1)
        turned[:, h, :] = nn(both, stacked(v[:, at], first))
    o_ref[...] = turned[...].astype(BF16)


def backward_kernel(x_ref, p_ref, g_ref, o_ref, turned):
    x = x_ref[...].astype(F32)
    steps = x.shape[1] // 3
    q, k, v = qkv_of(x, steps)
    n = q.shape[0]
    turned[...] = g_ref[...].astype(F32)
    first = lane_masks(n)
    for h in range(HEADS // 2):
        at = slice(h * 128, (h + 1) * 128)
        grads = pair_backward(
            p_ref[h, :, 0:n],
            p_ref[h, :, n : 2 * n],
            q[:, at],
            k[:, at],
            v[:, at],
            turned[:, h, :].astype(BF16),
            first,
        )
        joined = jnp.concatenate([d.reshape(n // steps, steps, 128) for d in grads], axis=1)
        o_ref[:, :, at] = joined.astype(BF16)


def middle_kernel(
    me_ref, w_hbm, x_ref, rest_hbm, gain_ref, slope_ref, row_ref, col_ref, turn_ref, inner_hbm, width_hbm,
    gr_ref, gt_ref, rest_v, inner_ref, width_v, qkv_v, fc_v, out_v, turned, proj, joined, sem,
):
    sp = w_hbm.shape[0]
    tm = w_hbm.shape[1] // 40
    n, third = 8 * tm, 2 * tm
    copies = []

    def load(src, dst):
        copies.append(pltpu.make_async_copy(src, dst, sem.at[len(copies)]))
        copies[-1].start()

    load(inner_hbm, inner_ref)
    load(rest_hbm.at[:, me_ref[0]], rest_v)
    at = 3 * n
    for dst, base, tail in (
        (fc_v, at, at + 12 * tm),
        (out_v, at + 6 * tm, at + 12 * tm + third),
    ):
        load(w_hbm.at[:, pl.ds(base, 6 * tm), :], dst.at[:, :, pl.ds(0, 768)])
        for j in range(3):
            load(
                w_hbm.at[:, pl.ds(tail, third), pl.ds(j * 256, 256)],
                dst.at[:, pl.ds(j * third, third), pl.ds(768, 256)],
            )
    load(width_hbm, width_v)
    for j in range(3):
        load(w_hbm.at[:, pl.ds(j * n, n), :], qkv_v.at[:, :, pl.ds(j * 768, 768)])

    tokens = x_ref.shape[0]
    width = gain_ref.shape[1]
    inner = 768
    rows, cols = row_ref[...], col_ref[...]
    distance = jnp.abs((rows >> 5) - (cols >> 5)) + jnp.abs((rows & 31) - (cols & 31))
    distance = distance.astype(F32)
    gain = gain_ref[...]
    turn = turn_ref[...]
    turned[...] = x_ref[...].astype(F32)
    mixed = jnp.concatenate([turned[:, h, :] for h in range(6)], axis=1).astype(BF16)
    mixed = nn(turn, mixed).astype(BF16)

    for c in copies[:6]:
        c.wait()
    mixed = nn(mixed, inner_ref[...]).astype(BF16)
    rest = rest_v[...].reshape(tokens, 2 * width)
    cot = rest[:, width:]
    fc = fc_v[...].reshape(inner, width)
    hidden = rest[:, :width].astype(F32) + nn(mixed, fc)
    centred = hidden - jnp.mean(hidden, axis=-1, keepdims=True)
    inv_std = lax.rsqrt(jnp.mean(centred * centred, axis=-1, keepdims=True) + EPSILON)
    normed = centred * inv_std
    normed_in = (normed * gain).astype(BF16)

    for c in copies[6:11]:
        c.wait()
    normed_in = nn(normed_in, width_v[...]).astype(BF16)
    grad_mixed = nt(cot, out_v[...].reshape(inner, width)).astype(BF16)
    grad_mixed = nt(grad_mixed, inner_ref[...]).astype(BF16)

    for c in copies[11:]:
        c.wait()
    qkv = qkv_v[...].reshape(width, 3 * inner)
    proj[...] = nn(normed_in, qkv).astype(BF16)

    first = lane_masks(tokens)
    for h in range(HEADS // 2):
        q, k, v = (proj[:, j * inner + h * 128 : j * inner + (h + 1) * 128] for j in range(3))
        g = grad_mixed[:, h * 128 : (h + 1) * 128]
        p0, p1 = pair_probs(
            q, stacked(k, first), -slope_ref[2 * h] * distance, -slope_ref[2 * h + 1] * distance
        )
        for j, d in enumerate(pair_backward(p0, p1, q, k, v, g, first)):
            joined[:, j * inner + h * 128 : j * inner + (h + 1) * 128] = d.astype(BF16)

    grad_normed = nt(joined[...], qkv).astype(BF16)
    grad_normed = nt(grad_normed, width_v[...])
    scaled = grad_normed * gain
    first_mean = jnp.mean(scaled, axis=-1, keepdims=True)
    second_mean = jnp.mean(scaled * normed, axis=-1, keepdims=True)
    term = inv_std * (scaled - first_mean - normed * second_mean)
    grad_resid = (cot.astype(F32) + term).astype(BF16)
    gr_ref[...] = grad_resid
    grad_time = nt(grad_resid, fc).astype(BF16)
    grad_time = nt(grad_time, inner_ref[...]).astype(BF16)
    grad_time = tn(turn, grad_time)
    for h in range(6):
        turned[:, h, :] = grad_time[:, h * 128 : (h + 1) * 128]
    gt_ref[...] = turned[...].astype(BF16)


def body(
    time_query,
    time_key,
    time_value,
    residual_in,
    fc_weight,
    norm_gain,
    qkv_weight,
    out_weight,
    bias_slope,
    visible,
    cotangent,
):
    tm, sp = lax.axis_size("tm"), lax.axis_size("space")
    steps, tubes, inner = time_query.shape[1:]
    width = residual_in.shape[-1]
    total = tm * steps
    both = ("tm", "space")
    shape = jax.ShapeDtypeStruct

    def exchange(x, axes):
        return lax.all_to_all(x, axes, split_axis=0, concat_axis=0, tiled=True)

    to_tubes = jnp.asarray(transposed_rows(steps, tubes))
    to_steps = jnp.asarray(transposed_rows(tubes, steps))
    to_order = jnp.asarray(transposed_rows(tm, sp))
    main_map, rest_map = map(jnp.asarray, shard_order(tm))
    inner_map = jnp.asarray(gathered_order(tm, sp, fc_weight.shape[0]))
    width_map = jnp.asarray(gathered_order(tm, sp, qkv_weight.shape[0]))

    me = lax.axis_index("space").astype(jnp.int32).reshape(1)
    shards, rest = pl.pallas_call(
        first_kernel,
        out_shape=(shape((tm, 40, inner), BF16), shape((steps, tubes, 2 * width), BF16)),
        in_specs=[HBM] * 5,
        out_specs=(VMEM, HBM),
        scratch_shapes=[
            pltpu.VMEM(fc_weight.shape, BF16),
            pltpu.VMEM(out_weight.shape, BF16),
            pltpu.VMEM(qkv_weight.shape, BF16),
            pltpu.SemaphoreType.DMA((5,)),
        ],
        compiler_params=params(56),
        name="first",
    )(fc_weight, out_weight, qkv_weight, residual_in, cotangent)
    rest = lax.all_gather(rest, "space", axis=0)
    shards = exchange(shards, "tm")

    send = pl.pallas_call(
        pack_kernel,
        out_shape=shape((tubes, 3 * steps, inner), BF16),
        in_specs=[VMEM] * 4,
        out_specs=VMEM,
        compiler_params=params(16),
        cost_estimate=pl.CostEstimate(flops=10**9, bytes_accessed=4 * 10**6, transcendentals=0),
        name="pack",
    )(time_query, time_key, time_value, to_tubes)

    shards = pl.pallas_call(
        weights_unpack_kernel,
        out_shape=shape((40 * tm, inner), BF16),
        in_specs=[VMEM] * 3,
        out_specs=VMEM,
        compiler_params=params(24),
        name="weights_unpack",
    )(shards, main_map, rest_map)
    weights = lax.all_gather(shards, "space", axis=0)

    send, shards = lax.optimization_barrier((send, shards))
    got = exchange(send, "tm")

    mixed, probs = pl.pallas_call(
        forward_kernel,
        out_shape=(shape((total, 6, 128), BF16), shape((HEADS // 2, total, 2 * total), F32)),
        in_specs=[VMEM],
        out_specs=(VMEM, VMEM),
        scratch_shapes=[pltpu.VMEM((total, 6, 128), F32)],
        compiler_params=params(24),
        cost_estimate=pl.CostEstimate(flops=10**8, bytes_accessed=2 * 10**6, transcendentals=2 * 10**5),
        name="temporal_forward",
    )(got)
    mixed = exchange(mixed, both)

    grad_resid, grad_time = pl.pallas_call(
        middle_kernel,
        out_shape=(shape((total, width), BF16), shape((total, 6, 128), BF16)),
        in_specs=[SMEM, HBM, VMEM, HBM, VMEM, SMEM, VMEM, VMEM, VMEM, HBM, HBM],
        out_specs=(VMEM, VMEM),
        scratch_shapes=[
            pltpu.VMEM((sp, tubes, 2 * width), BF16),
            pltpu.VMEM((inner, inner), BF16),
            pltpu.VMEM((width, width), BF16),
            pltpu.VMEM((sp, 8 * tm, 3 * inner), BF16),
            pltpu.VMEM((sp, 6 * tm, width), BF16),
            pltpu.VMEM((sp, 6 * tm, width), BF16),
            pltpu.VMEM((total, 6, 128), F32),
            pltpu.VMEM((total, 3 * inner), BF16),
            pltpu.VMEM((total, 3 * inner), BF16),
            pltpu.SemaphoreType.DMA((14,)),
        ],
        compiler_params=params(48),
        cost_estimate=pl.CostEstimate(flops=4 * 10**9, bytes_accessed=10**7, transcendentals=2 * 10**5),
        name="middle",
    )(
        me,
        weights,
        mixed,
        rest,
        norm_gain.reshape(1, width),
        bias_slope,
        visible.reshape(total, 1),
        visible.reshape(1, total),
        to_order,
        inner_map,
        width_map,
    )
    grad_resid = lax.all_gather(grad_resid, "space", axis=0)
    grad_time = exchange(grad_time, both)

    back = pl.pallas_call(
        backward_kernel,
        out_shape=shape((tm, 3 * steps, inner), BF16),
        in_specs=[VMEM] * 3,
        out_specs=VMEM,
        scratch_shapes=[pltpu.VMEM((total, 6, 128), F32)],
        compiler_params=params(24),
        cost_estimate=pl.CostEstimate(flops=3 * 10**8, bytes_accessed=2 * 10**6, transcendentals=0),
        name="temporal_backward",
    )(got, probs, grad_time)
    back = exchange(back, "tm")
    outs = pl.pallas_call(
        unpack_kernel,
        out_shape=(shape(time_query.shape, BF16),) * 3 + (shape(residual_in.shape, BF16),),
        in_specs=[SMEM, VMEM, VMEM, HBM],
        out_specs=(VMEM, VMEM, VMEM, HBM),
        scratch_shapes=[pltpu.SemaphoreType.DMA],
        compiler_params=params(56),
        name="unpack",
    )(me, back, to_steps, grad_resid)
    return (outs[3], *outs[:3])


def solution(mesh):
    token = P("dp", "tm", "space", None)
    row = P(("tm", "space"), None)
    in_specs = (token, token, token, token, row, P(), row, row, P(), P("dp", None), token)
    return jax.shard_map(
        body, mesh=mesh, in_specs=in_specs, out_specs=(token,) * 4, check_vma=False
    )
```

```python
import numpy as np
import jax
import jax.numpy as jnp
from jax import lax
from jax.experimental import pallas as pl
from jax.experimental.pallas import tpu as pltpu
from jax.sharding import PartitionSpec as P

HEADS = 12
HD = 64
GRID = 32
SCALE = HD ** (-0.5)
EPSILON = 1e-05
F32 = jnp.float32
BF16 = jnp.bfloat16
VMEM = pl.BlockSpec(memory_space=pltpu.VMEM)
SMEM = pl.BlockSpec(memory_space=pltpu.SMEM)
HBM = pl.BlockSpec(memory_space=pltpu.HBM)


def params(mib):
    return pltpu.CompilerParams(vmem_limit_bytes=mib * 2**20)


def nn(a, b):
    return jnp.dot(a, b, preferred_element_type=F32)


def nt(a, b):
    return lax.dot_general(a, b, (((1,), (1,)), ((), ())), preferred_element_type=F32)


def tn(a, b):
    return lax.dot_general(a, b, (((0,), (0,)), ((), ())), preferred_element_type=F32)


def transposed_rows(outer, inner):
    m = np.zeros((outer * inner, outer * inner), np.float32)
    i, j = np.meshgrid(np.arange(outer), np.arange(inner), indexing="ij")
    m[(j * outer + i).ravel(), (i * inner + j).ravel()] = 1
    return m.astype(BF16)


def gathered_order(tm, sp, rows):
    size = tm * sp * rows
    m = np.zeros((size, size), np.float32)
    a, b, r = (v.ravel() for v in np.meshgrid(*map(np.arange, (tm, sp, rows)), indexing="ij"))
    m[(a * sp + b) * rows + r, (b * tm + a) * rows + r] = 1
    return m.astype(BF16)


def shard_order(tm):
    main = np.zeros((12 * tm, 16 * tm), np.float32)
    rest = np.zeros((3, 3, 4 * tm, 16 * tm), np.float32)
    third = 2 * tm
    for which in range(2):
        for n in range(6 * tm):
            a, r = divmod(n, 6)
            g = which * 6 + r
            main[which * 6 * tm + n, a * 16 + g] = 1
            rest[n // third, g // 4, which * third + n % third, a * 16 + 12 + g % 4] = 1
    return main.astype(BF16), rest.astype(BF16)


def first_kernel(fc_hbm, out_hbm, qkv_hbm, res_hbm, cot_hbm, o_ref, rest_ref, fc_ref, out_ref, qkv_ref, sem):
    width = res_hbm.shape[-1]
    copies = [
        pltpu.make_async_copy(res_hbm.at[0], rest_ref.at[:, :, pl.ds(0, width)], sem.at[0]),
        pltpu.make_async_copy(cot_hbm.at[0], rest_ref.at[:, :, pl.ds(width, width)], sem.at[1]),
        pltpu.make_async_copy(fc_hbm, fc_ref, sem.at[2]),
        pltpu.make_async_copy(out_hbm, out_ref, sem.at[3]),
        pltpu.make_async_copy(qkv_hbm, qkv_ref, sem.at[4]),
    ]
    for c in copies:
        c.start()
    for c in copies[2:]:
        c.wait()
    both = jnp.concatenate([fc_ref[...].astype(F32), out_ref[...].astype(F32)], axis=0)
    tail = both[:, 768:]
    tail = jnp.concatenate([tail[0:4], tail[4:8], tail[8:12]], axis=1)
    qkv = qkv_ref[...].astype(F32)
    block = jnp.concatenate(
        [both[:, :768], tail, qkv[:, :768], qkv[:, 768:1536], qkv[:, 1536:]], axis=0
    )
    o_ref[...] = jnp.broadcast_to(block[None], o_ref.shape).astype(BF16)
    for c in copies[:2]:
        c.wait()


def weights_unpack_kernel(x_ref, main_ref, rest_ref, o_ref):
    tm = x_ref.shape[0]
    x = x_ref[...].astype(F32)
    fo = x[:, 0:16].reshape(16 * tm, 768).astype(BF16)
    n = 8 * tm
    for j in range(3):
        o_ref[pl.ds(j * n, n), :] = x[:, 16 + 8 * j : 24 + 8 * j].reshape(n, 768).astype(BF16)
    o_ref[pl.ds(3 * n, 12 * tm), :] = nn(main_ref[...], fo).astype(BF16)
    for j in range(3):
        part = nn(rest_ref[j, 0], fo[:, :256])
        part += nn(rest_ref[j, 1], fo[:, 256:512])
        part += nn(rest_ref[j, 2], fo[:, 512:])
        o_ref[pl.ds(3 * n + 12 * tm, 4 * tm), pl.ds(j * 256, 256)] = part.astype(BF16)


def pack_kernel(q_ref, k_ref, v_ref, turn_ref, o_ref):
    steps, tubes, inner = q_ref.shape[1:]
    rows = steps * tubes
    parts = [
        nn(turn_ref[...], ref[0].reshape(rows, inner)).reshape(tubes, steps, inner)
        for ref in (q_ref, k_ref, v_ref)
    ]
    o_ref[...] = jnp.concatenate(parts, axis=1).astype(BF16)


def unpack_kernel(me_ref, x_ref, turn_ref, gr_hbm, *refs):
    outs, gr_out, sem = refs[:3], refs[3], refs[4]
    mine = outs[0].shape[2]
    at = pl.multiple_of(me_ref[0] * mine, mine)
    copy = pltpu.make_async_copy(gr_hbm.at[:, pl.ds(at, mine), :], gr_out.at[0], sem)
    copy.start()
    x = x_ref[...].astype(F32)
    tubes, steps = x.shape[0], x.shape[1] // 3
    for j, o_ref in enumerate(outs):
        part = x[:, j * steps : (j + 1) * steps].reshape(tubes * steps, -1).astype(BF16)
        o_ref[0] = nn(turn_ref[...], part).astype(BF16).reshape(steps, tubes, -1)
    copy.wait()


def lane_masks(rows):
    lane = lax.broadcasted_iota(jnp.int32, (rows, 2 * HD), 1)
    return lane < HD


def stacked(block, first):
    zero = jnp.zeros_like(block)
    return jnp.concatenate([jnp.where(first, block, zero), jnp.where(first, zero, block)], axis=0)


def softmax(scores):
    exponent = jnp.exp(scores - jnp.max(scores, axis=-1, keepdims=True))
    return exponent / jnp.sum(exponent, axis=-1, keepdims=True)


def pair_probs(q, k2, bias0=None, bias1=None):
    n = q.shape[0]
    scores = nt(q, k2) * SCALE
    s0, s1 = scores[:, :n], scores[:, n:]
    if bias0 is not None:
        s0, s1 = s0 + bias0, s1 + bias1
    return softmax(s0), softmax(s1)


def pair_backward(p0, p1, q, k, v, g, first):
    n = q.shape[0]
    k2, v2, q2, g2 = (stacked(x, first) for x in (k, v, q, g))
    gp = nt(g, v2)
    g0, g1 = gp[:, :n], gp[:, n:]
    d0 = (p0 * (g0 - jnp.sum(p0 * g0, axis=-1, keepdims=True))).astype(BF16)
    d1 = (p1 * (g1 - jnp.sum(p1 * g1, axis=-1, keepdims=True))).astype(BF16)
    grad_q = nn(jnp.concatenate([d0, d1], axis=1), k2)
    grad_k = tn(jnp.concatenate([d0, d1], axis=0), q2)
    grad_v = tn(jnp.concatenate([p0.astype(BF16), p1.astype(BF16)], axis=0), g2)
    return grad_q * SCALE, grad_k * SCALE, grad_v


def qkv_of(x, steps):
    return [
        x[:, j * steps : (j + 1) * steps].reshape(x.shape[0] * steps, -1).astype(BF16)
        for j in range(3)
    ]


def forward_kernel(x_ref, o_ref, p_ref, turned):
    x = x_ref[...].astype(F32)
    q, k, v = qkv_of(x, x.shape[1] // 3)
    n = q.shape[0]
    first = lane_masks(n)
    for h in range(HEADS // 2):
        at = slice(h * 128, (h + 1) * 128)
        p0, p1 = pair_probs(q[:, at], stacked(k[:, at], first))
        p_ref[h, :, 0:n] = p0
        p_ref[h, :, n : 2 * n] = p1
        both = jnp.concatenate([p0.astype(BF16), p1.astype(BF16)], axis=1)
        turned[:, h, :] = nn(both, stacked(v[:, at], first))
    o_ref[...] = turned[...].astype(BF16)


def backward_kernel(x_ref, p_ref, g_ref, o_ref, turned):
    x = x_ref[...].astype(F32)
    steps = x.shape[1] // 3
    q, k, v = qkv_of(x, steps)
    n = q.shape[0]
    turned[...] = g_ref[...].astype(F32)
    first = lane_masks(n)
    for h in range(HEADS // 2):
        at = slice(h * 128, (h + 1) * 128)
        grads = pair_backward(
            p_ref[h, :, 0:n],
            p_ref[h, :, n : 2 * n],
            q[:, at],
            k[:, at],
            v[:, at],
            turned[:, h, :].astype(BF16),
            first,
        )
        joined = jnp.concatenate([d.reshape(n // steps, steps, 128) for d in grads], axis=1)
        o_ref[:, :, at] = joined.astype(BF16)


def middle_kernel(
    me_ref, w_hbm, x_ref, rest_hbm, gain_ref, slope_ref, row_ref, col_ref, turn_ref, inner_hbm, width_hbm,
    gr_ref, gt_ref, rest_v, inner_ref, width_v, qkv_v, fc_v, out_v, turned, proj, joined, sem,
):
    sp = w_hbm.shape[0]
    tm = w_hbm.shape[1] // 40
    n, third = 8 * tm, 2 * tm
    copies = []

    def load(src, dst):
        copies.append(pltpu.make_async_copy(src, dst, sem.at[len(copies)]))
        copies[-1].start()

    load(inner_hbm, inner_ref)
    load(rest_hbm.at[:, me_ref[0]], rest_v)
    at = 3 * n
    for dst, base, tail in (
        (fc_v, at, at + 12 * tm),
        (out_v, at + 6 * tm, at + 12 * tm + third),
    ):
        load(w_hbm.at[:, pl.ds(base, 6 * tm), :], dst.at[:, :, pl.ds(0, 768)])
        for j in range(3):
            load(
                w_hbm.at[:, pl.ds(tail, third), pl.ds(j * 256, 256)],
                dst.at[:, pl.ds(j * third, third), pl.ds(768, 256)],
            )
    load(width_hbm, width_v)
    for j in range(3):
        load(w_hbm.at[:, pl.ds(j * n, n), :], qkv_v.at[:, :, pl.ds(j * 768, 768)])

    tokens = x_ref.shape[0]
    width = gain_ref.shape[1]
    inner = 768
    rows, cols = row_ref[...], col_ref[...]
    distance = jnp.abs((rows >> 5) - (cols >> 5)) + jnp.abs((rows & 31) - (cols & 31))
    distance = distance.astype(F32)
    gain = gain_ref[...]
    turn = turn_ref[...]
    turned[...] = x_ref[...].astype(F32)
    mixed = jnp.concatenate([turned[:, h, :] for h in range(6)], axis=1).astype(BF16)
    mixed = nn(turn, mixed).astype(BF16)

    for c in copies[:6]:
        c.wait()
    mixed = nn(mixed, inner_ref[...]).astype(BF16)
    rest = rest_v[...].reshape(tokens, 2 * width)
    cot = rest[:, width:]
    fc = fc_v[...].reshape(inner, width)
    hidden = rest[:, :width].astype(F32) + nn(mixed, fc)
    centred = hidden - jnp.mean(hidden, axis=-1, keepdims=True)
    inv_std = lax.rsqrt(jnp.mean(centred * centred, axis=-1, keepdims=True) + EPSILON)
    normed = centred * inv_std
    normed_in = (normed * gain).astype(BF16)

    for c in copies[6:11]:
        c.wait()
    normed_in = nn(normed_in, width_v[...]).astype(BF16)
    grad_mixed = nt(cot, out_v[...].reshape(inner, width)).astype(BF16)
    grad_mixed = nt(grad_mixed, inner_ref[...]).astype(BF16)

    for c in copies[11:]:
        c.wait()
    qkv = qkv_v[...].reshape(width, 3 * inner)
    proj[...] = nn(normed_in, qkv).astype(BF16)

    first = lane_masks(tokens)
    for h in range(HEADS // 2):
        q, k, v = (proj[:, j * inner + h * 128 : j * inner + (h + 1) * 128] for j in range(3))
        g = grad_mixed[:, h * 128 : (h + 1) * 128]
        p0, p1 = pair_probs(
            q, stacked(k, first), -slope_ref[2 * h] * distance, -slope_ref[2 * h + 1] * distance
        )
        for j, d in enumerate(pair_backward(p0, p1, q, k, v, g, first)):
            joined[:, j * inner + h * 128 : j * inner + (h + 1) * 128] = d.astype(BF16)

    grad_normed = nt(joined[...], qkv).astype(BF16)
    grad_normed = nt(grad_normed, width_v[...])
    scaled = grad_normed * gain
    first_mean = jnp.mean(scaled, axis=-1, keepdims=True)
    second_mean = jnp.mean(scaled * normed, axis=-1, keepdims=True)
    term = inv_std * (scaled - first_mean - normed * second_mean)
    grad_resid = (cot.astype(F32) + term).astype(BF16)
    gr_ref[...] = grad_resid
    grad_time = nt(grad_resid, fc).astype(BF16)
    grad_time = nt(grad_time, inner_ref[...]).astype(BF16)
    grad_time = tn(turn, grad_time)
    for h in range(6):
        turned[:, h, :] = grad_time[:, h * 128 : (h + 1) * 128]
    gt_ref[...] = turned[...].astype(BF16)


def body(
    time_query,
    time_key,
    time_value,
    residual_in,
    fc_weight,
    norm_gain,
    qkv_weight,
    out_weight,
    bias_slope,
    visible,
    cotangent,
):
    tm, sp = lax.axis_size("tm"), lax.axis_size("space")
    steps, tubes, inner = time_query.shape[1:]
    width = residual_in.shape[-1]
    total = tm * steps
    both = ("tm", "space")
    shape = jax.ShapeDtypeStruct

    def exchange(x, axes):
        return lax.all_to_all(x, axes, split_axis=0, concat_axis=0, tiled=True)

    to_tubes = jnp.asarray(transposed_rows(steps, tubes))
    to_steps = jnp.asarray(transposed_rows(tubes, steps))
    to_order = jnp.asarray(transposed_rows(tm, sp))
    main_map, rest_map = map(jnp.asarray, shard_order(tm))
    inner_map = jnp.asarray(gathered_order(tm, sp, fc_weight.shape[0]))
    width_map = jnp.asarray(gathered_order(tm, sp, qkv_weight.shape[0]))

    me = lax.axis_index("space").astype(jnp.int32).reshape(1)
    shards, rest = pl.pallas_call(
        first_kernel,
        out_shape=(shape((tm, 40, inner), BF16), shape((steps, tubes, 2 * width), BF16)),
        in_specs=[HBM] * 5,
        out_specs=(VMEM, VMEM),
        scratch_shapes=[
            pltpu.VMEM(fc_weight.shape, BF16),
            pltpu.VMEM(out_weight.shape, BF16),
            pltpu.VMEM(qkv_weight.shape, BF16),
            pltpu.SemaphoreType.DMA((5,)),
        ],
        compiler_params=params(56),
        name="first",
    )(fc_weight, out_weight, qkv_weight, residual_in, cotangent)
    rest = lax.all_gather(rest, "space", axis=0)
    shards = exchange(shards, "tm")

    send = pl.pallas_call(
        pack_kernel,
        out_shape=shape((tubes, 3 * steps, inner), BF16),
        in_specs=[VMEM] * 4,
        out_specs=VMEM,
        compiler_params=params(16),
        cost_estimate=pl.CostEstimate(flops=10**9, bytes_accessed=4 * 10**6, transcendentals=0),
        name="pack",
    )(time_query, time_key, time_value, to_tubes)

    shards = pl.pallas_call(
        weights_unpack_kernel,
        out_shape=shape((40 * tm, inner), BF16),
        in_specs=[VMEM] * 3,
        out_specs=VMEM,
        compiler_params=params(24),
        name="weights_unpack",
    )(shards, main_map, rest_map)
    weights = lax.all_gather(shards, "space", axis=0)

    send, shards = lax.optimization_barrier((send, shards))
    got = exchange(send, "tm")

    mixed, probs = pl.pallas_call(
        forward_kernel,
        out_shape=(shape((total, 6, 128), BF16), shape((HEADS // 2, total, 2 * total), F32)),
        in_specs=[VMEM],
        out_specs=(VMEM, VMEM),
        scratch_shapes=[pltpu.VMEM((total, 6, 128), F32)],
        compiler_params=params(56),
        cost_estimate=pl.CostEstimate(flops=10**8, bytes_accessed=2 * 10**6, transcendentals=2 * 10**5),
        name="temporal_forward",
    )(got)
    mixed = exchange(mixed, both)

    grad_resid, grad_time = pl.pallas_call(
        middle_kernel,
        out_shape=(shape((total, width), BF16), shape((total, 6, 128), BF16)),
        in_specs=[SMEM, HBM, VMEM, HBM, VMEM, SMEM, VMEM, VMEM, VMEM, HBM, HBM],
        out_specs=(VMEM, VMEM),
        scratch_shapes=[
            pltpu.VMEM((sp, tubes, 2 * width), BF16),
            pltpu.VMEM((inner, inner), BF16),
            pltpu.VMEM((width, width), BF16),
            pltpu.VMEM((sp, 8 * tm, 3 * inner), BF16),
            pltpu.VMEM((sp, 6 * tm, width), BF16),
            pltpu.VMEM((sp, 6 * tm, width), BF16),
            pltpu.VMEM((total, 6, 128), F32),
            pltpu.VMEM((total, 3 * inner), BF16),
            pltpu.VMEM((total, 3 * inner), BF16),
            pltpu.SemaphoreType.DMA((14,)),
        ],
        compiler_params=params(56),
        cost_estimate=pl.CostEstimate(flops=4 * 10**9, bytes_accessed=10**7, transcendentals=2 * 10**5),
        name="middle",
    )(
        me,
        weights,
        mixed,
        rest,
        norm_gain.reshape(1, width),
        bias_slope,
        visible.reshape(total, 1),
        visible.reshape(1, total),
        to_order,
        inner_map,
        width_map,
    )
    grad_resid = lax.all_gather(grad_resid, "space", axis=0)
    grad_time = exchange(grad_time, both)

    back = pl.pallas_call(
        backward_kernel,
        out_shape=shape((tm, 3 * steps, inner), BF16),
        in_specs=[VMEM] * 3,
        out_specs=VMEM,
        scratch_shapes=[pltpu.VMEM((total, 6, 128), F32)],
        compiler_params=params(56),
        cost_estimate=pl.CostEstimate(flops=3 * 10**8, bytes_accessed=2 * 10**6, transcendentals=0),
        name="temporal_backward",
    )(got, probs, grad_time)
    back = exchange(back, "tm")
    outs = pl.pallas_call(
        unpack_kernel,
        out_shape=(shape(time_query.shape, BF16),) * 3 + (shape(residual_in.shape, BF16),),
        in_specs=[SMEM, VMEM, VMEM, HBM],
        out_specs=(VMEM, VMEM, VMEM, VMEM),
        scratch_shapes=[pltpu.SemaphoreType.DMA],
        compiler_params=params(56),
        name="unpack",
    )(me, back, to_steps, grad_resid)
    return (outs[3], *outs[:3])


def solution(mesh):
    token = P("dp", "tm", "space", None)
    row = P(("tm", "space"), None)
    in_specs = (token, token, token, token, row, P(), row, row, P(), P("dp", None), token)
    return jax.shard_map(
        body, mesh=mesh, in_specs=in_specs, out_specs=(token,) * 4, check_vma=False
    )
```

```python
import numpy as np
import jax
import jax.numpy as jnp
from jax import lax
from jax.experimental import pallas as pl
from jax.experimental.pallas import tpu as pltpu
from jax.sharding import PartitionSpec as P

HEADS = 12
HD = 64
GRID = 32
SCALE = HD ** (-0.5)
EPSILON = 1e-05
F32 = jnp.float32
BF16 = jnp.bfloat16
VMEM = pl.BlockSpec(memory_space=pltpu.VMEM)
SMEM = pl.BlockSpec(memory_space=pltpu.SMEM)
HBM = pl.BlockSpec(memory_space=pltpu.HBM)


def params(mib):
    return pltpu.CompilerParams(vmem_limit_bytes=mib * 2**20)


def nn(a, b):
    return jnp.dot(a, b, preferred_element_type=F32)


def nt(a, b):
    return lax.dot_general(a, b, (((1,), (1,)), ((), ())), preferred_element_type=F32)


def tn(a, b):
    return lax.dot_general(a, b, (((0,), (0,)), ((), ())), preferred_element_type=F32)


def transposed_rows(outer, inner):
    m = np.zeros((outer * inner, outer * inner), np.float32)
    i, j = np.meshgrid(np.arange(outer), np.arange(inner), indexing="ij")
    m[(j * outer + i).ravel(), (i * inner + j).ravel()] = 1
    return m.astype(BF16)


def gathered_order(tm, sp, rows):
    size = tm * sp * rows
    at = lax.broadcasted_iota(jnp.int32, (size, 1), 0)
    block = (at * (65536 // rows + 1)) >> 16
    a = (block * (65536 // sp + 1)) >> 16
    to = ((block - a * sp) * tm + a) * rows + at - block * rows
    column = lax.broadcasted_iota(jnp.int32, (size, size), 1)
    return jnp.where(column == to, 1.0, 0.0).astype(BF16)


def sixth(n):
    return (n * 10923) >> 16


def main_order(tm):
    at = lax.broadcasted_iota(jnp.int32, (12 * tm, 1), 0)
    which = jnp.where(at >= 6 * tm, 1, 0)
    n = at - which * 6 * tm
    a = sixth(n)
    source = a * 16 + which * 6 + n - a * 6
    column = lax.broadcasted_iota(jnp.int32, (12 * tm, 16 * tm), 1)
    return jnp.where(column == source, 1.0, 0.0).astype(BF16)


def rest_order(tm, to, src):
    third = 2 * tm
    at = lax.broadcasted_iota(jnp.int32, (2 * third, 1), 0)
    which = jnp.where(at >= third, 1, 0)
    n = at - which * third + to * third
    a = sixth(n)
    g = which * 6 + n - a * 6
    source = jnp.where((g >> 2) == src, a * 16 + 12 + (g & 3), -1)
    column = lax.broadcasted_iota(jnp.int32, (2 * third, 16 * tm), 1)
    return jnp.where(column == source, 1.0, 0.0).astype(BF16)


def first_kernel(fc_hbm, out_hbm, qkv_hbm, res_hbm, cot_hbm, o_ref, rest_ref, fc_ref, out_ref, qkv_ref, sem):
    width = res_hbm.shape[-1]
    copies = [
        pltpu.make_async_copy(res_hbm.at[0], rest_ref.at[:, :, pl.ds(0, width)], sem.at[0]),
        pltpu.make_async_copy(cot_hbm.at[0], rest_ref.at[:, :, pl.ds(width, width)], sem.at[1]),
        pltpu.make_async_copy(fc_hbm, fc_ref, sem.at[2]),
        pltpu.make_async_copy(out_hbm, out_ref, sem.at[3]),
        pltpu.make_async_copy(qkv_hbm, qkv_ref, sem.at[4]),
    ]
    for c in copies:
        c.start()
    for c in copies[2:]:
        c.wait()
    both = jnp.concatenate([fc_ref[...].astype(F32), out_ref[...].astype(F32)], axis=0)
    tail = both[:, 768:]
    tail = jnp.concatenate([tail[0:4], tail[4:8], tail[8:12]], axis=1)
    qkv = qkv_ref[...].astype(F32)
    block = jnp.concatenate(
        [both[:, :768], tail, qkv[:, :768], qkv[:, 768:1536], qkv[:, 1536:]], axis=0
    )
    o_ref[...] = jnp.broadcast_to(block[None], o_ref.shape).astype(BF16)
    for c in copies[:2]:
        c.wait()


def weights_unpack_kernel(x_ref, o_ref):
    tm = x_ref.shape[0]
    x = x_ref[...].astype(F32)
    fo = x[:, 0:16].reshape(16 * tm, 768).astype(BF16)
    n = 8 * tm
    for j in range(3):
        o_ref[pl.ds(j * n, n), :] = x[:, 16 + 8 * j : 24 + 8 * j].reshape(n, 768).astype(BF16)
    o_ref[pl.ds(3 * n, 12 * tm), :] = nn(main_order(tm), fo).astype(BF16)
    for j in range(3):
        part = nn(rest_order(tm, j, 0), fo[:, :256])
        part += nn(rest_order(tm, j, 1), fo[:, 256:512])
        part += nn(rest_order(tm, j, 2), fo[:, 512:])
        o_ref[pl.ds(3 * n + 12 * tm, 4 * tm), pl.ds(j * 256, 256)] = part.astype(BF16)


def pack_kernel(q_ref, k_ref, v_ref, turn_ref, o_ref):
    steps, tubes, inner = q_ref.shape[1:]
    rows = steps * tubes
    parts = [
        nn(turn_ref[...], ref[0].reshape(rows, inner)).reshape(tubes, steps, inner)
        for ref in (q_ref, k_ref, v_ref)
    ]
    o_ref[...] = jnp.concatenate(parts, axis=1).astype(BF16)


def slice_kernel(me_ref, gr_hbm, o_ref, sem):
    mine = o_ref.shape[2]
    at = pl.multiple_of(me_ref[0] * mine, mine)
    copy = pltpu.make_async_copy(gr_hbm.at[:, pl.ds(at, mine), :], o_ref.at[0], sem)
    copy.start()
    copy.wait()


def unpack_kernel(x_ref, turn_ref, *outs):
    x = x_ref[...].astype(F32)
    tubes, steps = x.shape[0], x.shape[1] // 3
    for j, o_ref in enumerate(outs):
        part = x[:, j * steps : (j + 1) * steps].reshape(tubes * steps, -1).astype(BF16)
        o_ref[0] = nn(turn_ref[...], part).astype(BF16).reshape(steps, tubes, -1)


def lane_masks(rows):
    lane = lax.broadcasted_iota(jnp.int32, (rows, 2 * HD), 1)
    return lane < HD


def stacked(block, first):
    zero = jnp.zeros_like(block)
    return jnp.concatenate([jnp.where(first, block, zero), jnp.where(first, zero, block)], axis=0)


def softmax(scores):
    exponent = jnp.exp(scores - jnp.max(scores, axis=-1, keepdims=True))
    return exponent / jnp.sum(exponent, axis=-1, keepdims=True)


def pair_probs(q, k2, bias0=None, bias1=None):
    n = q.shape[0]
    scores = nt(q, k2) * SCALE
    s0, s1 = scores[:, :n], scores[:, n:]
    if bias0 is not None:
        s0, s1 = s0 + bias0, s1 + bias1
    return softmax(s0), softmax(s1)


def pair_backward(p0, p1, q, k, v, g, first):
    n = q.shape[0]
    k2, v2, q2, g2 = (stacked(x, first) for x in (k, v, q, g))
    gp = nt(g, v2)
    g0, g1 = gp[:, :n], gp[:, n:]
    d0 = (p0 * (g0 - jnp.sum(p0 * g0, axis=-1, keepdims=True))).astype(BF16)
    d1 = (p1 * (g1 - jnp.sum(p1 * g1, axis=-1, keepdims=True))).astype(BF16)
    grad_q = nn(jnp.concatenate([d0, d1], axis=1), k2)
    grad_k = tn(jnp.concatenate([d0, d1], axis=0), q2)
    grad_v = tn(jnp.concatenate([p0.astype(BF16), p1.astype(BF16)], axis=0), g2)
    return grad_q * SCALE, grad_k * SCALE, grad_v


def qkv_of(x, steps):
    return [
        x[:, j * steps : (j + 1) * steps].reshape(x.shape[0] * steps, -1).astype(BF16)
        for j in range(3)
    ]


def forward_kernel(x_ref, o_ref, turned):
    x = x_ref[...].astype(F32)
    q, k, v = qkv_of(x, x.shape[1] // 3)
    n = q.shape[0]
    first = lane_masks(n)
    for h in range(HEADS // 2):
        at = slice(h * 128, (h + 1) * 128)
        p0, p1 = pair_probs(q[:, at], stacked(k[:, at], first))
        both = jnp.concatenate([p0.astype(BF16), p1.astype(BF16)], axis=1)
        turned[:, h, :] = nn(both, stacked(v[:, at], first))
    o_ref[...] = turned[...].astype(BF16)


def backward_kernel(x_ref, g_ref, o_ref, turned):
    x = x_ref[...].astype(F32)
    steps = x.shape[1] // 3
    q, k, v = qkv_of(x, steps)
    n = q.shape[0]
    turned[...] = g_ref[...].astype(F32)
    first = lane_masks(n)
    for h in range(HEADS // 2):
        at = slice(h * 128, (h + 1) * 128)
        p0, p1 = pair_probs(q[:, at], stacked(k[:, at], first))
        grads = pair_backward(
            p0,
            p1,
            q[:, at],
            k[:, at],
            v[:, at],
            turned[:, h, :].astype(BF16),
            first,
        )
        joined = jnp.concatenate([d.reshape(n // steps, steps, 128) for d in grads], axis=1)
        o_ref[:, :, at] = joined.astype(BF16)


def middle_kernel(
    me_ref, w_hbm, x_ref, rest_hbm, gain_ref, slope_ref, row_ref, col_ref, turn_ref,
    gr_ref, gt_ref, rest_v, inner_ref, width_v, qkv_v, fc_v, out_v, turned, proj, joined, sem,
):
    sp = w_hbm.shape[0]
    tm = w_hbm.shape[1] // 40
    n, third = 8 * tm, 2 * tm
    copies = []

    def load(src, dst):
        copies.append(pltpu.make_async_copy(src, dst, sem.at[len(copies)]))
        copies[-1].start()

    load(rest_hbm.at[:, me_ref[0]], rest_v)
    at = 3 * n
    for dst, base, tail in (
        (fc_v, at, at + 12 * tm),
        (out_v, at + 6 * tm, at + 12 * tm + third),
    ):
        load(w_hbm.at[:, pl.ds(base, 6 * tm), :], dst.at[:, :, pl.ds(0, 768)])
        for j in range(3):
            load(
                w_hbm.at[:, pl.ds(tail, third), pl.ds(j * 256, 256)],
                dst.at[:, pl.ds(j * third, third), pl.ds(768, 256)],
            )
    for j in range(3):
        load(w_hbm.at[:, pl.ds(j * n, n), :], qkv_v.at[:, :, pl.ds(j * 768, 768)])

    tokens = x_ref.shape[0]
    width = gain_ref.shape[1]
    inner = 768
    rows, cols = row_ref[...], col_ref[...]
    distance = jnp.abs((rows >> 5) - (cols >> 5)) + jnp.abs((rows & 31) - (cols & 31))
    distance = distance.astype(F32)
    gain = gain_ref[...]
    turn = turn_ref[...]
    turned[...] = x_ref[...].astype(F32)
    mixed = jnp.concatenate([turned[:, h, :] for h in range(6)], axis=1).astype(BF16)
    mixed = nn(turn, mixed).astype(BF16)

    inner_ref[...] = gathered_order(tm, sp, 6)
    width_v[...] = gathered_order(tm, sp, 8)
    mixed = nn(mixed, inner_ref[...]).astype(BF16)
    for c in copies[:5]:
        c.wait()
    rest = rest_v[...].reshape(tokens, 2 * width)
    cot = rest[:, width:]
    fc = fc_v[...].reshape(inner, width)
    hidden = rest[:, :width].astype(F32) + nn(mixed, fc)
    centred = hidden - jnp.mean(hidden, axis=-1, keepdims=True)
    inv_std = lax.rsqrt(jnp.mean(centred * centred, axis=-1, keepdims=True) + EPSILON)
    normed = centred * inv_std
    normed_in = (normed * gain).astype(BF16)

    for c in copies[5:9]:
        c.wait()
    normed_in = nn(normed_in, width_v[...]).astype(BF16)
    grad_mixed = nt(cot, out_v[...].reshape(inner, width)).astype(BF16)
    grad_mixed = nt(grad_mixed, inner_ref[...]).astype(BF16)

    for c in copies[9:]:
        c.wait()
    qkv = qkv_v[...].reshape(width, 3 * inner)
    proj[...] = nn(normed_in, qkv).astype(BF16)

    first = lane_masks(tokens)
    for h in range(HEADS // 2):
        q, k, v = (proj[:, j * inner + h * 128 : j * inner + (h + 1) * 128] for j in range(3))
        g = grad_mixed[:, h * 128 : (h + 1) * 128]
        p0, p1 = pair_probs(
            q, stacked(k, first), -slope_ref[2 * h] * distance, -slope_ref[2 * h + 1] * distance
        )
        for j, d in enumerate(pair_backward(p0, p1, q, k, v, g, first)):
            joined[:, j * inner + h * 128 : j * inner + (h + 1) * 128] = d.astype(BF16)

    grad_normed = nt(joined[...], qkv).astype(BF16)
    grad_normed = nt(grad_normed, width_v[...])
    scaled = grad_normed * gain
    first_mean = jnp.mean(scaled, axis=-1, keepdims=True)
    second_mean = jnp.mean(scaled * normed, axis=-1, keepdims=True)
    term = inv_std * (scaled - first_mean - normed * second_mean)
    grad_resid = (cot.astype(F32) + term).astype(BF16)
    gr_ref[...] = grad_resid
    grad_time = nt(grad_resid, fc).astype(BF16)
    grad_time = nt(grad_time, inner_ref[...]).astype(BF16)
    grad_time = tn(turn, grad_time)
    for h in range(6):
        turned[:, h, :] = grad_time[:, h * 128 : (h + 1) * 128]
    gt_ref[...] = turned[...].astype(BF16)


def body(
    time_query,
    time_key,
    time_value,
    residual_in,
    fc_weight,
    norm_gain,
    qkv_weight,
    out_weight,
    bias_slope,
    visible,
    cotangent,
):
    tm, sp = lax.axis_size("tm"), lax.axis_size("space")
    steps, tubes, inner = time_query.shape[1:]
    width = residual_in.shape[-1]
    total = tm * steps
    both = ("tm", "space")
    shape = jax.ShapeDtypeStruct

    def exchange(x, axes):
        return lax.all_to_all(x, axes, split_axis=0, concat_axis=0, tiled=True)

    to_tubes = jnp.asarray(transposed_rows(steps, tubes))
    to_steps = jnp.asarray(transposed_rows(tubes, steps))
    to_order = jnp.asarray(transposed_rows(tm, sp))
    me = lax.axis_index("space").astype(jnp.int32).reshape(1)
    shards, rest = pl.pallas_call(
        first_kernel,
        out_shape=(shape((tm, 40, inner), BF16), shape((steps, tubes, 2 * width), BF16)),
        in_specs=[HBM] * 5,
        out_specs=(VMEM, VMEM),
        scratch_shapes=[
            pltpu.VMEM(fc_weight.shape, BF16),
            pltpu.VMEM(out_weight.shape, BF16),
            pltpu.VMEM(qkv_weight.shape, BF16),
            pltpu.SemaphoreType.DMA((5,)),
        ],
        compiler_params=params(56),
        name="first",
    )(fc_weight, out_weight, qkv_weight, residual_in, cotangent)
    rest = lax.all_gather(rest, "space", axis=0)
    shards = exchange(shards, "tm")

    send = pl.pallas_call(
        pack_kernel,
        out_shape=shape((tubes, 3 * steps, inner), BF16),
        in_specs=[VMEM] * 4,
        out_specs=VMEM,
        compiler_params=params(16),
        cost_estimate=pl.CostEstimate(flops=10**9, bytes_accessed=4 * 10**6, transcendentals=0),
        name="pack",
    )(time_query, time_key, time_value, to_tubes)

    shards = pl.pallas_call(
        weights_unpack_kernel,
        out_shape=shape((40 * tm, inner), BF16),
        in_specs=[VMEM],
        out_specs=VMEM,
        compiler_params=params(24),
        name="weights_unpack",
    )(shards)
    weights = lax.all_gather(shards, "space", axis=0)

    send, shards = lax.optimization_barrier((send, shards))
    got = exchange(send, "tm")

    mixed = pl.pallas_call(
        forward_kernel,
        out_shape=shape((total, 6, 128), BF16),
        in_specs=[VMEM],
        out_specs=VMEM,
        scratch_shapes=[pltpu.VMEM((total, 6, 128), F32)],
        compiler_params=params(24),
        cost_estimate=pl.CostEstimate(flops=10**8, bytes_accessed=2 * 10**6, transcendentals=2 * 10**5),
        name="temporal_forward",
    )(got)
    mixed = exchange(mixed, both)

    grad_resid, grad_time = pl.pallas_call(
        middle_kernel,
        out_shape=(shape((total, width), BF16), shape((total, 6, 128), BF16)),
        in_specs=[SMEM, HBM, VMEM, HBM, VMEM, SMEM, VMEM, VMEM, VMEM],
        out_specs=(VMEM, VMEM),
        scratch_shapes=[
            pltpu.VMEM((sp, tubes, 2 * width), BF16),
            pltpu.VMEM((inner, inner), BF16),
            pltpu.VMEM((width, width), BF16),
            pltpu.VMEM((sp, 8 * tm, 3 * inner), BF16),
            pltpu.VMEM((sp, 6 * tm, width), BF16),
            pltpu.VMEM((sp, 6 * tm, width), BF16),
            pltpu.VMEM((total, 6, 128), F32),
            pltpu.VMEM((total, 3 * inner), BF16),
            pltpu.VMEM((total, 3 * inner), BF16),
            pltpu.SemaphoreType.DMA((12,)),
        ],
        compiler_params=params(56),
        cost_estimate=pl.CostEstimate(flops=4 * 10**9, bytes_accessed=10**7, transcendentals=2 * 10**5),
        name="middle",
    )(
        me,
        weights,
        mixed,
        rest,
        norm_gain.reshape(1, width),
        bias_slope,
        visible.reshape(total, 1),
        visible.reshape(1, total),
        to_order,
    )
    grad_resid = lax.all_gather(grad_resid, "space", axis=0)
    grad_time = exchange(grad_time, both)

    back = pl.pallas_call(
        backward_kernel,
        out_shape=shape((tm, 3 * steps, inner), BF16),
        in_specs=[VMEM] * 2,
        out_specs=VMEM,
        scratch_shapes=[pltpu.VMEM((total, 6, 128), F32)],
        compiler_params=params(24),
        cost_estimate=pl.CostEstimate(flops=3 * 10**8, bytes_accessed=2 * 10**6, transcendentals=0),
        name="temporal_backward",
    )(got, grad_time)
    back, grad_resid = lax.optimization_barrier((back, grad_resid))
    back = exchange(back, "tm")
    outs = pl.pallas_call(
        unpack_kernel,
        out_shape=(shape(time_query.shape, BF16),) * 3,
        in_specs=[VMEM, VMEM],
        out_specs=(VMEM,) * 3,
        compiler_params=params(24),
        name="unpack",
    )(back, to_steps)
    grad_resid = pl.pallas_call(
        slice_kernel,
        out_shape=shape(residual_in.shape, BF16),
        in_specs=[SMEM, HBM],
        out_specs=VMEM,
        scratch_shapes=[pltpu.SemaphoreType.DMA],
        compiler_params=params(56),
        cost_estimate=pl.CostEstimate(flops=10**9, bytes_accessed=4 * 10**6, transcendentals=0),
        name="slice",
    )(me, grad_resid)
    return (grad_resid, *outs)


def solution(mesh):
    token = P("dp", "tm", "space", None)
    row = P(("tm", "space"), None)
    in_specs = (token, token, token, token, row, P(), row, row, P(), P("dp", None), token)
    return jax.shard_map(
        body, mesh=mesh, in_specs=in_specs, out_specs=(token,) * 4, check_vma=False
    )
```

```python
import numpy as np
import jax
import jax.numpy as jnp
from jax import lax
from jax.experimental import pallas as pl
from jax.experimental.pallas import tpu as pltpu
from jax.sharding import PartitionSpec as P

HEADS = 12
HD = 64
GRID = 32
SCALE = HD ** (-0.5)
EPSILON = 1e-05
F32 = jnp.float32
BF16 = jnp.bfloat16
VMEM = pl.BlockSpec(memory_space=pltpu.VMEM)
SMEM = pl.BlockSpec(memory_space=pltpu.SMEM)
HBM = pl.BlockSpec(memory_space=pltpu.HBM)


def params(mib):
    return pltpu.CompilerParams(vmem_limit_bytes=mib * 2**20)


def nn(a, b):
    return jnp.dot(a, b, preferred_element_type=F32)


def nt(a, b):
    return lax.dot_general(a, b, (((1,), (1,)), ((), ())), preferred_element_type=F32)


def tn(a, b):
    return lax.dot_general(a, b, (((0,), (0,)), ((), ())), preferred_element_type=F32)


def transposed_rows(outer, inner):
    m = np.zeros((outer * inner, outer * inner), np.float32)
    i, j = np.meshgrid(np.arange(outer), np.arange(inner), indexing="ij")
    m[(j * outer + i).ravel(), (i * inner + j).ravel()] = 1
    return m.astype(BF16)


def gathered_order(tm, sp, rows):
    size = tm * sp * rows
    at = lax.broadcasted_iota(jnp.int32, (size, 1), 0)
    block = (at * (65536 // rows + 1)) >> 16
    a = (block * (65536 // sp + 1)) >> 16
    to = ((block - a * sp) * tm + a) * rows + at - block * rows
    column = lax.broadcasted_iota(jnp.int32, (size, size), 1)
    return jnp.where(column == to, 1.0, 0.0).astype(BF16)


def sixth(n):
    return (n * 10923) >> 16


def main_order(tm):
    at = lax.broadcasted_iota(jnp.int32, (12 * tm, 1), 0)
    which = jnp.where(at >= 6 * tm, 1, 0)
    n = at - which * 6 * tm
    a = sixth(n)
    source = a * 16 + which * 6 + n - a * 6
    column = lax.broadcasted_iota(jnp.int32, (12 * tm, 16 * tm), 1)
    return jnp.where(column == source, 1.0, 0.0).astype(BF16)


def rest_order(tm, to, src):
    third = 2 * tm
    at = lax.broadcasted_iota(jnp.int32, (2 * third, 1), 0)
    which = jnp.where(at >= third, 1, 0)
    n = at - which * third + to * third
    a = sixth(n)
    g = which * 6 + n - a * 6
    source = jnp.where((g >> 2) == src, a * 16 + 12 + (g & 3), -1)
    column = lax.broadcasted_iota(jnp.int32, (2 * third, 16 * tm), 1)
    return jnp.where(column == source, 1.0, 0.0).astype(BF16)


def first_kernel(me_ref, fc_hbm, out_hbm, qkv_hbm, res_hbm, cot_hbm, o_ref, *refs):
    pieces, (fc_ref, out_ref, qkv_ref, sem) = refs[:-4], refs[-4:]
    width = res_hbm.shape[-1]
    n = len(pieces)
    copies = [
        pltpu.make_async_copy(fc_hbm, fc_ref, sem.at[0]),
        pltpu.make_async_copy(out_hbm, out_ref, sem.at[1]),
        pltpu.make_async_copy(qkv_hbm, qkv_ref, sem.at[2]),
    ]
    for k, ref in enumerate(pieces):
        to = lax.rem(me_ref[0] + k, n)
        for j, src in enumerate((res_hbm, cot_hbm)):
            copies.append(
                pltpu.make_async_copy(
                    src.at[0, to], ref.at[:, pl.ds(j * width, width)], sem.at[3 + 2 * k + j]
                )
            )
    for c in copies:
        c.start()
    for c in copies[:3]:
        c.wait()
    both = jnp.concatenate([fc_ref[...].astype(F32), out_ref[...].astype(F32)], axis=0)
    tail = both[:, 768:]
    tail = jnp.concatenate([tail[0:4], tail[4:8], tail[8:12]], axis=1)
    qkv = qkv_ref[...].astype(F32)
    block = jnp.concatenate(
        [both[:, :768], tail, qkv[:, :768], qkv[:, 768:1536], qkv[:, 1536:]], axis=0
    )
    o_ref[...] = jnp.broadcast_to(block[None], o_ref.shape).astype(BF16)
    for c in copies[3:]:
        c.wait()


def weights_unpack_kernel(x_ref, o_ref):
    tm = x_ref.shape[0]
    x = x_ref[...].astype(F32)
    fo = x[:, 0:16].reshape(16 * tm, 768).astype(BF16)
    n = 8 * tm
    for j in range(3):
        o_ref[pl.ds(j * n, n), :] = x[:, 16 + 8 * j : 24 + 8 * j].reshape(n, 768).astype(BF16)
    o_ref[pl.ds(3 * n, 12 * tm), :] = nn(main_order(tm), fo).astype(BF16)
    for j in range(3):
        part = nn(rest_order(tm, j, 0), fo[:, :256])
        part += nn(rest_order(tm, j, 1), fo[:, 256:512])
        part += nn(rest_order(tm, j, 2), fo[:, 512:])
        o_ref[pl.ds(3 * n + 12 * tm, 4 * tm), pl.ds(j * 256, 256)] = part.astype(BF16)


def pack_kernel(q_ref, k_ref, v_ref, turn_ref, o_ref):
    steps, tubes, inner = q_ref.shape[1:]
    rows = steps * tubes
    parts = [
        nn(turn_ref[...], ref[0].reshape(rows, inner)).reshape(tubes, steps, inner)
        for ref in (q_ref, k_ref, v_ref)
    ]
    o_ref[...] = jnp.concatenate(parts, axis=1).astype(BF16)


def assemble_kernel(me_ref, *refs):
    pieces, o_ref = refs[:-1], refs[-1]
    n = len(pieces)
    for k, ref in enumerate(pieces):
        o_ref[0, lax.rem(me_ref[0] + n - k, n)] = ref[...]


def unpack_kernel(x_ref, turn_ref, *outs):
    x = x_ref[...].astype(F32)
    tubes, steps = x.shape[0], x.shape[1] // 3
    for j, o_ref in enumerate(outs):
        part = x[:, j * steps : (j + 1) * steps].reshape(tubes * steps, -1).astype(BF16)
        o_ref[0] = nn(turn_ref[...], part).astype(BF16).reshape(steps, tubes, -1)


def lane_masks(rows):
    lane = lax.broadcasted_iota(jnp.int32, (rows, 2 * HD), 1)
    return lane < HD


def stacked(block, first):
    zero = jnp.zeros_like(block)
    return jnp.concatenate([jnp.where(first, block, zero), jnp.where(first, zero, block)], axis=0)


def softmax(scores):
    exponent = jnp.exp(scores - jnp.max(scores, axis=-1, keepdims=True))
    return exponent / jnp.sum(exponent, axis=-1, keepdims=True)


def pair_probs(q, k2, bias0=None, bias1=None):
    n = q.shape[0]
    scores = nt(q, k2) * SCALE
    s0, s1 = scores[:, :n], scores[:, n:]
    if bias0 is not None:
        s0, s1 = s0 + bias0, s1 + bias1
    return softmax(s0), softmax(s1)


def pair_backward(p0, p1, q, k, v, g, first):
    n = q.shape[0]
    k2, v2, q2, g2 = (stacked(x, first) for x in (k, v, q, g))
    gp = nt(g, v2)
    g0, g1 = gp[:, :n], gp[:, n:]
    d0 = (p0 * (g0 - jnp.sum(p0 * g0, axis=-1, keepdims=True))).astype(BF16)
    d1 = (p1 * (g1 - jnp.sum(p1 * g1, axis=-1, keepdims=True))).astype(BF16)
    grad_q = nn(jnp.concatenate([d0, d1], axis=1), k2)
    grad_k = tn(jnp.concatenate([d0, d1], axis=0), q2)
    grad_v = tn(jnp.concatenate([p0.astype(BF16), p1.astype(BF16)], axis=0), g2)
    return grad_q * SCALE, grad_k * SCALE, grad_v


def qkv_of(x, steps):
    return [
        x[:, j * steps : (j + 1) * steps].reshape(x.shape[0] * steps, -1).astype(BF16)
        for j in range(3)
    ]


def forward_kernel(x_ref, o_ref, turned):
    x = x_ref[...].astype(F32)
    q, k, v = qkv_of(x, x.shape[1] // 3)
    n = q.shape[0]
    first = lane_masks(n)
    for h in range(HEADS // 2):
        at = slice(h * 128, (h + 1) * 128)
        p0, p1 = pair_probs(q[:, at], stacked(k[:, at], first))
        both = jnp.concatenate([p0.astype(BF16), p1.astype(BF16)], axis=1)
        turned[:, h, :] = nn(both, stacked(v[:, at], first))
    o_ref[...] = turned[...].astype(BF16)


def backward_kernel(x_ref, g_ref, o_ref, turned):
    x = x_ref[...].astype(F32)
    steps = x.shape[1] // 3
    q, k, v = qkv_of(x, steps)
    n = q.shape[0]
    turned[...] = g_ref[...].astype(F32)
    first = lane_masks(n)
    for h in range(HEADS // 2):
        at = slice(h * 128, (h + 1) * 128)
        p0, p1 = pair_probs(q[:, at], stacked(k[:, at], first))
        grads = pair_backward(
            p0,
            p1,
            q[:, at],
            k[:, at],
            v[:, at],
            turned[:, h, :].astype(BF16),
            first,
        )
        joined = jnp.concatenate([d.reshape(n // steps, steps, 128) for d in grads], axis=1)
        o_ref[:, :, at] = joined.astype(BF16)


def middle_kernel(
    me_ref, w_hbm, x_ref, gain_ref, slope_ref, row_ref, col_ref, turn_ref, *refs,
):
    pieces, refs = refs[: w_hbm.shape[0]], refs[w_hbm.shape[0] :]
    grs, refs = refs[: w_hbm.shape[0]], refs[w_hbm.shape[0] :]
    (gt_ref, gr_v, rest_v, inner_ref, width_v, qkv_v, fc_v, out_v, turned, proj, joined, sem) = refs
    sp = w_hbm.shape[0]
    tm = w_hbm.shape[1] // 40
    n, third = 8 * tm, 2 * tm
    copies = []

    def load(src, dst):
        copies.append(pltpu.make_async_copy(src, dst, sem.at[len(copies)]))
        copies[-1].start()

    for k, p in enumerate(pieces):
        load(p, rest_v.at[lax.rem(me_ref[0] + sp - k, sp)])
    at = 3 * n
    for dst, base, tail in (
        (fc_v, at, at + 12 * tm),
        (out_v, at + 6 * tm, at + 12 * tm + third),
    ):
        load(w_hbm.at[:, pl.ds(base, 6 * tm), :], dst.at[:, :, pl.ds(0, 768)])
        for j in range(3):
            load(
                w_hbm.at[:, pl.ds(tail, third), pl.ds(j * 256, 256)],
                dst.at[:, pl.ds(j * third, third), pl.ds(768, 256)],
            )
    for j in range(3):
        load(w_hbm.at[:, pl.ds(j * n, n), :], qkv_v.at[:, :, pl.ds(j * 768, 768)])

    tokens = x_ref.shape[0]
    width = gain_ref.shape[1]
    inner = 768
    rows, cols = row_ref[...], col_ref[...]
    distance = jnp.abs((rows >> 5) - (cols >> 5)) + jnp.abs((rows & 31) - (cols & 31))
    distance = distance.astype(F32)
    gain = gain_ref[...]
    turn = turn_ref[...]
    turned[...] = x_ref[...].astype(F32)
    mixed = jnp.concatenate([turned[:, h, :] for h in range(6)], axis=1).astype(BF16)
    mixed = nn(turn, mixed).astype(BF16)

    inner_ref[...] = gathered_order(tm, sp, 6)
    width_v[...] = gathered_order(tm, sp, 8)
    mixed = nn(mixed, inner_ref[...]).astype(BF16)
    for c in copies[: sp + 4]:
        c.wait()
    rest = rest_v[...].reshape(tokens, 2 * width)
    cot = rest[:, width:]
    fc = fc_v[...].reshape(inner, width)
    hidden = rest[:, :width].astype(F32) + nn(mixed, fc)
    centred = hidden - jnp.mean(hidden, axis=-1, keepdims=True)
    inv_std = lax.rsqrt(jnp.mean(centred * centred, axis=-1, keepdims=True) + EPSILON)
    normed = centred * inv_std
    normed_in = (normed * gain).astype(BF16)

    for c in copies[sp + 4 : sp + 8]:
        c.wait()
    normed_in = nn(normed_in, width_v[...]).astype(BF16)
    grad_mixed = nt(cot, out_v[...].reshape(inner, width)).astype(BF16)
    grad_mixed = nt(grad_mixed, inner_ref[...]).astype(BF16)

    for c in copies[sp + 8 :]:
        c.wait()
    qkv = qkv_v[...].reshape(width, 3 * inner)
    proj[...] = nn(normed_in, qkv).astype(BF16)

    first = lane_masks(tokens)
    for h in range(HEADS // 2):
        q, k, v = (proj[:, j * inner + h * 128 : j * inner + (h + 1) * 128] for j in range(3))
        g = grad_mixed[:, h * 128 : (h + 1) * 128]
        p0, p1 = pair_probs(
            q, stacked(k, first), -slope_ref[2 * h] * distance, -slope_ref[2 * h + 1] * distance
        )
        for j, d in enumerate(pair_backward(p0, p1, q, k, v, g, first)):
            joined[:, j * inner + h * 128 : j * inner + (h + 1) * 128] = d.astype(BF16)

    grad_normed = nt(joined[...], qkv).astype(BF16)
    grad_normed = nt(grad_normed, width_v[...])
    scaled = grad_normed * gain
    first_mean = jnp.mean(scaled, axis=-1, keepdims=True)
    second_mean = jnp.mean(scaled * normed, axis=-1, keepdims=True)
    term = inv_std * (scaled - first_mean - normed * second_mean)
    grad_resid = (cot.astype(F32) + term).astype(BF16)
    gr_v[...] = grad_resid.reshape(gr_v.shape)
    for k, ref in enumerate(grs):
        ref[...] = gr_v[lax.rem(me_ref[0] + k, sp)]
    grad_time = nt(grad_resid, fc).astype(BF16)
    grad_time = nt(grad_time, inner_ref[...]).astype(BF16)
    grad_time = tn(turn, grad_time)
    for h in range(6):
        turned[:, h, :] = grad_time[:, h * 128 : (h + 1) * 128]
    gt_ref[...] = turned[...].astype(BF16)


def body(
    time_query,
    time_key,
    time_value,
    residual_in,
    fc_weight,
    norm_gain,
    qkv_weight,
    out_weight,
    bias_slope,
    visible,
    cotangent,
):
    tm, sp = lax.axis_size("tm"), lax.axis_size("space")
    steps, tubes, inner = time_query.shape[1:]
    width = residual_in.shape[-1]
    total = tm * steps
    both = ("tm", "space")
    shape = jax.ShapeDtypeStruct

    def turned_round(parts):
        return [
            lax.ppermute(p, "space", [(i, (i + k) % sp) for i in range(sp)]) if k else p
            for k, p in enumerate(parts)
        ]

    def exchange(x, axes):
        return lax.all_to_all(x, axes, split_axis=0, concat_axis=0, tiled=True)

    to_tubes = jnp.asarray(transposed_rows(steps, tubes))
    to_steps = jnp.asarray(transposed_rows(tubes, steps))
    to_order = jnp.asarray(transposed_rows(tm, sp))
    me = lax.axis_index("space").astype(jnp.int32).reshape(1)
    shards, *pieces = pl.pallas_call(
        first_kernel,
        out_shape=(shape((tm, 40, inner), BF16),) + (shape((tubes, 2 * width), BF16),) * sp,
        in_specs=[SMEM] + [HBM] * 5,
        out_specs=(VMEM,) * (sp + 1),
        scratch_shapes=[
            pltpu.VMEM(fc_weight.shape, BF16),
            pltpu.VMEM(out_weight.shape, BF16),
            pltpu.VMEM(qkv_weight.shape, BF16),
            pltpu.SemaphoreType.DMA((3 + 2 * sp,)),
        ],
        compiler_params=params(56),
        name="first",
    )(me, fc_weight, out_weight, qkv_weight, residual_in, cotangent)
    pieces = turned_round(pieces)
    shards = exchange(shards, "tm")

    send = pl.pallas_call(
        pack_kernel,
        out_shape=shape((tubes, 3 * steps, inner), BF16),
        in_specs=[VMEM] * 4,
        out_specs=VMEM,
        compiler_params=params(16),
        cost_estimate=pl.CostEstimate(flops=10**9, bytes_accessed=4 * 10**6, transcendentals=0),
        name="pack",
    )(time_query, time_key, time_value, to_tubes)

    shards = pl.pallas_call(
        weights_unpack_kernel,
        out_shape=shape((40 * tm, inner), BF16),
        in_specs=[VMEM],
        out_specs=VMEM,
        compiler_params=params(24),
        name="weights_unpack",
    )(shards)
    weights = lax.all_gather(shards, "space", axis=0)

    send, shards = lax.optimization_barrier((send, shards))
    got = exchange(send, "tm")

    mixed = pl.pallas_call(
        forward_kernel,
        out_shape=shape((total, 6, 128), BF16),
        in_specs=[VMEM],
        out_specs=VMEM,
        scratch_shapes=[pltpu.VMEM((total, 6, 128), F32)],
        compiler_params=params(24),
        cost_estimate=pl.CostEstimate(flops=10**8, bytes_accessed=2 * 10**6, transcendentals=2 * 10**5),
        name="temporal_forward",
    )(got)
    mixed = exchange(mixed, both)

    *grs, grad_time = pl.pallas_call(
        middle_kernel,
        out_shape=(shape((tubes, width), BF16),) * sp + (shape((total, 6, 128), BF16),),
        in_specs=[SMEM, HBM, VMEM, VMEM, SMEM, VMEM, VMEM, VMEM] + [HBM] * sp,
        out_specs=(VMEM,) * (sp + 1),
        scratch_shapes=[
            pltpu.VMEM((sp, tubes, width), BF16),
            pltpu.VMEM((sp, tubes, 2 * width), BF16),
            pltpu.VMEM((inner, inner), BF16),
            pltpu.VMEM((width, width), BF16),
            pltpu.VMEM((sp, 8 * tm, 3 * inner), BF16),
            pltpu.VMEM((sp, 6 * tm, width), BF16),
            pltpu.VMEM((sp, 6 * tm, width), BF16),
            pltpu.VMEM((total, 6, 128), F32),
            pltpu.VMEM((total, 3 * inner), BF16),
            pltpu.VMEM((total, 3 * inner), BF16),
            pltpu.SemaphoreType.DMA((11 + sp,)),
        ],
        compiler_params=params(56),
        cost_estimate=pl.CostEstimate(flops=4 * 10**9, bytes_accessed=10**7, transcendentals=2 * 10**5),
        name="middle",
    )(
        me,
        weights,
        mixed,
        norm_gain.reshape(1, width),
        bias_slope,
        visible.reshape(total, 1),
        visible.reshape(1, total),
        to_order,
        *pieces,
    )
    grs = turned_round(grs)
    grad_time = exchange(grad_time, both)

    back = pl.pallas_call(
        backward_kernel,
        out_shape=shape((tm, 3 * steps, inner), BF16),
        in_specs=[VMEM] * 2,
        out_specs=VMEM,
        scratch_shapes=[pltpu.VMEM((total, 6, 128), F32)],
        compiler_params=params(24),
        cost_estimate=pl.CostEstimate(flops=3 * 10**8, bytes_accessed=2 * 10**6, transcendentals=0),
        name="temporal_backward",
    )(got, grad_time)
    back, grs = lax.optimization_barrier((back, grs))
    back = exchange(back, "tm")
    outs = pl.pallas_call(
        unpack_kernel,
        out_shape=(shape(time_query.shape, BF16),) * 3,
        in_specs=[VMEM, VMEM],
        out_specs=(VMEM,) * 3,
        compiler_params=params(24),
        name="unpack",
    )(back, to_steps)
    grad_resid = pl.pallas_call(
        assemble_kernel,
        out_shape=shape(residual_in.shape, BF16),
        in_specs=[SMEM] + [VMEM] * sp,
        out_specs=VMEM,
        compiler_params=params(24),
        cost_estimate=pl.CostEstimate(flops=10**9, bytes_accessed=4 * 10**6, transcendentals=0),
        name="assemble",
    )(me, *grs)
    return (grad_resid, *outs)


def solution(mesh):
    token = P("dp", "tm", "space", None)
    row = P(("tm", "space"), None)
    in_specs = (token, token, token, token, row, P(), row, row, P(), P("dp", None), token)
    return jax.shard_map(
        body, mesh=mesh, in_specs=in_specs, out_specs=(token,) * 4, check_vma=False
    )
```

```python
import numpy as np
import jax
import jax.numpy as jnp
from jax import lax
from jax.experimental import pallas as pl
from jax.experimental.pallas import tpu as pltpu
from jax.sharding import PartitionSpec as P

HEADS = 12
HD = 64
GRID = 32
SCALE = HD ** (-0.5)
EPSILON = 1e-05
F32 = jnp.float32
BF16 = jnp.bfloat16
VMEM = pl.BlockSpec(memory_space=pltpu.VMEM)
SMEM = pl.BlockSpec(memory_space=pltpu.SMEM)
HBM = pl.BlockSpec(memory_space=pltpu.HBM)


def params(mib):
    return pltpu.CompilerParams(vmem_limit_bytes=mib * 2**20)


def nn(a, b):
    return jnp.dot(a, b, preferred_element_type=F32)


def nt(a, b):
    return lax.dot_general(a, b, (((1,), (1,)), ((), ())), preferred_element_type=F32)


def tn(a, b):
    return lax.dot_general(a, b, (((0,), (0,)), ((), ())), preferred_element_type=F32)


def transposed_rows(outer, inner):
    m = np.zeros((outer * inner, outer * inner), np.float32)
    i, j = np.meshgrid(np.arange(outer), np.arange(inner), indexing="ij")
    m[(j * outer + i).ravel(), (i * inner + j).ravel()] = 1
    return m.astype(BF16)


def gathered_order(tm, sp, rows):
    size = tm * sp * rows
    at = lax.broadcasted_iota(jnp.int32, (size, 1), 0)
    block = (at * (65536 // rows + 1)) >> 16
    a = (block * (65536 // sp + 1)) >> 16
    to = ((block - a * sp) * tm + a) * rows + at - block * rows
    column = lax.broadcasted_iota(jnp.int32, (size, size), 1)
    return jnp.where(column == to, 1.0, 0.0).astype(BF16)


def sixth(n):
    return (n * 10923) >> 16


def main_order(tm):
    at = lax.broadcasted_iota(jnp.int32, (12 * tm, 1), 0)
    which = jnp.where(at >= 6 * tm, 1, 0)
    n = at - which * 6 * tm
    a = sixth(n)
    source = a * 16 + which * 6 + n - a * 6
    column = lax.broadcasted_iota(jnp.int32, (12 * tm, 16 * tm), 1)
    return jnp.where(column == source, 1.0, 0.0).astype(BF16)


def rest_order(tm, to, src):
    third = 2 * tm
    at = lax.broadcasted_iota(jnp.int32, (2 * third, 1), 0)
    which = jnp.where(at >= third, 1, 0)
    n = at - which * third + to * third
    a = sixth(n)
    g = which * 6 + n - a * 6
    source = jnp.where((g >> 2) == src, a * 16 + 12 + (g & 3), -1)
    column = lax.broadcasted_iota(jnp.int32, (2 * third, 16 * tm), 1)
    return jnp.where(column == source, 1.0, 0.0).astype(BF16)


def first_kernel(fc_hbm, out_hbm, qkv_hbm, res_hbm, cot_hbm, o_ref, rest_ref, fc_ref, out_ref, qkv_ref, sem):
    width = res_hbm.shape[-1]
    copies = [
        pltpu.make_async_copy(res_hbm.at[0], rest_ref.at[:, :, pl.ds(0, width)], sem.at[0]),
        pltpu.make_async_copy(cot_hbm.at[0], rest_ref.at[:, :, pl.ds(width, width)], sem.at[1]),
        pltpu.make_async_copy(fc_hbm, fc_ref, sem.at[2]),
        pltpu.make_async_copy(out_hbm, out_ref, sem.at[3]),
        pltpu.make_async_copy(qkv_hbm, qkv_ref, sem.at[4]),
    ]
    for c in copies:
        c.start()
    for c in copies[2:]:
        c.wait()
    both = jnp.concatenate([fc_ref[...].astype(F32), out_ref[...].astype(F32)], axis=0)
    tail = both[:, 768:]
    tail = jnp.concatenate([tail[0:4], tail[4:8], tail[8:12]], axis=1)
    qkv = qkv_ref[...].astype(F32)
    block = jnp.concatenate(
        [both[:, :768], tail, qkv[:, :768], qkv[:, 768:1536], qkv[:, 1536:]], axis=0
    )
    o_ref[...] = jnp.broadcast_to(block[None], o_ref.shape).astype(BF16)
    for c in copies[:2]:
        c.wait()


def weights_unpack_kernel(x_ref, o_ref):
    tm = x_ref.shape[0]
    x = x_ref[...].astype(F32)
    fo = x[:, 0:16].reshape(16 * tm, 768).astype(BF16)
    n = 8 * tm
    for j in range(3):
        o_ref[pl.ds(j * n, n), :] = x[:, 16 + 8 * j : 24 + 8 * j].reshape(n, 768).astype(BF16)
    o_ref[pl.ds(3 * n, 12 * tm), :] = nn(main_order(tm), fo).astype(BF16)
    for j in range(3):
        part = nn(rest_order(tm, j, 0), fo[:, :256])
        part += nn(rest_order(tm, j, 1), fo[:, 256:512])
        part += nn(rest_order(tm, j, 2), fo[:, 512:])
        o_ref[pl.ds(3 * n + 12 * tm, 4 * tm), pl.ds(j * 256, 256)] = part.astype(BF16)


def pack_kernel(q_ref, k_ref, v_ref, turn_ref, o_ref):
    steps, tubes, inner = q_ref.shape[1:]
    rows = steps * tubes
    parts = [
        nn(turn_ref[...], ref[0].reshape(rows, inner)).reshape(tubes, steps, inner)
        for ref in (q_ref, k_ref, v_ref)
    ]
    o_ref[...] = jnp.concatenate(parts, axis=1).astype(BF16)


def slice_kernel(me_ref, gr_hbm, o_ref, sem):
    mine = o_ref.shape[2]
    at = pl.multiple_of(me_ref[0] * mine, mine)
    copy = pltpu.make_async_copy(gr_hbm.at[:, pl.ds(at, mine), :], o_ref.at[0], sem)
    copy.start()
    copy.wait()


def unpack_kernel(x_ref, turn_ref, *outs):
    x = x_ref[...].astype(F32)
    tubes, steps = x.shape[0], x.shape[1] // 3
    for j, o_ref in enumerate(outs):
        part = x[:, j * steps : (j + 1) * steps].reshape(tubes * steps, -1).astype(BF16)
        o_ref[0] = nn(turn_ref[...], part).astype(BF16).reshape(steps, tubes, -1)


def lane_masks(rows):
    lane = lax.broadcasted_iota(jnp.int32, (rows, 2 * HD), 1)
    return lane < HD


def stacked(block, first):
    zero = jnp.zeros_like(block)
    return jnp.concatenate([jnp.where(first, block, zero), jnp.where(first, zero, block)], axis=0)


def softmax(scores):
    exponent = jnp.exp(scores - jnp.max(scores, axis=-1, keepdims=True))
    return exponent * (1.0 / jnp.sum(exponent, axis=-1, keepdims=True))


def pair_probs(q, k2, bias0=None, bias1=None):
    n = q.shape[0]
    scores = nt(q, k2) * SCALE
    s0, s1 = scores[:, :n], scores[:, n:]
    if bias0 is not None:
        s0, s1 = s0 + bias0, s1 + bias1
    return softmax(s0), softmax(s1)


def pair_backward(p0, p1, q, k, v, g, first):
    n = q.shape[0]
    k2, v2, q2, g2 = (stacked(x, first) for x in (k, v, q, g))
    gp = nt(g, v2)
    g0, g1 = gp[:, :n], gp[:, n:]
    d0 = (p0 * (g0 - jnp.sum(p0 * g0, axis=-1, keepdims=True))).astype(BF16)
    d1 = (p1 * (g1 - jnp.sum(p1 * g1, axis=-1, keepdims=True))).astype(BF16)
    grad_q = nn(jnp.concatenate([d0, d1], axis=1), k2)
    grad_k = tn(jnp.concatenate([d0, d1], axis=0), q2)
    grad_v = tn(jnp.concatenate([p0.astype(BF16), p1.astype(BF16)], axis=0), g2)
    return grad_q * SCALE, grad_k * SCALE, grad_v


def qkv_of(x, steps):
    return [
        x[:, j * steps : (j + 1) * steps].reshape(x.shape[0] * steps, -1).astype(BF16)
        for j in range(3)
    ]


def forward_kernel(x_ref, o_ref, turned):
    x = x_ref[...].astype(F32)
    q, k, v = qkv_of(x, x.shape[1] // 3)
    n = q.shape[0]
    first = lane_masks(n)
    for h in range(HEADS // 2):
        at = slice(h * 128, (h + 1) * 128)
        p0, p1 = pair_probs(q[:, at], stacked(k[:, at], first))
        both = jnp.concatenate([p0.astype(BF16), p1.astype(BF16)], axis=1)
        turned[:, h, :] = nn(both, stacked(v[:, at], first))
    o_ref[...] = turned[...].astype(BF16)


def probs_kernel(x_ref, p_ref):
    x = x_ref[...].astype(F32)
    q, k, _ = qkv_of(x, x.shape[1] // 3)
    n = q.shape[0]
    first = lane_masks(n)
    for h in range(HEADS // 2):
        at = slice(h * 128, (h + 1) * 128)
        p0, p1 = pair_probs(q[:, at], stacked(k[:, at], first))
        p_ref[h, :, 0:n] = p0
        p_ref[h, :, n : 2 * n] = p1


def backward_kernel(x_ref, p_ref, g_ref, o_ref, turned):
    x = x_ref[...].astype(F32)
    steps = x.shape[1] // 3
    q, k, v = qkv_of(x, steps)
    n = q.shape[0]
    turned[...] = g_ref[...].astype(F32)
    first = lane_masks(n)
    for h in range(HEADS // 2):
        at = slice(h * 128, (h + 1) * 128)
        grads = pair_backward(
            p_ref[h, :, 0:n],
            p_ref[h, :, n : 2 * n],
            q[:, at],
            k[:, at],
            v[:, at],
            turned[:, h, :].astype(BF16),
            first,
        )
        joined = jnp.concatenate([d.reshape(n // steps, steps, 128) for d in grads], axis=1)
        o_ref[:, :, at] = joined.astype(BF16)


def middle_kernel(
    me_ref, w_hbm, x_ref, rest_hbm, gain_ref, slope_ref, row_ref, col_ref, turn_ref,
    gr_ref, gt_ref, rest_v, inner_ref, width_v, qkv_v, fc_v, out_v, turned, proj, joined, sem,
):
    sp = w_hbm.shape[0]
    tm = w_hbm.shape[1] // 40
    n, third = 8 * tm, 2 * tm
    copies = []

    def load(src, dst):
        copies.append(pltpu.make_async_copy(src, dst, sem.at[len(copies)]))
        copies[-1].start()

    load(rest_hbm.at[:, me_ref[0]], rest_v)
    at = 3 * n
    for dst, base, tail in (
        (fc_v, at, at + 12 * tm),
        (out_v, at + 6 * tm, at + 12 * tm + third),
    ):
        load(w_hbm.at[:, pl.ds(base, 6 * tm), :], dst.at[:, :, pl.ds(0, 768)])
        for j in range(3):
            load(
                w_hbm.at[:, pl.ds(tail, third), pl.ds(j * 256, 256)],
                dst.at[:, pl.ds(j * third, third), pl.ds(768, 256)],
            )
    for j in range(3):
        load(w_hbm.at[:, pl.ds(j * n, n), :], qkv_v.at[:, :, pl.ds(j * 768, 768)])

    tokens = x_ref.shape[0]
    width = gain_ref.shape[1]
    inner = 768
    rows, cols = row_ref[...], col_ref[...]
    distance = jnp.abs((rows >> 5) - (cols >> 5)) + jnp.abs((rows & 31) - (cols & 31))
    distance = distance.astype(F32)
    gain = gain_ref[...]
    turn = turn_ref[...]
    turned[...] = x_ref[...].astype(F32)
    mixed = jnp.concatenate([turned[:, h, :] for h in range(6)], axis=1).astype(BF16)
    mixed = nn(turn, mixed).astype(BF16)

    inner_ref[...] = gathered_order(tm, sp, 6)
    width_v[...] = gathered_order(tm, sp, 8)
    mixed = nn(mixed, inner_ref[...]).astype(BF16)
    for c in copies[:5]:
        c.wait()
    rest = rest_v[...].reshape(tokens, 2 * width)
    cot = rest[:, width:]
    fc = fc_v[...].reshape(inner, width)
    hidden = rest[:, :width].astype(F32) + nn(mixed, fc)
    centred = hidden - jnp.mean(hidden, axis=-1, keepdims=True)
    inv_std = lax.rsqrt(jnp.mean(centred * centred, axis=-1, keepdims=True) + EPSILON)
    normed = centred * inv_std
    normed_in = (normed * gain).astype(BF16)

    for c in copies[5:9]:
        c.wait()
    normed_in = nn(normed_in, width_v[...]).astype(BF16)
    grad_mixed = nt(cot, out_v[...].reshape(inner, width)).astype(BF16)
    grad_mixed = nt(grad_mixed, inner_ref[...]).astype(BF16)

    for c in copies[9:]:
        c.wait()
    qkv = qkv_v[...].reshape(width, 3 * inner)
    proj[...] = nn(normed_in, qkv).astype(BF16)

    first = lane_masks(tokens)
    for h in range(HEADS // 2):
        q, k, v = (proj[:, j * inner + h * 128 : j * inner + (h + 1) * 128] for j in range(3))
        g = grad_mixed[:, h * 128 : (h + 1) * 128]
        p0, p1 = pair_probs(
            q, stacked(k, first), -slope_ref[2 * h] * distance, -slope_ref[2 * h + 1] * distance
        )
        for j, d in enumerate(pair_backward(p0, p1, q, k, v, g, first)):
            joined[:, j * inner + h * 128 : j * inner + (h + 1) * 128] = d.astype(BF16)

    grad_normed = nt(joined[...], qkv).astype(BF16)
    grad_normed = nt(grad_normed, width_v[...])
    scaled = grad_normed * gain
    first_mean = jnp.mean(scaled, axis=-1, keepdims=True)
    second_mean = jnp.mean(scaled * normed, axis=-1, keepdims=True)
    term = inv_std * (scaled - first_mean - normed * second_mean)
    grad_resid = (cot.astype(F32) + term).astype(BF16)
    gr_ref[...] = grad_resid
    grad_time = nt(grad_resid, fc).astype(BF16)
    grad_time = nt(grad_time, inner_ref[...]).astype(BF16)
    grad_time = tn(turn, grad_time)
    for h in range(6):
        turned[:, h, :] = grad_time[:, h * 128 : (h + 1) * 128]
    gt_ref[...] = turned[...].astype(BF16)


def body(
    time_query,
    time_key,
    time_value,
    residual_in,
    fc_weight,
    norm_gain,
    qkv_weight,
    out_weight,
    bias_slope,
    visible,
    cotangent,
):
    tm, sp = lax.axis_size("tm"), lax.axis_size("space")
    steps, tubes, inner = time_query.shape[1:]
    width = residual_in.shape[-1]
    total = tm * steps
    both = ("tm", "space")
    shape = jax.ShapeDtypeStruct

    def exchange(x, axes):
        return lax.all_to_all(x, axes, split_axis=0, concat_axis=0, tiled=True)

    to_tubes = jnp.asarray(transposed_rows(steps, tubes))
    to_steps = jnp.asarray(transposed_rows(tubes, steps))
    to_order = jnp.asarray(transposed_rows(tm, sp))
    me = lax.axis_index("space").astype(jnp.int32).reshape(1)
    shards, rest = pl.pallas_call(
        first_kernel,
        out_shape=(shape((tm, 40, inner), BF16), shape((steps, tubes, 2 * width), BF16)),
        in_specs=[HBM] * 5,
        out_specs=(VMEM, VMEM),
        scratch_shapes=[
            pltpu.VMEM(fc_weight.shape, BF16),
            pltpu.VMEM(out_weight.shape, BF16),
            pltpu.VMEM(qkv_weight.shape, BF16),
            pltpu.SemaphoreType.DMA((5,)),
        ],
        compiler_params=params(56),
        name="first",
    )(fc_weight, out_weight, qkv_weight, residual_in, cotangent)
    rest = lax.all_gather(rest, "space", axis=0)
    shards = exchange(shards, "tm")

    send = pl.pallas_call(
        pack_kernel,
        out_shape=shape((tubes, 3 * steps, inner), BF16),
        in_specs=[VMEM] * 4,
        out_specs=VMEM,
        compiler_params=params(16),
        cost_estimate=pl.CostEstimate(flops=10**9, bytes_accessed=4 * 10**6, transcendentals=0),
        name="pack",
    )(time_query, time_key, time_value, to_tubes)

    shards = pl.pallas_call(
        weights_unpack_kernel,
        out_shape=shape((40 * tm, inner), BF16),
        in_specs=[VMEM],
        out_specs=VMEM,
        compiler_params=params(24),
        name="weights_unpack",
    )(shards)
    weights = lax.all_gather(shards, "space", axis=0)

    send, shards = lax.optimization_barrier((send, shards))
    got = exchange(send, "tm")

    mixed = pl.pallas_call(
        forward_kernel,
        out_shape=shape((total, 6, 128), BF16),
        in_specs=[VMEM],
        out_specs=VMEM,
        scratch_shapes=[pltpu.VMEM((total, 6, 128), F32)],
        compiler_params=params(24),
        cost_estimate=pl.CostEstimate(flops=10**8, bytes_accessed=2 * 10**6, transcendentals=2 * 10**5),
        name="temporal_forward",
    )(got)
    mixed = exchange(mixed, both)

    grad_resid, grad_time = pl.pallas_call(
        middle_kernel,
        out_shape=(shape((total, width), BF16), shape((total, 6, 128), BF16)),
        in_specs=[SMEM, HBM, VMEM, HBM, VMEM, SMEM, VMEM, VMEM, VMEM],
        out_specs=(VMEM, VMEM),
        scratch_shapes=[
            pltpu.VMEM((sp, tubes, 2 * width), BF16),
            pltpu.VMEM((inner, inner), BF16),
            pltpu.VMEM((width, width), BF16),
            pltpu.VMEM((sp, 8 * tm, 3 * inner), BF16),
            pltpu.VMEM((sp, 6 * tm, width), BF16),
            pltpu.VMEM((sp, 6 * tm, width), BF16),
            pltpu.VMEM((total, 6, 128), F32),
            pltpu.VMEM((total, 3 * inner), BF16),
            pltpu.VMEM((total, 3 * inner), BF16),
            pltpu.SemaphoreType.DMA((12,)),
        ],
        compiler_params=params(56),
        cost_estimate=pl.CostEstimate(flops=4 * 10**9, bytes_accessed=10**7, transcendentals=2 * 10**5),
        name="middle",
    )(
        me,
        weights,
        mixed,
        rest,
        norm_gain.reshape(1, width),
        bias_slope,
        visible.reshape(total, 1),
        visible.reshape(1, total),
        to_order,
    )
    grad_resid = lax.all_gather(grad_resid, "space", axis=0)
    got, grad_time = lax.optimization_barrier((got, grad_time))
    grad_time = exchange(grad_time, both)
    probs = pl.pallas_call(
        probs_kernel,
        out_shape=shape((HEADS // 2, total, 2 * total), F32),
        in_specs=[VMEM],
        out_specs=VMEM,
        compiler_params=params(24),
        cost_estimate=pl.CostEstimate(flops=10**9, bytes_accessed=4 * 10**6, transcendentals=2 * 10**5),
        name="temporal_probs",
    )(got)

    back = pl.pallas_call(
        backward_kernel,
        out_shape=shape((tm, 3 * steps, inner), BF16),
        in_specs=[VMEM] * 3,
        out_specs=VMEM,
        scratch_shapes=[pltpu.VMEM((total, 6, 128), F32)],
        compiler_params=params(24),
        cost_estimate=pl.CostEstimate(flops=3 * 10**8, bytes_accessed=2 * 10**6, transcendentals=0),
        name="temporal_backward",
    )(got, probs, grad_time)
    back, grad_resid = lax.optimization_barrier((back, grad_resid))
    back = exchange(back, "tm")
    outs = pl.pallas_call(
        unpack_kernel,
        out_shape=(shape(time_query.shape, BF16),) * 3,
        in_specs=[VMEM, VMEM],
        out_specs=(VMEM,) * 3,
        compiler_params=params(24),
        name="unpack",
    )(back, to_steps)
    grad_resid = pl.pallas_call(
        slice_kernel,
        out_shape=shape(residual_in.shape, BF16),
        in_specs=[SMEM, HBM],
        out_specs=VMEM,
        scratch_shapes=[pltpu.SemaphoreType.DMA],
        compiler_params=params(56),
        cost_estimate=pl.CostEstimate(flops=10**9, bytes_accessed=4 * 10**6, transcendentals=0),
        name="slice",
    )(me, grad_resid)
    return (grad_resid, *outs)


def solution(mesh):
    token = P("dp", "tm", "space", None)
    row = P(("tm", "space"), None)
    in_specs = (token, token, token, token, row, P(), row, row, P(), P("dp", None), token)
    return jax.shard_map(
        body, mesh=mesh, in_specs=in_specs, out_specs=(token,) * 4, check_vma=False
    )
```

```python
import numpy as np
import jax
import jax.numpy as jnp
from jax import lax
from jax.experimental import pallas as pl
from jax.experimental.pallas import tpu as pltpu
from jax.sharding import PartitionSpec as P

HEADS = 12
HD = 64
GRID = 32
SCALE = HD ** (-0.5)
EPSILON = 1e-05
F32 = jnp.float32
BF16 = jnp.bfloat16
VMEM = pl.BlockSpec(memory_space=pltpu.VMEM)
SMEM = pl.BlockSpec(memory_space=pltpu.SMEM)
HBM = pl.BlockSpec(memory_space=pltpu.HBM)


def params(mib):
    return pltpu.CompilerParams(vmem_limit_bytes=mib * 2**20)


def nn(a, b):
    return jnp.dot(a, b, preferred_element_type=F32)


def nt(a, b):
    return lax.dot_general(a, b, (((1,), (1,)), ((), ())), preferred_element_type=F32)


def tn(a, b):
    return lax.dot_general(a, b, (((0,), (0,)), ((), ())), preferred_element_type=F32)


def transposed_rows(outer, inner):
    m = np.zeros((outer * inner, outer * inner), np.float32)
    i, j = np.meshgrid(np.arange(outer), np.arange(inner), indexing="ij")
    m[(j * outer + i).ravel(), (i * inner + j).ravel()] = 1
    return m.astype(BF16)


def gathered_order(tm, sp, rows):
    size = tm * sp * rows
    at = lax.broadcasted_iota(jnp.int32, (size, 1), 0)
    block = (at * (65536 // rows + 1)) >> 16
    a = (block * (65536 // sp + 1)) >> 16
    to = ((block - a * sp) * tm + a) * rows + at - block * rows
    column = lax.broadcasted_iota(jnp.int32, (size, size), 1)
    return jnp.where(column == to, 1.0, 0.0).astype(BF16)


def sixth(n):
    return (n * 10923) >> 16


def main_order(tm):
    at = lax.broadcasted_iota(jnp.int32, (12 * tm, 1), 0)
    which = jnp.where(at >= 6 * tm, 1, 0)
    n = at - which * 6 * tm
    a = sixth(n)
    source = a * 16 + which * 6 + n - a * 6
    column = lax.broadcasted_iota(jnp.int32, (12 * tm, 16 * tm), 1)
    return jnp.where(column == source, 1.0, 0.0).astype(BF16)


def rest_order(tm, to, src):
    third = 2 * tm
    at = lax.broadcasted_iota(jnp.int32, (2 * third, 1), 0)
    which = jnp.where(at >= third, 1, 0)
    n = at - which * third + to * third
    a = sixth(n)
    g = which * 6 + n - a * 6
    source = jnp.where((g >> 2) == src, a * 16 + 12 + (g & 3), -1)
    column = lax.broadcasted_iota(jnp.int32, (2 * third, 16 * tm), 1)
    return jnp.where(column == source, 1.0, 0.0).astype(BF16)


def first_kernel(fc_hbm, out_hbm, qkv_hbm, res_hbm, cot_hbm, o_ref, rest_ref, fc_ref, out_ref, qkv_ref, sem):
    width = res_hbm.shape[-1]
    copies = [
        pltpu.make_async_copy(res_hbm.at[0], rest_ref.at[:, :, pl.ds(0, width)], sem.at[0]),
        pltpu.make_async_copy(cot_hbm.at[0], rest_ref.at[:, :, pl.ds(width, width)], sem.at[1]),
        pltpu.make_async_copy(fc_hbm, fc_ref, sem.at[2]),
        pltpu.make_async_copy(out_hbm, out_ref, sem.at[3]),
        pltpu.make_async_copy(qkv_hbm, qkv_ref, sem.at[4]),
    ]
    for c in copies:
        c.start()
    for c in copies[2:]:
        c.wait()
    both = jnp.concatenate([fc_ref[...].astype(F32), out_ref[...].astype(F32)], axis=0)
    tail = both[:, 768:]
    tail = jnp.concatenate([tail[0:4], tail[4:8], tail[8:12]], axis=1)
    qkv = qkv_ref[...].astype(F32)
    block = jnp.concatenate(
        [both[:, :768], tail, qkv[:, :768], qkv[:, 768:1536], qkv[:, 1536:]], axis=0
    )
    o_ref[...] = jnp.broadcast_to(block[None], o_ref.shape).astype(BF16)
    for c in copies[:2]:
        c.wait()


def weights_unpack_kernel(x_ref, o_ref):
    tm = x_ref.shape[0]
    x = x_ref[...].astype(F32)
    fo = x[:, 0:16].reshape(16 * tm, 768).astype(BF16)
    n = 8 * tm
    for j in range(3):
        o_ref[pl.ds(j * n, n), :] = x[:, 16 + 8 * j : 24 + 8 * j].reshape(n, 768).astype(BF16)
    o_ref[pl.ds(3 * n, 12 * tm), :] = nn(main_order(tm), fo).astype(BF16)
    for j in range(3):
        part = nn(rest_order(tm, j, 0), fo[:, :256])
        part += nn(rest_order(tm, j, 1), fo[:, 256:512])
        part += nn(rest_order(tm, j, 2), fo[:, 512:])
        o_ref[pl.ds(3 * n + 12 * tm, 4 * tm), pl.ds(j * 256, 256)] = part.astype(BF16)


def pack_kernel(q_ref, k_ref, v_ref, turn_ref, o_ref):
    steps, tubes, inner = q_ref.shape[1:]
    rows = steps * tubes
    parts = [
        nn(turn_ref[...], ref[0].reshape(rows, inner)).reshape(tubes, steps, inner)
        for ref in (q_ref, k_ref, v_ref)
    ]
    o_ref[...] = jnp.concatenate(parts, axis=1).astype(BF16)


def unpack_kernel(x_ref, turn_ref, gr_ref, gr_out, *outs):
    gr_out[0] = gr_ref[...]
    x = x_ref[...].astype(F32)
    tubes, steps = x.shape[0], x.shape[1] // 3
    for j, o_ref in enumerate(outs):
        part = x[:, j * steps : (j + 1) * steps].reshape(tubes * steps, -1).astype(BF16)
        o_ref[0] = nn(turn_ref[...], part).astype(BF16).reshape(steps, tubes, -1)


def lane_masks(rows):
    lane = lax.broadcasted_iota(jnp.int32, (rows, 2 * HD), 1)
    return lane < HD


def stacked(block, first):
    zero = jnp.zeros_like(block)
    return jnp.concatenate([jnp.where(first, block, zero), jnp.where(first, zero, block)], axis=0)


def softmax(scores):
    exponent = jnp.exp(scores - jnp.max(scores, axis=-1, keepdims=True))
    return exponent * (1.0 / jnp.sum(exponent, axis=-1, keepdims=True))


def pair_probs(q, k2, bias0=None, bias1=None):
    n = q.shape[0]
    scores = nt(q, k2) * SCALE
    s0, s1 = scores[:, :n], scores[:, n:]
    if bias0 is not None:
        s0, s1 = s0 + bias0, s1 + bias1
    return softmax(s0), softmax(s1)


def pair_backward(p0, p1, q, k, v, g, first):
    n = q.shape[0]
    k2, v2, q2, g2 = (stacked(x, first) for x in (k, v, q, g))
    gp = nt(g, v2)
    g0, g1 = gp[:, :n], gp[:, n:]
    d0 = (p0 * (g0 - jnp.sum(p0 * g0, axis=-1, keepdims=True))).astype(BF16)
    d1 = (p1 * (g1 - jnp.sum(p1 * g1, axis=-1, keepdims=True))).astype(BF16)
    grad_q = nn(jnp.concatenate([d0, d1], axis=1), k2)
    grad_k = tn(jnp.concatenate([d0, d1], axis=0), q2)
    grad_v = tn(jnp.concatenate([p0.astype(BF16), p1.astype(BF16)], axis=0), g2)
    return grad_q * SCALE, grad_k * SCALE, grad_v


def qkv_of(x, steps):
    return [
        x[:, j * steps : (j + 1) * steps].reshape(x.shape[0] * steps, -1).astype(BF16)
        for j in range(3)
    ]


def forward_kernel(x_ref, o_ref, turned):
    x = x_ref[...].astype(F32)
    q, k, v = qkv_of(x, x.shape[1] // 3)
    n = q.shape[0]
    first = lane_masks(n)
    for h in range(HEADS // 2):
        at = slice(h * 128, (h + 1) * 128)
        p0, p1 = pair_probs(q[:, at], stacked(k[:, at], first))
        both = jnp.concatenate([p0.astype(BF16), p1.astype(BF16)], axis=1)
        turned[:, h, :] = nn(both, stacked(v[:, at], first))
    o_ref[...] = turned[...].astype(BF16)


def probs_kernel(x_ref, p_ref):
    x = x_ref[...].astype(F32)
    q, k, _ = qkv_of(x, x.shape[1] // 3)
    n = q.shape[0]
    first = lane_masks(n)
    for h in range(HEADS // 2):
        at = slice(h * 128, (h + 1) * 128)
        p0, p1 = pair_probs(q[:, at], stacked(k[:, at], first))
        p_ref[h, :, 0:n] = p0
        p_ref[h, :, n : 2 * n] = p1


def backward_kernel(x_ref, p_ref, g_ref, o_ref, turned):
    x = x_ref[...].astype(F32)
    steps = x.shape[1] // 3
    q, k, v = qkv_of(x, steps)
    n = q.shape[0]
    turned[...] = g_ref[...].astype(F32)
    first = lane_masks(n)
    for h in range(HEADS // 2):
        at = slice(h * 128, (h + 1) * 128)
        grads = pair_backward(
            p_ref[h, :, 0:n],
            p_ref[h, :, n : 2 * n],
            q[:, at],
            k[:, at],
            v[:, at],
            turned[:, h, :].astype(BF16),
            first,
        )
        joined = jnp.concatenate([d.reshape(n // steps, steps, 128) for d in grads], axis=1)
        o_ref[:, :, at] = joined.astype(BF16)


def middle_kernel(
    me_ref, w_hbm, x_ref, rest_hbm, gain_ref, slope_ref, row_ref, col_ref, turn_ref,
    gr_ref, gt_ref, rest_v, inner_ref, width_v, qkv_v, fc_v, out_v, turned, proj, joined, sem,
):
    sp = w_hbm.shape[0]
    tm = w_hbm.shape[1] // 40
    n, third = 8 * tm, 2 * tm
    copies = []

    def load(src, dst):
        copies.append(pltpu.make_async_copy(src, dst, sem.at[len(copies)]))
        copies[-1].start()

    load(rest_hbm.at[:, me_ref[0]], rest_v)
    at = 3 * n
    for dst, base, tail in (
        (fc_v, at, at + 12 * tm),
        (out_v, at + 6 * tm, at + 12 * tm + third),
    ):
        load(w_hbm.at[:, pl.ds(base, 6 * tm), :], dst.at[:, :, pl.ds(0, 768)])
        for j in range(3):
            load(
                w_hbm.at[:, pl.ds(tail, third), pl.ds(j * 256, 256)],
                dst.at[:, pl.ds(j * third, third), pl.ds(768, 256)],
            )
    for j in range(3):
        load(w_hbm.at[:, pl.ds(j * n, n), :], qkv_v.at[:, :, pl.ds(j * 768, 768)])

    tokens = x_ref.shape[0]
    width = gain_ref.shape[1]
    inner = 768
    rows, cols = row_ref[...], col_ref[...]
    distance = jnp.abs((rows >> 5) - (cols >> 5)) + jnp.abs((rows & 31) - (cols & 31))
    distance = distance.astype(F32)
    gain = gain_ref[...]
    turn = turn_ref[...]
    turned[...] = x_ref[...].astype(F32)
    mixed = jnp.concatenate([turned[:, h, :] for h in range(6)], axis=1).astype(BF16)
    mixed = nn(turn, mixed).astype(BF16)

    inner_ref[...] = gathered_order(tm, sp, 6)
    width_v[...] = gathered_order(tm, sp, 8)
    mixed = nn(mixed, inner_ref[...]).astype(BF16)
    for c in copies[:5]:
        c.wait()
    rest = rest_v[...].reshape(tokens, 2 * width)
    cot = rest[:, width:]
    fc = fc_v[...].reshape(inner, width)
    hidden = rest[:, :width].astype(F32) + nn(mixed, fc)
    centred = hidden - jnp.mean(hidden, axis=-1, keepdims=True)
    inv_std = lax.rsqrt(jnp.mean(centred * centred, axis=-1, keepdims=True) + EPSILON)
    normed = centred * inv_std
    normed_in = (normed * gain).astype(BF16)

    for c in copies[5:9]:
        c.wait()
    normed_in = nn(normed_in, width_v[...]).astype(BF16)
    grad_mixed = nt(cot, out_v[...].reshape(inner, width)).astype(BF16)
    grad_mixed = nt(grad_mixed, inner_ref[...]).astype(BF16)

    for c in copies[9:]:
        c.wait()
    qkv = qkv_v[...].reshape(width, 3 * inner)
    proj[...] = nn(normed_in, qkv).astype(BF16)

    first = lane_masks(tokens)
    for h in range(HEADS // 2):
        q, k, v = (proj[:, j * inner + h * 128 : j * inner + (h + 1) * 128] for j in range(3))
        g = grad_mixed[:, h * 128 : (h + 1) * 128]
        p0, p1 = pair_probs(
            q, stacked(k, first), -slope_ref[2 * h] * distance, -slope_ref[2 * h + 1] * distance
        )
        for j, d in enumerate(pair_backward(p0, p1, q, k, v, g, first)):
            joined[:, j * inner + h * 128 : j * inner + (h + 1) * 128] = d.astype(BF16)

    grad_normed = nt(joined[...], qkv).astype(BF16)
    grad_normed = nt(grad_normed, width_v[...])
    scaled = grad_normed * gain
    first_mean = jnp.mean(scaled, axis=-1, keepdims=True)
    second_mean = jnp.mean(scaled * normed, axis=-1, keepdims=True)
    term = inv_std * (scaled - first_mean - normed * second_mean)
    grad_resid = (cot.astype(F32) + term).astype(BF16)
    gr_ref[...] = grad_resid
    grad_time = nt(grad_resid, fc).astype(BF16)
    grad_time = nt(grad_time, inner_ref[...]).astype(BF16)
    grad_time = tn(turn, grad_time)
    for h in range(6):
        turned[:, h, :] = grad_time[:, h * 128 : (h + 1) * 128]
    gt_ref[...] = turned[...].astype(BF16)


def body(
    time_query,
    time_key,
    time_value,
    residual_in,
    fc_weight,
    norm_gain,
    qkv_weight,
    out_weight,
    bias_slope,
    visible,
    cotangent,
):
    tm, sp = lax.axis_size("tm"), lax.axis_size("space")
    steps, tubes, inner = time_query.shape[1:]
    width = residual_in.shape[-1]
    total = tm * steps
    both = ("tm", "space")
    shape = jax.ShapeDtypeStruct

    def exchange(x, axes):
        return lax.all_to_all(x, axes, split_axis=0, concat_axis=0, tiled=True)

    to_tubes = jnp.asarray(transposed_rows(steps, tubes))
    to_steps = jnp.asarray(transposed_rows(tubes, steps))
    to_order = jnp.asarray(transposed_rows(tm, sp))
    me = lax.axis_index("space").astype(jnp.int32).reshape(1)
    shards, rest = pl.pallas_call(
        first_kernel,
        out_shape=(shape((tm, 40, inner), BF16), shape((steps, tubes, 2 * width), BF16)),
        in_specs=[HBM] * 5,
        out_specs=(VMEM, VMEM),
        scratch_shapes=[
            pltpu.VMEM(fc_weight.shape, BF16),
            pltpu.VMEM(out_weight.shape, BF16),
            pltpu.VMEM(qkv_weight.shape, BF16),
            pltpu.SemaphoreType.DMA((5,)),
        ],
        compiler_params=params(56),
        name="first",
    )(fc_weight, out_weight, qkv_weight, residual_in, cotangent)
    rest = lax.all_gather(rest, "space", axis=0)
    shards = exchange(shards, "tm")

    send = pl.pallas_call(
        pack_kernel,
        out_shape=shape((tubes, 3 * steps, inner), BF16),
        in_specs=[VMEM] * 4,
        out_specs=VMEM,
        compiler_params=params(16),
        cost_estimate=pl.CostEstimate(flops=10**9, bytes_accessed=4 * 10**6, transcendentals=0),
        name="pack",
    )(time_query, time_key, time_value, to_tubes)

    shards = pl.pallas_call(
        weights_unpack_kernel,
        out_shape=shape((40 * tm, inner), BF16),
        in_specs=[VMEM],
        out_specs=VMEM,
        compiler_params=params(24),
        name="weights_unpack",
    )(shards)
    weights = lax.all_gather(shards, "space", axis=0)

    send, shards = lax.optimization_barrier((send, shards))
    got = exchange(send, "tm")

    mixed = pl.pallas_call(
        forward_kernel,
        out_shape=shape((total, 6, 128), BF16),
        in_specs=[VMEM],
        out_specs=VMEM,
        scratch_shapes=[pltpu.VMEM((total, 6, 128), F32)],
        compiler_params=params(24),
        cost_estimate=pl.CostEstimate(flops=10**8, bytes_accessed=2 * 10**6, transcendentals=2 * 10**5),
        name="temporal_forward",
    )(got)
    mixed = exchange(mixed, both)

    grad_resid, grad_time = pl.pallas_call(
        middle_kernel,
        out_shape=(shape((total, width), BF16), shape((total, 6, 128), BF16)),
        in_specs=[SMEM, HBM, VMEM, HBM, VMEM, SMEM, VMEM, VMEM, VMEM],
        out_specs=(VMEM, VMEM),
        scratch_shapes=[
            pltpu.VMEM((sp, tubes, 2 * width), BF16),
            pltpu.VMEM((inner, inner), BF16),
            pltpu.VMEM((width, width), BF16),
            pltpu.VMEM((sp, 8 * tm, 3 * inner), BF16),
            pltpu.VMEM((sp, 6 * tm, width), BF16),
            pltpu.VMEM((sp, 6 * tm, width), BF16),
            pltpu.VMEM((total, 6, 128), F32),
            pltpu.VMEM((total, 3 * inner), BF16),
            pltpu.VMEM((total, 3 * inner), BF16),
            pltpu.SemaphoreType.DMA((12,)),
        ],
        compiler_params=params(56),
        cost_estimate=pl.CostEstimate(flops=4 * 10**9, bytes_accessed=10**7, transcendentals=2 * 10**5),
        name="middle",
    )(
        me,
        weights,
        mixed,
        rest,
        norm_gain.reshape(1, width),
        bias_slope,
        visible.reshape(total, 1),
        visible.reshape(1, total),
        to_order,
    )
    got, grad_time = lax.optimization_barrier((got, grad_time))
    grad_time = exchange(grad_time, both)
    probs = pl.pallas_call(
        probs_kernel,
        out_shape=shape((HEADS // 2, total, 2 * total), F32),
        in_specs=[VMEM],
        out_specs=VMEM,
        compiler_params=params(24),
        cost_estimate=pl.CostEstimate(flops=10**9, bytes_accessed=4 * 10**6, transcendentals=2 * 10**5),
        name="temporal_probs",
    )(got)

    grad_resid, grad_time = lax.optimization_barrier((grad_resid, grad_time))
    grad_resid = exchange(grad_resid.reshape(steps, tubes, width), "space")
    back = pl.pallas_call(
        backward_kernel,
        out_shape=shape((tm, 3 * steps, inner), BF16),
        in_specs=[VMEM] * 3,
        out_specs=VMEM,
        scratch_shapes=[pltpu.VMEM((total, 6, 128), F32)],
        compiler_params=params(24),
        cost_estimate=pl.CostEstimate(flops=3 * 10**8, bytes_accessed=2 * 10**6, transcendentals=0),
        name="temporal_backward",
    )(got, probs, grad_time)
    back, grad_resid = lax.optimization_barrier((back, grad_resid))
    back = exchange(back, "tm")
    outs = pl.pallas_call(
        unpack_kernel,
        out_shape=(shape(residual_in.shape, BF16),) + (shape(time_query.shape, BF16),) * 3,
        in_specs=[VMEM] * 3,
        out_specs=(VMEM,) * 4,
        compiler_params=params(24),
        name="unpack",
    )(back, to_steps, grad_resid)
    return tuple(outs)


def solution(mesh):
    token = P("dp", "tm", "space", None)
    row = P(("tm", "space"), None)
    in_specs = (token, token, token, token, row, P(), row, row, P(), P("dp", None), token)
    return jax.shard_map(
        body, mesh=mesh, in_specs=in_specs, out_specs=(token,) * 4, check_vma=False
    )
```

```python
import numpy as np
import jax
import jax.numpy as jnp
from jax import lax
from jax.experimental import pallas as pl
from jax.experimental.pallas import tpu as pltpu
from jax.sharding import PartitionSpec as P

HEADS = 12
HD = 64
GRID = 32
SCALE = HD ** (-0.5)
EPSILON = 1e-05
F32 = jnp.float32
BF16 = jnp.bfloat16
VMEM = pl.BlockSpec(memory_space=pltpu.VMEM)
SMEM = pl.BlockSpec(memory_space=pltpu.SMEM)
HBM = pl.BlockSpec(memory_space=pltpu.HBM)


def params(mib):
    return pltpu.CompilerParams(vmem_limit_bytes=mib * 2**20)


def nn(a, b):
    return jnp.dot(a, b, preferred_element_type=F32)


def nt(a, b):
    return lax.dot_general(a, b, (((1,), (1,)), ((), ())), preferred_element_type=F32)


def tn(a, b):
    return lax.dot_general(a, b, (((0,), (0,)), ((), ())), preferred_element_type=F32)


def transposed_rows(outer, inner):
    m = np.zeros((outer * inner, outer * inner), np.float32)
    i, j = np.meshgrid(np.arange(outer), np.arange(inner), indexing="ij")
    m[(j * outer + i).ravel(), (i * inner + j).ravel()] = 1
    return m.astype(BF16)


def gathered_order(tm, sp, rows):
    size = tm * sp * rows
    at = lax.broadcasted_iota(jnp.int32, (size, 1), 0)
    block = (at * (65536 // rows + 1)) >> 16
    a = (block * (65536 // sp + 1)) >> 16
    to = ((block - a * sp) * tm + a) * rows + at - block * rows
    column = lax.broadcasted_iota(jnp.int32, (size, size), 1)
    return jnp.where(column == to, 1.0, 0.0).astype(BF16)


def sixth(n):
    return (n * 10923) >> 16


def main_order(tm):
    at = lax.broadcasted_iota(jnp.int32, (12 * tm, 1), 0)
    which = jnp.where(at >= 6 * tm, 1, 0)
    n = at - which * 6 * tm
    a = sixth(n)
    source = a * 16 + which * 6 + n - a * 6
    column = lax.broadcasted_iota(jnp.int32, (12 * tm, 16 * tm), 1)
    return jnp.where(column == source, 1.0, 0.0).astype(BF16)


def rest_order(tm, to, src):
    third = 2 * tm
    at = lax.broadcasted_iota(jnp.int32, (2 * third, 1), 0)
    which = jnp.where(at >= third, 1, 0)
    n = at - which * third + to * third
    a = sixth(n)
    g = which * 6 + n - a * 6
    source = jnp.where((g >> 2) == src, a * 16 + 12 + (g & 3), -1)
    column = lax.broadcasted_iota(jnp.int32, (2 * third, 16 * tm), 1)
    return jnp.where(column == source, 1.0, 0.0).astype(BF16)


def first_kernel(
    fc_hbm, out_hbm, qkv_hbm, res_hbm, cot_hbm, q_hbm, k_hbm, v_hbm, turn_ref,
    o_ref, rest_ref, send_ref, fc_ref, out_ref, qkv_ref, time_ref, sem,
):
    width = res_hbm.shape[-1]
    copies = [
        pltpu.make_async_copy(res_hbm.at[0], rest_ref.at[:, :, pl.ds(0, width)], sem.at[0]),
        pltpu.make_async_copy(cot_hbm.at[0], rest_ref.at[:, :, pl.ds(width, width)], sem.at[1]),
        pltpu.make_async_copy(fc_hbm, fc_ref, sem.at[2]),
        pltpu.make_async_copy(out_hbm, out_ref, sem.at[3]),
        pltpu.make_async_copy(qkv_hbm, qkv_ref, sem.at[4]),
    ]
    for j, src in enumerate((q_hbm, k_hbm, v_hbm)):
        copies.append(pltpu.make_async_copy(src.at[0], time_ref.at[j], sem.at[5 + j]))
    for c in copies[2:] + copies[:2]:
        c.start()
    for c in copies[2:5]:
        c.wait()
    both = jnp.concatenate([fc_ref[...].astype(F32), out_ref[...].astype(F32)], axis=0)
    tail = both[:, 768:]
    tail = jnp.concatenate([tail[0:4], tail[4:8], tail[8:12]], axis=1)
    qkv = qkv_ref[...].astype(F32)
    block = jnp.concatenate(
        [both[:, :768], tail, qkv[:, :768], qkv[:, 768:1536], qkv[:, 1536:]], axis=0
    )
    o_ref[...] = jnp.broadcast_to(block[None], o_ref.shape).astype(BF16)
    steps, tubes, inner = time_ref.shape[1:]
    parts = []
    for j in range(3):
        copies[5 + j].wait()
        turned = nn(turn_ref[...], time_ref[j].reshape(steps * tubes, inner))
        parts.append(turned.reshape(tubes, steps, inner))
    send_ref[...] = jnp.concatenate(parts, axis=1).astype(BF16)
    for c in copies[:2]:
        c.wait()


def weights_unpack_kernel(x_ref, o_ref):
    tm = x_ref.shape[0]
    x = x_ref[...].astype(F32)
    fo = x[:, 0:16].reshape(16 * tm, 768).astype(BF16)
    n = 8 * tm
    for j in range(3):
        o_ref[pl.ds(j * n, n), :] = x[:, 16 + 8 * j : 24 + 8 * j].reshape(n, 768).astype(BF16)
    o_ref[pl.ds(3 * n, 12 * tm), :] = nn(main_order(tm), fo).astype(BF16)
    for j in range(3):
        part = nn(rest_order(tm, j, 0), fo[:, :256])
        part += nn(rest_order(tm, j, 1), fo[:, 256:512])
        part += nn(rest_order(tm, j, 2), fo[:, 512:])
        o_ref[pl.ds(3 * n + 12 * tm, 4 * tm), pl.ds(j * 256, 256)] = part.astype(BF16)


def unpack_kernel(x_ref, turn_ref, gr_ref, gr_out, *outs):
    gr_out[0] = gr_ref[...]
    x = x_ref[...].astype(F32)
    tubes, steps = x.shape[0], x.shape[1] // 3
    for j, o_ref in enumerate(outs):
        part = x[:, j * steps : (j + 1) * steps].reshape(tubes * steps, -1).astype(BF16)
        o_ref[0] = nn(turn_ref[...], part).astype(BF16).reshape(steps, tubes, -1)


def lane_masks(rows):
    lane = lax.broadcasted_iota(jnp.int32, (rows, 2 * HD), 1)
    return lane < HD


def stacked(block, first):
    zero = jnp.zeros_like(block)
    return jnp.concatenate([jnp.where(first, block, zero), jnp.where(first, zero, block)], axis=0)


def softmax(scores):
    exponent = jnp.exp(scores - jnp.max(scores, axis=-1, keepdims=True))
    return exponent * (1.0 / jnp.sum(exponent, axis=-1, keepdims=True))


def pair_probs(q, k2, bias0=None, bias1=None):
    n = q.shape[0]
    scores = nt(q, k2) * SCALE
    s0, s1 = scores[:, :n], scores[:, n:]
    if bias0 is not None:
        s0, s1 = s0 + bias0, s1 + bias1
    return softmax(s0), softmax(s1)


def pair_backward(p0, p1, q, k, v, g, first):
    n = q.shape[0]
    k2, v2, q2, g2 = (stacked(x, first) for x in (k, v, q, g))
    gp = nt(g, v2)
    g0, g1 = gp[:, :n], gp[:, n:]
    d0 = (p0 * (g0 - jnp.sum(p0 * g0, axis=-1, keepdims=True))).astype(BF16)
    d1 = (p1 * (g1 - jnp.sum(p1 * g1, axis=-1, keepdims=True))).astype(BF16)
    grad_q = nn(jnp.concatenate([d0, d1], axis=1), k2)
    grad_k = tn(jnp.concatenate([d0, d1], axis=0), q2)
    grad_v = tn(jnp.concatenate([p0.astype(BF16), p1.astype(BF16)], axis=0), g2)
    return grad_q * SCALE, grad_k * SCALE, grad_v


def qkv_of(x, steps):
    return [
        x[:, j * steps : (j + 1) * steps].reshape(x.shape[0] * steps, -1).astype(BF16)
        for j in range(3)
    ]


def forward_kernel(x_ref, o_ref, turned):
    x = x_ref[...].astype(F32)
    q, k, v = qkv_of(x, x.shape[1] // 3)
    n = q.shape[0]
    first = lane_masks(n)
    for h in range(HEADS // 2):
        at = slice(h * 128, (h + 1) * 128)
        p0, p1 = pair_probs(q[:, at], stacked(k[:, at], first))
        both = jnp.concatenate([p0.astype(BF16), p1.astype(BF16)], axis=1)
        turned[:, h, :] = nn(both, stacked(v[:, at], first))
    o_ref[...] = turned[...].astype(BF16)


def probs_kernel(x_ref, p_ref):
    x = x_ref[...].astype(F32)
    q, k, _ = qkv_of(x, x.shape[1] // 3)
    n = q.shape[0]
    first = lane_masks(n)
    for h in range(HEADS // 2):
        at = slice(h * 128, (h + 1) * 128)
        p0, p1 = pair_probs(q[:, at], stacked(k[:, at], first))
        p_ref[h, :, 0:n] = p0
        p_ref[h, :, n : 2 * n] = p1


def backward_kernel(x_ref, p_ref, g_ref, o_ref, turned):
    x = x_ref[...].astype(F32)
    steps = x.shape[1] // 3
    q, k, v = qkv_of(x, steps)
    n = q.shape[0]
    turned[...] = g_ref[...].astype(F32)
    first = lane_masks(n)
    for h in range(HEADS // 2):
        at = slice(h * 128, (h + 1) * 128)
        grads = pair_backward(
            p_ref[h, :, 0:n],
            p_ref[h, :, n : 2 * n],
            q[:, at],
            k[:, at],
            v[:, at],
            turned[:, h, :].astype(BF16),
            first,
        )
        joined = jnp.concatenate([d.reshape(n // steps, steps, 128) for d in grads], axis=1)
        o_ref[:, :, at] = joined.astype(BF16)


def middle_kernel(
    me_ref, w_hbm, x_ref, rest_hbm, gain_ref, slope_ref, row_ref, col_ref, turn_ref,
    gr_ref, gt_ref, rest_v, inner_ref, width_v, qkv_v, fc_v, out_v, turned, proj, joined, sem,
):
    sp = w_hbm.shape[0]
    tm = w_hbm.shape[1] // 40
    n, third = 8 * tm, 2 * tm
    copies = []

    def load(src, dst):
        copies.append(pltpu.make_async_copy(src, dst, sem.at[len(copies)]))
        copies[-1].start()

    load(rest_hbm.at[:, me_ref[0]], rest_v)
    at = 3 * n
    for dst, base, tail in (
        (fc_v, at, at + 12 * tm),
        (out_v, at + 6 * tm, at + 12 * tm + third),
    ):
        load(w_hbm.at[:, pl.ds(base, 6 * tm), :], dst.at[:, :, pl.ds(0, 768)])
        for j in range(3):
            load(
                w_hbm.at[:, pl.ds(tail, third), pl.ds(j * 256, 256)],
                dst.at[:, pl.ds(j * third, third), pl.ds(768, 256)],
            )
    for j in range(3):
        load(w_hbm.at[:, pl.ds(j * n, n), :], qkv_v.at[:, :, pl.ds(j * 768, 768)])

    tokens = x_ref.shape[0]
    width = gain_ref.shape[1]
    inner = 768
    rows, cols = row_ref[...], col_ref[...]
    distance = jnp.abs((rows >> 5) - (cols >> 5)) + jnp.abs((rows & 31) - (cols & 31))
    distance = distance.astype(F32)
    gain = gain_ref[...]
    turn = turn_ref[...]
    turned[...] = x_ref[...].astype(F32)
    mixed = jnp.concatenate([turned[:, h, :] for h in range(6)], axis=1).astype(BF16)
    mixed = nn(turn, mixed).astype(BF16)

    inner_ref[...] = gathered_order(tm, sp, 6)
    width_v[...] = gathered_order(tm, sp, 8)
    mixed = nn(mixed, inner_ref[...]).astype(BF16)
    for c in copies[:5]:
        c.wait()
    rest = rest_v[...].reshape(tokens, 2 * width)
    cot = rest[:, width:]
    fc = fc_v[...].reshape(inner, width)
    hidden = rest[:, :width].astype(F32) + nn(mixed, fc)
    centred = hidden - jnp.mean(hidden, axis=-1, keepdims=True)
    inv_std = lax.rsqrt(jnp.mean(centred * centred, axis=-1, keepdims=True) + EPSILON)
    normed = centred * inv_std
    normed_in = (normed * gain).astype(BF16)

    for c in copies[5:9]:
        c.wait()
    normed_in = nn(normed_in, width_v[...]).astype(BF16)
    grad_mixed = nt(cot, out_v[...].reshape(inner, width)).astype(BF16)
    grad_mixed = nt(grad_mixed, inner_ref[...]).astype(BF16)

    for c in copies[9:]:
        c.wait()
    qkv = qkv_v[...].reshape(width, 3 * inner)
    proj[...] = nn(normed_in, qkv).astype(BF16)

    first = lane_masks(tokens)
    for h in range(HEADS // 2):
        q, k, v = (proj[:, j * inner + h * 128 : j * inner + (h + 1) * 128] for j in range(3))
        g = grad_mixed[:, h * 128 : (h + 1) * 128]
        p0, p1 = pair_probs(
            q, stacked(k, first), -slope_ref[2 * h] * distance, -slope_ref[2 * h + 1] * distance
        )
        for j, d in enumerate(pair_backward(p0, p1, q, k, v, g, first)):
            joined[:, j * inner + h * 128 : j * inner + (h + 1) * 128] = d.astype(BF16)

    grad_normed = nt(joined[...], qkv).astype(BF16)
    grad_normed = nt(grad_normed, width_v[...])
    scaled = grad_normed * gain
    first_mean = jnp.mean(scaled, axis=-1, keepdims=True)
    second_mean = jnp.mean(scaled * normed, axis=-1, keepdims=True)
    term = inv_std * (scaled - first_mean - normed * second_mean)
    grad_resid = (cot.astype(F32) + term).astype(BF16)
    gr_ref[...] = grad_resid
    grad_time = nt(grad_resid, fc).astype(BF16)
    grad_time = nt(grad_time, inner_ref[...]).astype(BF16)
    grad_time = tn(turn, grad_time)
    for h in range(6):
        turned[:, h, :] = grad_time[:, h * 128 : (h + 1) * 128]
    gt_ref[...] = turned[...].astype(BF16)


def body(
    time_query,
    time_key,
    time_value,
    residual_in,
    fc_weight,
    norm_gain,
    qkv_weight,
    out_weight,
    bias_slope,
    visible,
    cotangent,
):
    tm, sp = lax.axis_size("tm"), lax.axis_size("space")
    steps, tubes, inner = time_query.shape[1:]
    width = residual_in.shape[-1]
    total = tm * steps
    both = ("tm", "space")
    shape = jax.ShapeDtypeStruct

    def exchange(x, axes):
        return lax.all_to_all(x, axes, split_axis=0, concat_axis=0, tiled=True)

    to_tubes = jnp.asarray(transposed_rows(steps, tubes))
    to_steps = jnp.asarray(transposed_rows(tubes, steps))
    to_order = jnp.asarray(transposed_rows(tm, sp))
    me = lax.axis_index("space").astype(jnp.int32).reshape(1)
    shards, rest, send = pl.pallas_call(
        first_kernel,
        out_shape=(
            shape((tm, 40, inner), BF16),
            shape((steps, tubes, 2 * width), BF16),
            shape((tubes, 3 * steps, inner), BF16),
        ),
        in_specs=[HBM] * 8 + [VMEM],
        out_specs=(VMEM,) * 3,
        scratch_shapes=[
            pltpu.VMEM(fc_weight.shape, BF16),
            pltpu.VMEM(out_weight.shape, BF16),
            pltpu.VMEM(qkv_weight.shape, BF16),
            pltpu.VMEM((3, steps, tubes, inner), BF16),
            pltpu.SemaphoreType.DMA((8,)),
        ],
        compiler_params=params(56),
        name="first",
    )(
        fc_weight,
        out_weight,
        qkv_weight,
        residual_in,
        cotangent,
        time_query,
        time_key,
        time_value,
        to_tubes,
    )
    rest = lax.all_gather(rest, "space", axis=0)
    shards = exchange(shards, "tm")

    shards = pl.pallas_call(
        weights_unpack_kernel,
        out_shape=shape((40 * tm, inner), BF16),
        in_specs=[VMEM],
        out_specs=VMEM,
        compiler_params=params(24),
        name="weights_unpack",
    )(shards)
    weights = lax.all_gather(shards, "space", axis=0)

    send, shards = lax.optimization_barrier((send, shards))
    got = exchange(send, "tm")

    mixed = pl.pallas_call(
        forward_kernel,
        out_shape=shape((total, 6, 128), BF16),
        in_specs=[VMEM],
        out_specs=VMEM,
        scratch_shapes=[pltpu.VMEM((total, 6, 128), F32)],
        compiler_params=params(24),
        cost_estimate=pl.CostEstimate(flops=10**8, bytes_accessed=2 * 10**6, transcendentals=2 * 10**5),
        name="temporal_forward",
    )(got)
    mixed = exchange(mixed, both)

    grad_resid, grad_time = pl.pallas_call(
        middle_kernel,
        out_shape=(shape((total, width), BF16), shape((total, 6, 128), BF16)),
        in_specs=[SMEM, HBM, VMEM, HBM, VMEM, SMEM, VMEM, VMEM, VMEM],
        out_specs=(VMEM, VMEM),
        scratch_shapes=[
            pltpu.VMEM((sp, tubes, 2 * width), BF16),
            pltpu.VMEM((inner, inner), BF16),
            pltpu.VMEM((width, width), BF16),
            pltpu.VMEM((sp, 8 * tm, 3 * inner), BF16),
            pltpu.VMEM((sp, 6 * tm, width), BF16),
            pltpu.VMEM((sp, 6 * tm, width), BF16),
            pltpu.VMEM((total, 6, 128), F32),
            pltpu.VMEM((total, 3 * inner), BF16),
            pltpu.VMEM((total, 3 * inner), BF16),
            pltpu.SemaphoreType.DMA((12,)),
        ],
        compiler_params=params(52),
        cost_estimate=pl.CostEstimate(flops=4 * 10**9, bytes_accessed=10**7, transcendentals=2 * 10**5),
        name="middle",
    )(
        me,
        weights,
        mixed,
        rest,
        norm_gain.reshape(1, width),
        bias_slope,
        visible.reshape(total, 1),
        visible.reshape(1, total),
        to_order,
    )
    got, grad_time = lax.optimization_barrier((got, grad_time))
    grad_time = exchange(grad_time, both)
    probs = pl.pallas_call(
        probs_kernel,
        out_shape=shape((HEADS // 2, total, 2 * total), F32),
        in_specs=[VMEM],
        out_specs=VMEM,
        compiler_params=params(24),
        cost_estimate=pl.CostEstimate(flops=10**9, bytes_accessed=4 * 10**6, transcendentals=2 * 10**5),
        name="temporal_probs",
    )(got)

    grad_resid, grad_time = lax.optimization_barrier((grad_resid, grad_time))
    grad_resid = exchange(grad_resid.reshape(steps, tubes, width), "space")
    back = pl.pallas_call(
        backward_kernel,
        out_shape=shape((tm, 3 * steps, inner), BF16),
        in_specs=[VMEM] * 3,
        out_specs=VMEM,
        scratch_shapes=[pltpu.VMEM((total, 6, 128), F32)],
        compiler_params=params(24),
        cost_estimate=pl.CostEstimate(flops=3 * 10**8, bytes_accessed=2 * 10**6, transcendentals=0),
        name="temporal_backward",
    )(got, probs, grad_time)
    back, grad_resid = lax.optimization_barrier((back, grad_resid))
    back = exchange(back, "tm")
    outs = pl.pallas_call(
        unpack_kernel,
        out_shape=(shape(residual_in.shape, BF16),) + (shape(time_query.shape, BF16),) * 3,
        in_specs=[VMEM] * 3,
        out_specs=(VMEM,) * 4,
        compiler_params=params(24),
        name="unpack",
    )(back, to_steps, grad_resid)
    return tuple(outs)


def solution(mesh):
    token = P("dp", "tm", "space", None)
    row = P(("tm", "space"), None)
    in_specs = (token, token, token, token, row, P(), row, row, P(), P("dp", None), token)
    return jax.shard_map(
        body, mesh=mesh, in_specs=in_specs, out_specs=(token,) * 4, check_vma=False
    )
```

```python
import numpy as np
import jax
import jax.numpy as jnp
from jax import lax
from jax.experimental import pallas as pl
from jax.experimental.pallas import tpu as pltpu
from jax.sharding import PartitionSpec as P

HEADS = 12
HD = 64
GRID = 32
SCALE = HD ** (-0.5)
EPSILON = 1e-05
F32 = jnp.float32
BF16 = jnp.bfloat16
VMEM = pl.BlockSpec(memory_space=pltpu.VMEM)
SMEM = pl.BlockSpec(memory_space=pltpu.SMEM)
HBM = pl.BlockSpec(memory_space=pltpu.HBM)


def params(mib):
    return pltpu.CompilerParams(vmem_limit_bytes=mib * 2**20)


def nn(a, b):
    return jnp.dot(a, b, preferred_element_type=F32)


def nt(a, b):
    return lax.dot_general(a, b, (((1,), (1,)), ((), ())), preferred_element_type=F32)


def tn(a, b):
    return lax.dot_general(a, b, (((0,), (0,)), ((), ())), preferred_element_type=F32)


def transposed_rows(outer, inner):
    m = np.zeros((outer * inner, outer * inner), np.float32)
    i, j = np.meshgrid(np.arange(outer), np.arange(inner), indexing="ij")
    m[(j * outer + i).ravel(), (i * inner + j).ravel()] = 1
    return m.astype(BF16)


def gathered_order(tm, sp, rows):
    size = tm * sp * rows
    at = lax.broadcasted_iota(jnp.int32, (size, 1), 0)
    block = (at * (65536 // rows + 1)) >> 16
    a = (block * (65536 // sp + 1)) >> 16
    to = ((block - a * sp) * tm + a) * rows + at - block * rows
    column = lax.broadcasted_iota(jnp.int32, (size, size), 1)
    return jnp.where(column == to, 1.0, 0.0).astype(BF16)


def sixth(n):
    return (n * 10923) >> 16


def main_order(tm):
    at = lax.broadcasted_iota(jnp.int32, (12 * tm, 1), 0)
    which = jnp.where(at >= 6 * tm, 1, 0)
    n = at - which * 6 * tm
    a = sixth(n)
    source = a * 16 + which * 6 + n - a * 6
    column = lax.broadcasted_iota(jnp.int32, (12 * tm, 16 * tm), 1)
    return jnp.where(column == source, 1.0, 0.0).astype(BF16)


def rest_order(tm, to, src):
    third = 2 * tm
    at = lax.broadcasted_iota(jnp.int32, (2 * third, 1), 0)
    which = jnp.where(at >= third, 1, 0)
    n = at - which * third + to * third
    a = sixth(n)
    g = which * 6 + n - a * 6
    source = jnp.where((g >> 2) == src, a * 16 + 12 + (g & 3), -1)
    column = lax.broadcasted_iota(jnp.int32, (2 * third, 16 * tm), 1)
    return jnp.where(column == source, 1.0, 0.0).astype(BF16)


def first_kernel(fc_hbm, out_hbm, qkv_hbm, res_hbm, cot_hbm, o_ref, rest_ref, fc_ref, out_ref, qkv_ref, sem):
    width = res_hbm.shape[-1]
    copies = [
        pltpu.make_async_copy(res_hbm.at[0], rest_ref.at[:, :, pl.ds(0, width)], sem.at[0]),
        pltpu.make_async_copy(cot_hbm.at[0], rest_ref.at[:, :, pl.ds(width, width)], sem.at[1]),
        pltpu.make_async_copy(fc_hbm, fc_ref, sem.at[2]),
        pltpu.make_async_copy(out_hbm, out_ref, sem.at[3]),
        pltpu.make_async_copy(qkv_hbm, qkv_ref, sem.at[4]),
    ]
    for c in copies:
        c.start()
    for c in copies[2:]:
        c.wait()
    both = jnp.concatenate([fc_ref[...].astype(F32), out_ref[...].astype(F32)], axis=0)
    tail = both[:, 768:]
    tail = jnp.concatenate([tail[0:4], tail[4:8], tail[8:12]], axis=1)
    qkv = qkv_ref[...].astype(F32)
    block = jnp.concatenate(
        [both[:, :768], tail, qkv[:, :768], qkv[:, 768:1536], qkv[:, 1536:]], axis=0
    )
    o_ref[...] = jnp.broadcast_to(block[None], o_ref.shape).astype(BF16)
    for c in copies[:2]:
        c.wait()


def weights_unpack_kernel(x_ref, o_ref):
    tm = x_ref.shape[0]
    x = x_ref[...].astype(F32)
    fo = x[:, 0:16].reshape(16 * tm, 768).astype(BF16)
    n = 8 * tm
    for j in range(3):
        o_ref[pl.ds(j * n, n), :] = x[:, 16 + 8 * j : 24 + 8 * j].reshape(n, 768).astype(BF16)
    o_ref[pl.ds(3 * n, 12 * tm), :] = nn(main_order(tm), fo).astype(BF16)
    for j in range(3):
        part = nn(rest_order(tm, j, 0), fo[:, :256])
        part += nn(rest_order(tm, j, 1), fo[:, 256:512])
        part += nn(rest_order(tm, j, 2), fo[:, 512:])
        o_ref[pl.ds(3 * n + 12 * tm, 4 * tm), pl.ds(j * 256, 256)] = part.astype(BF16)


def pack_kernel(q_ref, k_ref, v_ref, turn_ref, o_ref):
    steps, tubes, inner = q_ref.shape[1:]
    rows = steps * tubes
    parts = [
        nn(turn_ref[...], ref[0].reshape(rows, inner)).reshape(tubes, steps, inner)
        for ref in (q_ref, k_ref, v_ref)
    ]
    o_ref[...] = jnp.concatenate(parts, axis=1).astype(BF16)


def slice_kernel(me_ref, gr_hbm, o_ref, sem):
    mine = o_ref.shape[2]
    at = pl.multiple_of(me_ref[0] * mine, mine)
    copy = pltpu.make_async_copy(gr_hbm.at[:, pl.ds(at, mine), :], o_ref.at[0], sem)
    copy.start()
    copy.wait()


def unpack_kernel(x_ref, turn_ref, *outs):
    x = x_ref[...].astype(F32)
    tubes, steps = x.shape[0], x.shape[1] // 3
    for j, o_ref in enumerate(outs):
        part = x[:, j * steps : (j + 1) * steps].reshape(tubes * steps, -1).astype(BF16)
        o_ref[0] = nn(turn_ref[...], part).astype(BF16).reshape(steps, tubes, -1)


def lane_masks(rows):
    lane = lax.broadcasted_iota(jnp.int32, (rows, 2 * HD), 1)
    return lane < HD


def stacked(block, first):
    zero = jnp.zeros_like(block)
    return jnp.concatenate([jnp.where(first, block, zero), jnp.where(first, zero, block)], axis=0)


def softmax(scores):
    exponent = jnp.exp(scores - jnp.max(scores, axis=-1, keepdims=True))
    return exponent * (1.0 / jnp.sum(exponent, axis=-1, keepdims=True))


def pair_probs(q, k2, bias0=None, bias1=None):
    n = q.shape[0]
    scores = nt(q, k2) * SCALE
    s0, s1 = scores[:, :n], scores[:, n:]
    if bias0 is not None:
        s0, s1 = s0 + bias0, s1 + bias1
    return softmax(s0), softmax(s1)


def pair_backward(p0, p1, q, k, v, g, first):
    n = q.shape[0]
    k2, v2, q2, g2 = (stacked(x, first) for x in (k, v, q, g))
    gp = nt(g, v2)
    g0, g1 = gp[:, :n], gp[:, n:]
    d0 = (p0 * (g0 - jnp.sum(p0 * g0, axis=-1, keepdims=True))).astype(BF16)
    d1 = (p1 * (g1 - jnp.sum(p1 * g1, axis=-1, keepdims=True))).astype(BF16)
    grad_q = nn(jnp.concatenate([d0, d1], axis=1), k2)
    grad_k = tn(jnp.concatenate([d0, d1], axis=0), q2)
    grad_v = tn(jnp.concatenate([p0.astype(BF16), p1.astype(BF16)], axis=0), g2)
    return grad_q * SCALE, grad_k * SCALE, grad_v


def qkv_of(x, steps):
    return [
        x[:, j * steps : (j + 1) * steps].reshape(x.shape[0] * steps, -1).astype(BF16)
        for j in range(3)
    ]


def forward_kernel(x_ref, o_ref, turned):
    x = x_ref[...].astype(F32)
    q, k, v = qkv_of(x, x.shape[1] // 3)
    n = q.shape[0]
    first = lane_masks(n)
    for h in range(HEADS // 2):
        at = slice(h * 128, (h + 1) * 128)
        p0, p1 = pair_probs(q[:, at], stacked(k[:, at], first))
        both = jnp.concatenate([p0.astype(BF16), p1.astype(BF16)], axis=1)
        turned[:, h, :] = nn(both, stacked(v[:, at], first))
    o_ref[...] = turned[...].astype(BF16)


def probs_kernel(x_ref, p_ref):
    x = x_ref[...].astype(F32)
    q, k, _ = qkv_of(x, x.shape[1] // 3)
    n = q.shape[0]
    first = lane_masks(n)
    for h in range(HEADS // 2):
        at = slice(h * 128, (h + 1) * 128)
        p0, p1 = pair_probs(q[:, at], stacked(k[:, at], first))
        p_ref[h, :, 0:n] = p0
        p_ref[h, :, n : 2 * n] = p1


def backward_kernel(x_ref, p_ref, g_ref, o_ref, turned):
    x = x_ref[...].astype(F32)
    steps = x.shape[1] // 3
    q, k, v = qkv_of(x, steps)
    n = q.shape[0]
    turned[...] = g_ref[...].astype(F32)
    first = lane_masks(n)
    for h in range(HEADS // 2):
        at = slice(h * 128, (h + 1) * 128)
        grads = pair_backward(
            p_ref[h, :, 0:n],
            p_ref[h, :, n : 2 * n],
            q[:, at],
            k[:, at],
            v[:, at],
            turned[:, h, :].astype(BF16),
            first,
        )
        joined = jnp.concatenate([d.reshape(n // steps, steps, 128) for d in grads], axis=1)
        o_ref[:, :, at] = joined.astype(BF16)


def middle_kernel(
    me_ref, w_hbm, x_ref, rest_hbm, gain_ref, slope_ref, row_ref, col_ref, turn_ref,
    gr_ref, gt_ref, rest_v, inner_ref, width_v, qkv_v, fc_v, out_v, turned, proj, joined, sem,
):
    sp = w_hbm.shape[0]
    tm = w_hbm.shape[1] // 40
    n, third = 8 * tm, 2 * tm
    copies = []

    def load(src, dst):
        copies.append(pltpu.make_async_copy(src, dst, sem.at[len(copies)]))
        copies[-1].start()

    load(rest_hbm.at[:, me_ref[0]], rest_v)
    at = 3 * n
    for dst, base, tail in (
        (fc_v, at, at + 12 * tm),
        (out_v, at + 6 * tm, at + 12 * tm + third),
    ):
        load(w_hbm.at[:, pl.ds(base, 6 * tm), :], dst.at[:, :, pl.ds(0, 768)])
        for j in range(3):
            load(
                w_hbm.at[:, pl.ds(tail, third), pl.ds(j * 256, 256)],
                dst.at[:, pl.ds(j * third, third), pl.ds(768, 256)],
            )
    for j in range(3):
        load(w_hbm.at[:, pl.ds(j * n, n), :], qkv_v.at[:, :, pl.ds(j * 768, 768)])

    tokens = x_ref.shape[0]
    width = gain_ref.shape[1]
    inner = 768
    rows, cols = row_ref[...], col_ref[...]
    distance = jnp.abs((rows >> 5) - (cols >> 5)) + jnp.abs((rows & 31) - (cols & 31))
    distance = distance.astype(F32)
    gain = gain_ref[...]
    turn = turn_ref[...]
    turned[...] = x_ref[...].astype(F32)
    mixed = jnp.concatenate([turned[:, h, :] for h in range(6)], axis=1).astype(BF16)
    mixed = nn(turn, mixed).astype(BF16)

    inner_ref[...] = gathered_order(tm, sp, 6)
    width_v[...] = gathered_order(tm, sp, 8)
    mixed = nn(mixed, inner_ref[...]).astype(BF16)
    for c in copies[:5]:
        c.wait()
    rest = rest_v[...].reshape(tokens, 2 * width)
    cot = rest[:, width:]
    fc = fc_v[...].reshape(inner, width)
    hidden = rest[:, :width].astype(F32) + nn(mixed, fc)
    centred = hidden - jnp.mean(hidden, axis=-1, keepdims=True)
    inv_std = lax.rsqrt(jnp.mean(centred * centred, axis=-1, keepdims=True) + EPSILON)
    normed = centred * inv_std
    normed_in = (normed * gain).astype(BF16)

    for c in copies[5:9]:
        c.wait()
    normed_in = nn(normed_in, width_v[...]).astype(BF16)
    grad_mixed = nt(cot, out_v[...].reshape(inner, width)).astype(BF16)
    grad_mixed = nt(grad_mixed, inner_ref[...]).astype(BF16)

    for c in copies[9:]:
        c.wait()
    qkv = qkv_v[...].reshape(width, 3 * inner)
    proj[...] = nn(normed_in, qkv).astype(BF16)

    first = lane_masks(tokens)
    for h in range(HEADS // 2):
        q, k, v = (proj[:, j * inner + h * 128 : j * inner + (h + 1) * 128] for j in range(3))
        g = grad_mixed[:, h * 128 : (h + 1) * 128]
        p0, p1 = pair_probs(
            q, stacked(k, first), -slope_ref[2 * h] * distance, -slope_ref[2 * h + 1] * distance
        )
        for j, d in enumerate(pair_backward(p0, p1, q, k, v, g, first)):
            joined[:, j * inner + h * 128 : j * inner + (h + 1) * 128] = d.astype(BF16)

    grad_normed = nt(joined[...], qkv).astype(BF16)
    grad_normed = nt(grad_normed, width_v[...])
    scaled = grad_normed * gain
    first_mean = jnp.mean(scaled, axis=-1, keepdims=True)
    second_mean = jnp.mean(scaled * normed, axis=-1, keepdims=True)
    term = inv_std * (scaled - first_mean - normed * second_mean)
    grad_resid = (cot.astype(F32) + term).astype(BF16)
    gr_ref[...] = grad_resid
    grad_time = nt(grad_resid, fc).astype(BF16)
    grad_time = nt(grad_time, inner_ref[...]).astype(BF16)
    grad_time = tn(turn, grad_time)
    for h in range(6):
        turned[:, h, :] = grad_time[:, h * 128 : (h + 1) * 128]
    gt_ref[...] = turned[...].astype(BF16)


def body(
    time_query,
    time_key,
    time_value,
    residual_in,
    fc_weight,
    norm_gain,
    qkv_weight,
    out_weight,
    bias_slope,
    visible,
    cotangent,
):
    tm, sp = lax.axis_size("tm"), lax.axis_size("space")
    steps, tubes, inner = time_query.shape[1:]
    width = residual_in.shape[-1]
    total = tm * steps
    both = ("tm", "space")
    shape = jax.ShapeDtypeStruct

    def exchange(x, axes):
        return lax.all_to_all(x, axes, split_axis=0, concat_axis=0, tiled=True)

    to_tubes = jnp.asarray(transposed_rows(steps, tubes))
    to_steps = jnp.asarray(transposed_rows(tubes, steps))
    to_order = jnp.asarray(transposed_rows(tm, sp))
    me = lax.axis_index("space").astype(jnp.int32).reshape(1)
    shards, rest = pl.pallas_call(
        first_kernel,
        out_shape=(shape((tm, 40, inner), BF16), shape((steps, tubes, 2 * width), BF16)),
        in_specs=[HBM] * 5,
        out_specs=(VMEM, VMEM),
        scratch_shapes=[
            pltpu.VMEM(fc_weight.shape, BF16),
            pltpu.VMEM(out_weight.shape, BF16),
            pltpu.VMEM(qkv_weight.shape, BF16),
            pltpu.SemaphoreType.DMA((5,)),
        ],
        compiler_params=params(56),
        name="first",
    )(fc_weight, out_weight, qkv_weight, residual_in, cotangent)
    rest = lax.all_gather(rest, "space", axis=0)
    shards = exchange(shards, "tm")

    send = pl.pallas_call(
        pack_kernel,
        out_shape=shape((tubes, 3 * steps, inner), BF16),
        in_specs=[VMEM] * 4,
        out_specs=VMEM,
        compiler_params=params(16),
        cost_estimate=pl.CostEstimate(flops=10**9, bytes_accessed=4 * 10**6, transcendentals=0),
        name="pack",
    )(time_query, time_key, time_value, to_tubes)

    shards = pl.pallas_call(
        weights_unpack_kernel,
        out_shape=shape((40 * tm, inner), BF16),
        in_specs=[VMEM],
        out_specs=VMEM,
        compiler_params=params(24),
        name="weights_unpack",
    )(shards)
    weights = lax.all_gather(shards, "space", axis=0)

    send, shards = lax.optimization_barrier((send, shards))
    got = exchange(send, "tm")

    mixed = pl.pallas_call(
        forward_kernel,
        out_shape=shape((total, 6, 128), BF16),
        in_specs=[VMEM],
        out_specs=VMEM,
        scratch_shapes=[pltpu.VMEM((total, 6, 128), F32)],
        compiler_params=params(24),
        cost_estimate=pl.CostEstimate(flops=10**8, bytes_accessed=2 * 10**6, transcendentals=2 * 10**5),
        name="temporal_forward",
    )(got)
    mixed = exchange(mixed, both)

    grad_resid, grad_time = pl.pallas_call(
        middle_kernel,
        out_shape=(shape((total, width), BF16), shape((total, 6, 128), BF16)),
        in_specs=[SMEM, HBM, VMEM, HBM, VMEM, SMEM, VMEM, VMEM, VMEM],
        out_specs=(VMEM, VMEM),
        scratch_shapes=[
            pltpu.VMEM((sp, tubes, 2 * width), BF16),
            pltpu.VMEM((inner, inner), BF16),
            pltpu.VMEM((width, width), BF16),
            pltpu.VMEM((sp, 8 * tm, 3 * inner), BF16),
            pltpu.VMEM((sp, 6 * tm, width), BF16),
            pltpu.VMEM((sp, 6 * tm, width), BF16),
            pltpu.VMEM((total, 6, 128), F32),
            pltpu.VMEM((total, 3 * inner), BF16),
            pltpu.VMEM((total, 3 * inner), BF16),
            pltpu.SemaphoreType.DMA((12,)),
        ],
        compiler_params=params(52),
        cost_estimate=pl.CostEstimate(flops=4 * 10**9, bytes_accessed=10**7, transcendentals=2 * 10**5),
        name="middle",
    )(
        me,
        weights,
        mixed,
        rest,
        norm_gain.reshape(1, width),
        bias_slope,
        visible.reshape(total, 1),
        visible.reshape(1, total),
        to_order,
    )
    grad_resid = lax.all_gather(grad_resid, "space", axis=0)
    got, grad_time = lax.optimization_barrier((got, grad_time))
    grad_time = exchange(grad_time, both)
    probs = pl.pallas_call(
        probs_kernel,
        out_shape=shape((HEADS // 2, total, 2 * total), F32),
        in_specs=[VMEM],
        out_specs=VMEM,
        compiler_params=params(24),
        cost_estimate=pl.CostEstimate(flops=10**9, bytes_accessed=4 * 10**6, transcendentals=2 * 10**5),
        name="temporal_probs",
    )(got)

    back = pl.pallas_call(
        backward_kernel,
        out_shape=shape((tm, 3 * steps, inner), BF16),
        in_specs=[VMEM] * 3,
        out_specs=VMEM,
        scratch_shapes=[pltpu.VMEM((total, 6, 128), F32)],
        compiler_params=params(24),
        cost_estimate=pl.CostEstimate(flops=3 * 10**8, bytes_accessed=2 * 10**6, transcendentals=0),
        name="temporal_backward",
    )(got, probs, grad_time)
    back, grad_resid = lax.optimization_barrier((back, grad_resid))
    back = exchange(back, "tm")
    outs = pl.pallas_call(
        unpack_kernel,
        out_shape=(shape(time_query.shape, BF16),) * 3,
        in_specs=[VMEM, VMEM],
        out_specs=(VMEM,) * 3,
        compiler_params=params(24),
        name="unpack",
    )(back, to_steps)
    grad_resid = pl.pallas_call(
        slice_kernel,
        out_shape=shape(residual_in.shape, BF16),
        in_specs=[SMEM, HBM],
        out_specs=VMEM,
        scratch_shapes=[pltpu.SemaphoreType.DMA],
        compiler_params=params(56),
        cost_estimate=pl.CostEstimate(flops=10**9, bytes_accessed=4 * 10**6, transcendentals=0),
        name="slice",
    )(me, grad_resid)
    return (grad_resid, *outs)


def solution(mesh):
    token = P("dp", "tm", "space", None)
    row = P(("tm", "space"), None)
    in_specs = (token, token, token, token, row, P(), row, row, P(), P("dp", None), token)
    return jax.shard_map(
        body, mesh=mesh, in_specs=in_specs, out_specs=(token,) * 4, check_vma=False
    )
```

```python
import numpy as np
import jax
import jax.numpy as jnp
from jax import lax
from jax.experimental import pallas as pl
from jax.experimental.pallas import tpu as pltpu
from jax.sharding import PartitionSpec as P

HEADS = 12
HD = 64
GRID = 32
SCALE = HD ** (-0.5)
EPSILON = 1e-05
F32 = jnp.float32
BF16 = jnp.bfloat16
VMEM = pl.BlockSpec(memory_space=pltpu.VMEM)
SMEM = pl.BlockSpec(memory_space=pltpu.SMEM)
HBM = pl.BlockSpec(memory_space=pltpu.HBM)


def params(mib):
    return pltpu.CompilerParams(vmem_limit_bytes=mib * 2**20)


def nn(a, b):
    return jnp.dot(a, b, preferred_element_type=F32)


def nt(a, b):
    return lax.dot_general(a, b, (((1,), (1,)), ((), ())), preferred_element_type=F32)


def tn(a, b):
    return lax.dot_general(a, b, (((0,), (0,)), ((), ())), preferred_element_type=F32)


def transposed_rows(outer, inner):
    m = np.zeros((outer * inner, outer * inner), np.float32)
    i, j = np.meshgrid(np.arange(outer), np.arange(inner), indexing="ij")
    m[(j * outer + i).ravel(), (i * inner + j).ravel()] = 1
    return m.astype(BF16)


def gathered_order(tm, sp, rows):
    size = tm * sp * rows
    at = lax.broadcasted_iota(jnp.int32, (size, 1), 0)
    block = (at * (65536 // rows + 1)) >> 16
    a = (block * (65536 // sp + 1)) >> 16
    to = ((block - a * sp) * tm + a) * rows + at - block * rows
    column = lax.broadcasted_iota(jnp.int32, (size, size), 1)
    return jnp.where(column == to, 1.0, 0.0).astype(BF16)


def sixth(n):
    return (n * 10923) >> 16


def main_order(tm):
    at = lax.broadcasted_iota(jnp.int32, (12 * tm, 1), 0)
    which = jnp.where(at >= 6 * tm, 1, 0)
    n = at - which * 6 * tm
    a = sixth(n)
    source = a * 16 + which * 6 + n - a * 6
    column = lax.broadcasted_iota(jnp.int32, (12 * tm, 16 * tm), 1)
    return jnp.where(column == source, 1.0, 0.0).astype(BF16)


def rest_order(tm, to, src):
    third = 2 * tm
    at = lax.broadcasted_iota(jnp.int32, (2 * third, 1), 0)
    which = jnp.where(at >= third, 1, 0)
    n = at - which * third + to * third
    a = sixth(n)
    g = which * 6 + n - a * 6
    source = jnp.where((g >> 2) == src, a * 16 + 12 + (g & 3), -1)
    column = lax.broadcasted_iota(jnp.int32, (2 * third, 16 * tm), 1)
    return jnp.where(column == source, 1.0, 0.0).astype(BF16)


def first_kernel(fc_hbm, out_hbm, qkv_hbm, o_ref, fc_ref, out_ref, qkv_ref, sem):
    copies = [
        pltpu.make_async_copy(fc_hbm, fc_ref, sem.at[0]),
        pltpu.make_async_copy(out_hbm, out_ref, sem.at[1]),
        pltpu.make_async_copy(qkv_hbm, qkv_ref, sem.at[2]),
    ]
    for c in copies:
        c.start()
    for c in copies:
        c.wait()
    both = jnp.concatenate([fc_ref[...].astype(F32), out_ref[...].astype(F32)], axis=0)
    tail = both[:, 768:]
    tail = jnp.concatenate([tail[0:4], tail[4:8], tail[8:12]], axis=1)
    qkv = qkv_ref[...].astype(F32)
    block = jnp.concatenate(
        [both[:, :768], tail, qkv[:, :768], qkv[:, 768:1536], qkv[:, 1536:]], axis=0
    )
    o_ref[...] = jnp.broadcast_to(block[None], o_ref.shape).astype(BF16)


def weights_unpack_kernel(x_ref, o_ref):
    tm = x_ref.shape[0]
    x = x_ref[...].astype(F32)
    fo = x[:, 0:16].reshape(16 * tm, 768).astype(BF16)
    n = 8 * tm
    for j in range(3):
        o_ref[pl.ds(j * n, n), :] = x[:, 16 + 8 * j : 24 + 8 * j].reshape(n, 768).astype(BF16)
    o_ref[pl.ds(3 * n, 12 * tm), :] = nn(main_order(tm), fo).astype(BF16)
    for j in range(3):
        part = nn(rest_order(tm, j, 0), fo[:, :256])
        part += nn(rest_order(tm, j, 1), fo[:, 256:512])
        part += nn(rest_order(tm, j, 2), fo[:, 512:])
        o_ref[pl.ds(3 * n + 12 * tm, 4 * tm), pl.ds(j * 256, 256)] = part.astype(BF16)


def pack_kernel(q_ref, k_ref, v_ref, turn_ref, o_ref):
    steps, tubes, inner = q_ref.shape[1:]
    rows = steps * tubes
    parts = [
        nn(turn_ref[...], ref[0].reshape(rows, inner)).reshape(tubes, steps, inner)
        for ref in (q_ref, k_ref, v_ref)
    ]
    o_ref[...] = jnp.concatenate(parts, axis=1).astype(BF16)


def slice_kernel(me_ref, gr_hbm, o_ref, sem):
    mine = o_ref.shape[2]
    at = pl.multiple_of(me_ref[0] * mine, mine)
    copy = pltpu.make_async_copy(gr_hbm.at[:, pl.ds(at, mine), :], o_ref.at[0], sem)
    copy.start()
    copy.wait()


def unpack_kernel(x_ref, turn_ref, *outs):
    x = x_ref[...].astype(F32)
    tubes, steps = x.shape[0], x.shape[1] // 3
    for j, o_ref in enumerate(outs):
        part = x[:, j * steps : (j + 1) * steps].reshape(tubes * steps, -1).astype(BF16)
        o_ref[0] = nn(turn_ref[...], part).astype(BF16).reshape(steps, tubes, -1)


def lane_masks(rows):
    lane = lax.broadcasted_iota(jnp.int32, (rows, 2 * HD), 1)
    return lane < HD


def stacked(block, first):
    zero = jnp.zeros_like(block)
    return jnp.concatenate([jnp.where(first, block, zero), jnp.where(first, zero, block)], axis=0)


def softmax(scores):
    exponent = jnp.exp(scores - jnp.max(scores, axis=-1, keepdims=True))
    return exponent * (1.0 / jnp.sum(exponent, axis=-1, keepdims=True))


def pair_probs(q, k2, bias0=None, bias1=None):
    n = q.shape[0]
    scores = nt(q, k2) * SCALE
    s0, s1 = scores[:, :n], scores[:, n:]
    if bias0 is not None:
        s0, s1 = s0 + bias0, s1 + bias1
    return softmax(s0), softmax(s1)


def pair_backward(p0, p1, q, k, v, g, first):
    n = q.shape[0]
    k2, v2, q2, g2 = (stacked(x, first) for x in (k, v, q, g))
    gp = nt(g, v2)
    g0, g1 = gp[:, :n], gp[:, n:]
    d0 = (p0 * (g0 - jnp.sum(p0 * g0, axis=-1, keepdims=True))).astype(BF16)
    d1 = (p1 * (g1 - jnp.sum(p1 * g1, axis=-1, keepdims=True))).astype(BF16)
    grad_q = nn(jnp.concatenate([d0, d1], axis=1), k2)
    grad_k = tn(jnp.concatenate([d0, d1], axis=0), q2)
    grad_v = tn(jnp.concatenate([p0.astype(BF16), p1.astype(BF16)], axis=0), g2)
    return grad_q * SCALE, grad_k * SCALE, grad_v


def qkv_of(x, steps):
    return [
        x[:, j * steps : (j + 1) * steps].reshape(x.shape[0] * steps, -1).astype(BF16)
        for j in range(3)
    ]


def forward_kernel(x_ref, o_ref, turned):
    x = x_ref[...].astype(F32)
    q, k, v = qkv_of(x, x.shape[1] // 3)
    n = q.shape[0]
    first = lane_masks(n)
    for h in range(HEADS // 2):
        at = slice(h * 128, (h + 1) * 128)
        p0, p1 = pair_probs(q[:, at], stacked(k[:, at], first))
        both = jnp.concatenate([p0.astype(BF16), p1.astype(BF16)], axis=1)
        turned[:, h, :] = nn(both, stacked(v[:, at], first))
    o_ref[...] = turned[...].astype(BF16)


def probs_kernel(x_ref, p_ref):
    x = x_ref[...].astype(F32)
    q, k, _ = qkv_of(x, x.shape[1] // 3)
    n = q.shape[0]
    first = lane_masks(n)
    for h in range(HEADS // 2):
        at = slice(h * 128, (h + 1) * 128)
        p0, p1 = pair_probs(q[:, at], stacked(k[:, at], first))
        p_ref[h, :, 0:n] = p0
        p_ref[h, :, n : 2 * n] = p1


def backward_kernel(x_ref, p_ref, g_ref, o_ref, turned):
    x = x_ref[...].astype(F32)
    steps = x.shape[1] // 3
    q, k, v = qkv_of(x, steps)
    n = q.shape[0]
    turned[...] = g_ref[...].astype(F32)
    first = lane_masks(n)
    for h in range(HEADS // 2):
        at = slice(h * 128, (h + 1) * 128)
        grads = pair_backward(
            p_ref[h, :, 0:n],
            p_ref[h, :, n : 2 * n],
            q[:, at],
            k[:, at],
            v[:, at],
            turned[:, h, :].astype(BF16),
            first,
        )
        joined = jnp.concatenate([d.reshape(n // steps, steps, 128) for d in grads], axis=1)
        o_ref[:, :, at] = joined.astype(BF16)


def middle_kernel(
    me_ref, w_hbm, x_ref, rest_hbm, gain_ref, slope_ref, row_ref, col_ref, turn_ref,
    gr_ref, gt_ref, rest_v, inner_ref, width_v, qkv_v, fc_v, out_v, turned, proj, joined, sem,
):
    sp = w_hbm.shape[0]
    tm = w_hbm.shape[1] // 40
    n, third = 8 * tm, 2 * tm
    copies = []

    def load(src, dst):
        copies.append(pltpu.make_async_copy(src, dst, sem.at[len(copies)]))
        copies[-1].start()

    load(rest_hbm.at[:, me_ref[0]], rest_v)
    at = 3 * n
    for dst, base, tail in (
        (fc_v, at, at + 12 * tm),
        (out_v, at + 6 * tm, at + 12 * tm + third),
    ):
        load(w_hbm.at[:, pl.ds(base, 6 * tm), :], dst.at[:, :, pl.ds(0, 768)])
        for j in range(3):
            load(
                w_hbm.at[:, pl.ds(tail, third), pl.ds(j * 256, 256)],
                dst.at[:, pl.ds(j * third, third), pl.ds(768, 256)],
            )
    for j in range(3):
        load(w_hbm.at[:, pl.ds(j * n, n), :], qkv_v.at[:, :, pl.ds(j * 768, 768)])

    tokens = x_ref.shape[0]
    width = gain_ref.shape[1]
    inner = 768
    rows, cols = row_ref[...], col_ref[...]
    distance = jnp.abs((rows >> 5) - (cols >> 5)) + jnp.abs((rows & 31) - (cols & 31))
    distance = distance.astype(F32)
    gain = gain_ref[...]
    turn = turn_ref[...]
    turned[...] = x_ref[...].astype(F32)
    mixed = jnp.concatenate([turned[:, h, :] for h in range(6)], axis=1).astype(BF16)
    mixed = nn(turn, mixed).astype(BF16)

    inner_ref[...] = gathered_order(tm, sp, 6)
    width_v[...] = gathered_order(tm, sp, 8)
    mixed = nn(mixed, inner_ref[...]).astype(BF16)
    for c in copies[:5]:
        c.wait()
    rest = rest_v[...].reshape(tokens, 2 * width)
    cot = rest[:, width:]
    fc = fc_v[...].reshape(inner, width)
    hidden = rest[:, :width].astype(F32) + nn(mixed, fc)
    centred = hidden - jnp.mean(hidden, axis=-1, keepdims=True)
    inv_std = lax.rsqrt(jnp.mean(centred * centred, axis=-1, keepdims=True) + EPSILON)
    normed = centred * inv_std
    normed_in = (normed * gain).astype(BF16)

    for c in copies[5:9]:
        c.wait()
    normed_in = nn(normed_in, width_v[...]).astype(BF16)
    grad_mixed = nt(cot, out_v[...].reshape(inner, width)).astype(BF16)
    grad_mixed = nt(grad_mixed, inner_ref[...]).astype(BF16)

    for c in copies[9:]:
        c.wait()
    qkv = qkv_v[...].reshape(width, 3 * inner)
    proj[...] = nn(normed_in, qkv).astype(BF16)

    first = lane_masks(tokens)
    for h in range(HEADS // 2):
        q, k, v = (proj[:, j * inner + h * 128 : j * inner + (h + 1) * 128] for j in range(3))
        g = grad_mixed[:, h * 128 : (h + 1) * 128]
        p0, p1 = pair_probs(
            q, stacked(k, first), -slope_ref[2 * h] * distance, -slope_ref[2 * h + 1] * distance
        )
        for j, d in enumerate(pair_backward(p0, p1, q, k, v, g, first)):
            joined[:, j * inner + h * 128 : j * inner + (h + 1) * 128] = d.astype(BF16)

    grad_normed = nt(joined[...], qkv).astype(BF16)
    grad_normed = nt(grad_normed, width_v[...])
    scaled = grad_normed * gain
    first_mean = jnp.mean(scaled, axis=-1, keepdims=True)
    second_mean = jnp.mean(scaled * normed, axis=-1, keepdims=True)
    term = inv_std * (scaled - first_mean - normed * second_mean)
    grad_resid = (cot.astype(F32) + term).astype(BF16)
    gr_ref[...] = grad_resid
    grad_time = nt(grad_resid, fc).astype(BF16)
    grad_time = nt(grad_time, inner_ref[...]).astype(BF16)
    grad_time = tn(turn, grad_time)
    for h in range(6):
        turned[:, h, :] = grad_time[:, h * 128 : (h + 1) * 128]
    gt_ref[...] = turned[...].astype(BF16)


def body(
    time_query,
    time_key,
    time_value,
    residual_in,
    fc_weight,
    norm_gain,
    qkv_weight,
    out_weight,
    bias_slope,
    visible,
    cotangent,
):
    tm, sp = lax.axis_size("tm"), lax.axis_size("space")
    steps, tubes, inner = time_query.shape[1:]
    width = residual_in.shape[-1]
    total = tm * steps
    both = ("tm", "space")
    shape = jax.ShapeDtypeStruct

    def exchange(x, axes):
        return lax.all_to_all(x, axes, split_axis=0, concat_axis=0, tiled=True)

    to_tubes = jnp.asarray(transposed_rows(steps, tubes))
    to_steps = jnp.asarray(transposed_rows(tubes, steps))
    to_order = jnp.asarray(transposed_rows(tm, sp))
    me = lax.axis_index("space").astype(jnp.int32).reshape(1)
    rest = jnp.concatenate([residual_in[0], cotangent[0]], axis=-1)
    rest, fc_weight = lax.optimization_barrier((rest, fc_weight))
    shards = pl.pallas_call(
        first_kernel,
        out_shape=shape((tm, 40, inner), BF16),
        in_specs=[HBM] * 3,
        out_specs=VMEM,
        scratch_shapes=[
            pltpu.VMEM(fc_weight.shape, BF16),
            pltpu.VMEM(out_weight.shape, BF16),
            pltpu.VMEM(qkv_weight.shape, BF16),
            pltpu.SemaphoreType.DMA((3,)),
        ],
        compiler_params=params(56),
        name="first",
    )(fc_weight, out_weight, qkv_weight)
    rest = lax.all_gather(rest, "space", axis=0)
    shards = exchange(shards, "tm")

    send = pl.pallas_call(
        pack_kernel,
        out_shape=shape((tubes, 3 * steps, inner), BF16),
        in_specs=[VMEM] * 4,
        out_specs=VMEM,
        compiler_params=params(16),
        cost_estimate=pl.CostEstimate(flops=10**9, bytes_accessed=4 * 10**6, transcendentals=0),
        name="pack",
    )(time_query, time_key, time_value, to_tubes)

    shards = pl.pallas_call(
        weights_unpack_kernel,
        out_shape=shape((40 * tm, inner), BF16),
        in_specs=[VMEM],
        out_specs=VMEM,
        compiler_params=params(24),
        name="weights_unpack",
    )(shards)
    weights = lax.all_gather(shards, "space", axis=0)

    send, shards = lax.optimization_barrier((send, shards))
    got = exchange(send, "tm")

    mixed = pl.pallas_call(
        forward_kernel,
        out_shape=shape((total, 6, 128), BF16),
        in_specs=[VMEM],
        out_specs=VMEM,
        scratch_shapes=[pltpu.VMEM((total, 6, 128), F32)],
        compiler_params=params(24),
        cost_estimate=pl.CostEstimate(flops=10**8, bytes_accessed=2 * 10**6, transcendentals=2 * 10**5),
        name="temporal_forward",
    )(got)
    mixed = exchange(mixed, both)

    grad_resid, grad_time = pl.pallas_call(
        middle_kernel,
        out_shape=(shape((total, width), BF16), shape((total, 6, 128), BF16)),
        in_specs=[SMEM, HBM, VMEM, HBM, VMEM, SMEM, VMEM, VMEM, VMEM],
        out_specs=(VMEM, VMEM),
        scratch_shapes=[
            pltpu.VMEM((sp, tubes, 2 * width), BF16),
            pltpu.VMEM((inner, inner), BF16),
            pltpu.VMEM((width, width), BF16),
            pltpu.VMEM((sp, 8 * tm, 3 * inner), BF16),
            pltpu.VMEM((sp, 6 * tm, width), BF16),
            pltpu.VMEM((sp, 6 * tm, width), BF16),
            pltpu.VMEM((total, 6, 128), F32),
            pltpu.VMEM((total, 3 * inner), BF16),
            pltpu.VMEM((total, 3 * inner), BF16),
            pltpu.SemaphoreType.DMA((12,)),
        ],
        compiler_params=params(52),
        cost_estimate=pl.CostEstimate(flops=4 * 10**9, bytes_accessed=10**7, transcendentals=2 * 10**5),
        name="middle",
    )(
        me,
        weights,
        mixed,
        rest,
        norm_gain.reshape(1, width),
        bias_slope,
        visible.reshape(total, 1),
        visible.reshape(1, total),
        to_order,
    )
    grad_resid = lax.all_gather(grad_resid, "space", axis=0)
    got, grad_time = lax.optimization_barrier((got, grad_time))
    grad_time = exchange(grad_time, both)
    probs = pl.pallas_call(
        probs_kernel,
        out_shape=shape((HEADS // 2, total, 2 * total), F32),
        in_specs=[VMEM],
        out_specs=VMEM,
        compiler_params=params(24),
        cost_estimate=pl.CostEstimate(flops=10**9, bytes_accessed=4 * 10**6, transcendentals=2 * 10**5),
        name="temporal_probs",
    )(got)

    back = pl.pallas_call(
        backward_kernel,
        out_shape=shape((tm, 3 * steps, inner), BF16),
        in_specs=[VMEM] * 3,
        out_specs=VMEM,
        scratch_shapes=[pltpu.VMEM((total, 6, 128), F32)],
        compiler_params=params(24),
        cost_estimate=pl.CostEstimate(flops=3 * 10**8, bytes_accessed=2 * 10**6, transcendentals=0),
        name="temporal_backward",
    )(got, probs, grad_time)
    back, grad_resid = lax.optimization_barrier((back, grad_resid))
    back = exchange(back, "tm")
    outs = pl.pallas_call(
        unpack_kernel,
        out_shape=(shape(time_query.shape, BF16),) * 3,
        in_specs=[VMEM, VMEM],
        out_specs=(VMEM,) * 3,
        compiler_params=params(24),
        name="unpack",
    )(back, to_steps)
    grad_resid = pl.pallas_call(
        slice_kernel,
        out_shape=shape(residual_in.shape, BF16),
        in_specs=[SMEM, HBM],
        out_specs=VMEM,
        scratch_shapes=[pltpu.SemaphoreType.DMA],
        compiler_params=params(56),
        cost_estimate=pl.CostEstimate(flops=10**9, bytes_accessed=4 * 10**6, transcendentals=0),
        name="slice",
    )(me, grad_resid)
    return (grad_resid, *outs)


def solution(mesh):
    token = P("dp", "tm", "space", None)
    row = P(("tm", "space"), None)
    in_specs = (token, token, token, token, row, P(), row, row, P(), P("dp", None), token)
    return jax.shard_map(
        body, mesh=mesh, in_specs=in_specs, out_specs=(token,) * 4, check_vma=False
    )
```

```python
import numpy as np
import jax
import jax.numpy as jnp
from jax import lax
from jax.experimental import pallas as pl
from jax.experimental.pallas import tpu as pltpu
from jax.sharding import PartitionSpec as P

HEADS = 12
HD = 64
GRID = 32
SCALE = HD ** (-0.5)
EPSILON = 1e-05
F32 = jnp.float32
BF16 = jnp.bfloat16
VMEM = pl.BlockSpec(memory_space=pltpu.VMEM)
SMEM = pl.BlockSpec(memory_space=pltpu.SMEM)
HBM = pl.BlockSpec(memory_space=pltpu.HBM)


def params(mib):
    return pltpu.CompilerParams(vmem_limit_bytes=mib * 2**20)


def nn(a, b):
    return jnp.dot(a, b, preferred_element_type=F32)


def nt(a, b):
    return lax.dot_general(a, b, (((1,), (1,)), ((), ())), preferred_element_type=F32)


def tn(a, b):
    return lax.dot_general(a, b, (((0,), (0,)), ((), ())), preferred_element_type=F32)


def transposed_rows(outer, inner):
    m = np.zeros((outer * inner, outer * inner), np.float32)
    i, j = np.meshgrid(np.arange(outer), np.arange(inner), indexing="ij")
    m[(j * outer + i).ravel(), (i * inner + j).ravel()] = 1
    return m.astype(BF16)


def gathered_order(tm, sp, rows):
    size = tm * sp * rows
    at = lax.broadcasted_iota(jnp.int32, (size, 1), 0)
    block = (at * (65536 // rows + 1)) >> 16
    a = (block * (65536 // sp + 1)) >> 16
    to = ((block - a * sp) * tm + a) * rows + at - block * rows
    column = lax.broadcasted_iota(jnp.int32, (size, size), 1)
    return jnp.where(column == to, 1.0, 0.0).astype(BF16)


def sixth(n):
    return (n * 10923) >> 16


def main_order(tm):
    at = lax.broadcasted_iota(jnp.int32, (12 * tm, 1), 0)
    which = jnp.where(at >= 6 * tm, 1, 0)
    n = at - which * 6 * tm
    a = sixth(n)
    source = a * 16 + which * 6 + n - a * 6
    column = lax.broadcasted_iota(jnp.int32, (12 * tm, 16 * tm), 1)
    return jnp.where(column == source, 1.0, 0.0).astype(BF16)


def rest_order(tm, to, src):
    third = 2 * tm
    at = lax.broadcasted_iota(jnp.int32, (2 * third, 1), 0)
    which = jnp.where(at >= third, 1, 0)
    n = at - which * third + to * third
    a = sixth(n)
    g = which * 6 + n - a * 6
    source = jnp.where((g >> 2) == src, a * 16 + 12 + (g & 3), -1)
    column = lax.broadcasted_iota(jnp.int32, (2 * third, 16 * tm), 1)
    return jnp.where(column == source, 1.0, 0.0).astype(BF16)


def join_kernel(res_hbm, cot_hbm, o_hbm, both, sem):
    width = res_hbm.shape[-1]
    part = both.shape[0] // 4
    loads, stores = [], []
    for i in range(4):
        at = pl.ds(i * part, part)
        for j, src in enumerate((res_hbm, cot_hbm)):
            dst = both.at[at, :, pl.ds(j * width, width)]
            loads.append(pltpu.make_async_copy(src.at[0, at], dst, sem.at[0, i, j]))
            loads[-1].start()
    for i in range(4):
        at = pl.ds(i * part, part)
        loads[2 * i].wait()
        loads[2 * i + 1].wait()
        stores.append(pltpu.make_async_copy(both.at[at], o_hbm.at[at], sem.at[1, i, 0]))
        stores[-1].start()
    for c in stores:
        c.wait()


def first_kernel(fc_hbm, out_hbm, qkv_hbm, o_ref, fc_ref, out_ref, qkv_ref, sem):
    copies = [
        pltpu.make_async_copy(fc_hbm, fc_ref, sem.at[0]),
        pltpu.make_async_copy(out_hbm, out_ref, sem.at[1]),
        pltpu.make_async_copy(qkv_hbm, qkv_ref, sem.at[2]),
    ]
    for c in copies:
        c.start()
    for c in copies:
        c.wait()
    both = jnp.concatenate([fc_ref[...].astype(F32), out_ref[...].astype(F32)], axis=0)
    tail = both[:, 768:]
    tail = jnp.concatenate([tail[0:4], tail[4:8], tail[8:12]], axis=1)
    qkv = qkv_ref[...].astype(F32)
    block = jnp.concatenate(
        [both[:, :768], tail, qkv[:, :768], qkv[:, 768:1536], qkv[:, 1536:]], axis=0
    )
    o_ref[...] = jnp.broadcast_to(block[None], o_ref.shape).astype(BF16)


def weights_unpack_kernel(x_ref, o_ref):
    tm = x_ref.shape[0]
    x = x_ref[...].astype(F32)
    fo = x[:, 0:16].reshape(16 * tm, 768).astype(BF16)
    n = 8 * tm
    for j in range(3):
        o_ref[pl.ds(j * n, n), :] = x[:, 16 + 8 * j : 24 + 8 * j].reshape(n, 768).astype(BF16)
    o_ref[pl.ds(3 * n, 12 * tm), :] = nn(main_order(tm), fo).astype(BF16)
    for j in range(3):
        part = nn(rest_order(tm, j, 0), fo[:, :256])
        part += nn(rest_order(tm, j, 1), fo[:, 256:512])
        part += nn(rest_order(tm, j, 2), fo[:, 512:])
        o_ref[pl.ds(3 * n + 12 * tm, 4 * tm), pl.ds(j * 256, 256)] = part.astype(BF16)


def pack_kernel(q_ref, k_ref, v_ref, turn_ref, o_ref):
    steps, tubes, inner = q_ref.shape[1:]
    rows = steps * tubes
    parts = [
        nn(turn_ref[...], ref[0].reshape(rows, inner)).reshape(tubes, steps, inner)
        for ref in (q_ref, k_ref, v_ref)
    ]
    o_ref[...] = jnp.concatenate(parts, axis=1).astype(BF16)


def slice_kernel(me_ref, gr_hbm, o_ref, sem):
    mine = o_ref.shape[2]
    at = pl.multiple_of(me_ref[0] * mine, mine)
    copy = pltpu.make_async_copy(gr_hbm.at[:, pl.ds(at, mine), :], o_ref.at[0], sem)
    copy.start()
    copy.wait()


def unpack_kernel(x_ref, turn_ref, *outs):
    x = x_ref[...].astype(F32)
    tubes, steps = x.shape[0], x.shape[1] // 3
    for j, o_ref in enumerate(outs):
        part = x[:, j * steps : (j + 1) * steps].reshape(tubes * steps, -1).astype(BF16)
        o_ref[0] = nn(turn_ref[...], part).astype(BF16).reshape(steps, tubes, -1)


def lane_masks(rows):
    lane = lax.broadcasted_iota(jnp.int32, (rows, 2 * HD), 1)
    return lane < HD


def stacked(block, first):
    zero = jnp.zeros_like(block)
    return jnp.concatenate([jnp.where(first, block, zero), jnp.where(first, zero, block)], axis=0)


def softmax(scores):
    exponent = jnp.exp(scores - jnp.max(scores, axis=-1, keepdims=True))
    return exponent * (1.0 / jnp.sum(exponent, axis=-1, keepdims=True))


def pair_probs(q, k2, bias0=None, bias1=None):
    n = q.shape[0]
    scores = nt(q, k2) * SCALE
    s0, s1 = scores[:, :n], scores[:, n:]
    if bias0 is not None:
        s0, s1 = s0 + bias0, s1 + bias1
    return softmax(s0), softmax(s1)


def pair_backward(p0, p1, q, k, v, g, first):
    n = q.shape[0]
    k2, v2, q2, g2 = (stacked(x, first) for x in (k, v, q, g))
    gp = nt(g, v2)
    g0, g1 = gp[:, :n], gp[:, n:]
    d0 = (p0 * (g0 - jnp.sum(p0 * g0, axis=-1, keepdims=True))).astype(BF16)
    d1 = (p1 * (g1 - jnp.sum(p1 * g1, axis=-1, keepdims=True))).astype(BF16)
    grad_q = nn(jnp.concatenate([d0, d1], axis=1), k2)
    grad_k = tn(jnp.concatenate([d0, d1], axis=0), q2)
    grad_v = tn(jnp.concatenate([p0.astype(BF16), p1.astype(BF16)], axis=0), g2)
    return grad_q * SCALE, grad_k * SCALE, grad_v


def qkv_of(x, steps):
    return [
        x[:, j * steps : (j + 1) * steps].reshape(x.shape[0] * steps, -1).astype(BF16)
        for j in range(3)
    ]


def forward_kernel(x_ref, o_ref, turned):
    x = x_ref[...].astype(F32)
    q, k, v = qkv_of(x, x.shape[1] // 3)
    n = q.shape[0]
    first = lane_masks(n)
    for h in range(HEADS // 2):
        at = slice(h * 128, (h + 1) * 128)
        p0, p1 = pair_probs(q[:, at], stacked(k[:, at], first))
        both = jnp.concatenate([p0.astype(BF16), p1.astype(BF16)], axis=1)
        turned[:, h, :] = nn(both, stacked(v[:, at], first))
    o_ref[...] = turned[...].astype(BF16)


def probs_kernel(x_ref, p_ref):
    x = x_ref[...].astype(F32)
    q, k, _ = qkv_of(x, x.shape[1] // 3)
    n = q.shape[0]
    first = lane_masks(n)
    for h in range(HEADS // 2):
        at = slice(h * 128, (h + 1) * 128)
        p0, p1 = pair_probs(q[:, at], stacked(k[:, at], first))
        p_ref[h, :, 0:n] = p0
        p_ref[h, :, n : 2 * n] = p1


def backward_kernel(x_ref, p_ref, g_ref, o_ref, turned):
    x = x_ref[...].astype(F32)
    steps = x.shape[1] // 3
    q, k, v = qkv_of(x, steps)
    n = q.shape[0]
    turned[...] = g_ref[...].astype(F32)
    first = lane_masks(n)
    for h in range(HEADS // 2):
        at = slice(h * 128, (h + 1) * 128)
        grads = pair_backward(
            p_ref[h, :, 0:n],
            p_ref[h, :, n : 2 * n],
            q[:, at],
            k[:, at],
            v[:, at],
            turned[:, h, :].astype(BF16),
            first,
        )
        joined = jnp.concatenate([d.reshape(n // steps, steps, 128) for d in grads], axis=1)
        o_ref[:, :, at] = joined.astype(BF16)


def middle_kernel(
    me_ref, w_hbm, x_ref, rest_hbm, gain_ref, slope_ref, row_ref, col_ref, turn_ref,
    gr_ref, gt_ref, rest_v, inner_ref, width_v, qkv_v, fc_v, out_v, turned, proj, joined, sem,
):
    sp = w_hbm.shape[0]
    tm = w_hbm.shape[1] // 40
    n, third = 8 * tm, 2 * tm
    copies = []

    def load(src, dst):
        copies.append(pltpu.make_async_copy(src, dst, sem.at[len(copies)]))
        copies[-1].start()

    load(rest_hbm.at[:, me_ref[0]], rest_v)
    at = 3 * n
    for dst, base, tail in (
        (fc_v, at, at + 12 * tm),
        (out_v, at + 6 * tm, at + 12 * tm + third),
    ):
        load(w_hbm.at[:, pl.ds(base, 6 * tm), :], dst.at[:, :, pl.ds(0, 768)])
        for j in range(3):
            load(
                w_hbm.at[:, pl.ds(tail, third), pl.ds(j * 256, 256)],
                dst.at[:, pl.ds(j * third, third), pl.ds(768, 256)],
            )
    for j in range(3):
        load(w_hbm.at[:, pl.ds(j * n, n), :], qkv_v.at[:, :, pl.ds(j * 768, 768)])

    tokens = x_ref.shape[0]
    width = gain_ref.shape[1]
    inner = 768
    rows, cols = row_ref[...], col_ref[...]
    distance = jnp.abs((rows >> 5) - (cols >> 5)) + jnp.abs((rows & 31) - (cols & 31))
    distance = distance.astype(F32)
    gain = gain_ref[...]
    turn = turn_ref[...]
    turned[...] = x_ref[...].astype(F32)
    mixed = jnp.concatenate([turned[:, h, :] for h in range(6)], axis=1).astype(BF16)
    mixed = nn(turn, mixed).astype(BF16)

    inner_ref[...] = gathered_order(tm, sp, 6)
    width_v[...] = gathered_order(tm, sp, 8)
    mixed = nn(mixed, inner_ref[...]).astype(BF16)
    for c in copies[:5]:
        c.wait()
    rest = rest_v[...].reshape(tokens, 2 * width)
    cot = rest[:, width:]
    fc = fc_v[...].reshape(inner, width)
    hidden = rest[:, :width].astype(F32) + nn(mixed, fc)
    centred = hidden - jnp.mean(hidden, axis=-1, keepdims=True)
    inv_std = lax.rsqrt(jnp.mean(centred * centred, axis=-1, keepdims=True) + EPSILON)
    normed = centred * inv_std
    normed_in = (normed * gain).astype(BF16)

    for c in copies[5:9]:
        c.wait()
    normed_in = nn(normed_in, width_v[...]).astype(BF16)
    grad_mixed = nt(cot, out_v[...].reshape(inner, width)).astype(BF16)
    grad_mixed = nt(grad_mixed, inner_ref[...]).astype(BF16)

    for c in copies[9:]:
        c.wait()
    qkv = qkv_v[...].reshape(width, 3 * inner)
    proj[...] = nn(normed_in, qkv).astype(BF16)

    first = lane_masks(tokens)
    for h in range(HEADS // 2):
        q, k, v = (proj[:, j * inner + h * 128 : j * inner + (h + 1) * 128] for j in range(3))
        g = grad_mixed[:, h * 128 : (h + 1) * 128]
        p0, p1 = pair_probs(
            q, stacked(k, first), -slope_ref[2 * h] * distance, -slope_ref[2 * h + 1] * distance
        )
        for j, d in enumerate(pair_backward(p0, p1, q, k, v, g, first)):
            joined[:, j * inner + h * 128 : j * inner + (h + 1) * 128] = d.astype(BF16)

    grad_normed = nt(joined[...], qkv).astype(BF16)
    grad_normed = nt(grad_normed, width_v[...])
    scaled = grad_normed * gain
    first_mean = jnp.mean(scaled, axis=-1, keepdims=True)
    second_mean = jnp.mean(scaled * normed, axis=-1, keepdims=True)
    term = inv_std * (scaled - first_mean - normed * second_mean)
    grad_resid = (cot.astype(F32) + term).astype(BF16)
    gr_ref[...] = grad_resid
    grad_time = nt(grad_resid, fc).astype(BF16)
    grad_time = nt(grad_time, inner_ref[...]).astype(BF16)
    grad_time = tn(turn, grad_time)
    for h in range(6):
        turned[:, h, :] = grad_time[:, h * 128 : (h + 1) * 128]
    gt_ref[...] = turned[...].astype(BF16)


def body(
    time_query,
    time_key,
    time_value,
    residual_in,
    fc_weight,
    norm_gain,
    qkv_weight,
    out_weight,
    bias_slope,
    visible,
    cotangent,
):
    tm, sp = lax.axis_size("tm"), lax.axis_size("space")
    steps, tubes, inner = time_query.shape[1:]
    width = residual_in.shape[-1]
    total = tm * steps
    both = ("tm", "space")
    shape = jax.ShapeDtypeStruct

    def exchange(x, axes):
        return lax.all_to_all(x, axes, split_axis=0, concat_axis=0, tiled=True)

    to_tubes = jnp.asarray(transposed_rows(steps, tubes))
    to_steps = jnp.asarray(transposed_rows(tubes, steps))
    to_order = jnp.asarray(transposed_rows(tm, sp))
    me = lax.axis_index("space").astype(jnp.int32).reshape(1)
    rest = pl.pallas_call(
        join_kernel,
        out_shape=shape((steps, tubes, 2 * width), BF16),
        in_specs=[HBM] * 2,
        out_specs=HBM,
        scratch_shapes=[pltpu.VMEM((steps, tubes, 2 * width), BF16), pltpu.SemaphoreType.DMA((2, 4, 2))],
        compiler_params=params(56),
        name="join",
    )(residual_in, cotangent)
    rest, fc_weight = lax.optimization_barrier((rest, fc_weight))
    shards = pl.pallas_call(
        first_kernel,
        out_shape=shape((tm, 40, inner), BF16),
        in_specs=[HBM] * 3,
        out_specs=VMEM,
        scratch_shapes=[
            pltpu.VMEM(fc_weight.shape, BF16),
            pltpu.VMEM(out_weight.shape, BF16),
            pltpu.VMEM(qkv_weight.shape, BF16),
            pltpu.SemaphoreType.DMA((3,)),
        ],
        compiler_params=params(56),
        name="first",
    )(fc_weight, out_weight, qkv_weight)
    rest = lax.all_gather(rest, "space", axis=0)
    shards = exchange(shards, "tm")

    send = pl.pallas_call(
        pack_kernel,
        out_shape=shape((tubes, 3 * steps, inner), BF16),
        in_specs=[VMEM] * 4,
        out_specs=VMEM,
        compiler_params=params(16),
        cost_estimate=pl.CostEstimate(flops=10**9, bytes_accessed=4 * 10**6, transcendentals=0),
        name="pack",
    )(time_query, time_key, time_value, to_tubes)

    shards = pl.pallas_call(
        weights_unpack_kernel,
        out_shape=shape((40 * tm, inner), BF16),
        in_specs=[VMEM],
        out_specs=VMEM,
        compiler_params=params(24),
        name="weights_unpack",
    )(shards)
    weights = lax.all_gather(shards, "space", axis=0)

    send, shards = lax.optimization_barrier((send, shards))
    got = exchange(send, "tm")

    mixed = pl.pallas_call(
        forward_kernel,
        out_shape=shape((total, 6, 128), BF16),
        in_specs=[VMEM],
        out_specs=VMEM,
        scratch_shapes=[pltpu.VMEM((total, 6, 128), F32)],
        compiler_params=params(24),
        cost_estimate=pl.CostEstimate(flops=10**8, bytes_accessed=2 * 10**6, transcendentals=2 * 10**5),
        name="temporal_forward",
    )(got)
    mixed = exchange(mixed, both)

    grad_resid, grad_time = pl.pallas_call(
        middle_kernel,
        out_shape=(shape((total, width), BF16), shape((total, 6, 128), BF16)),
        in_specs=[SMEM, HBM, VMEM, HBM, VMEM, SMEM, VMEM, VMEM, VMEM],
        out_specs=(VMEM, VMEM),
        scratch_shapes=[
            pltpu.VMEM((sp, tubes, 2 * width), BF16),
            pltpu.VMEM((inner, inner), BF16),
            pltpu.VMEM((width, width), BF16),
            pltpu.VMEM((sp, 8 * tm, 3 * inner), BF16),
            pltpu.VMEM((sp, 6 * tm, width), BF16),
            pltpu.VMEM((sp, 6 * tm, width), BF16),
            pltpu.VMEM((total, 6, 128), F32),
            pltpu.VMEM((total, 3 * inner), BF16),
            pltpu.VMEM((total, 3 * inner), BF16),
            pltpu.SemaphoreType.DMA((12,)),
        ],
        compiler_params=params(52),
        cost_estimate=pl.CostEstimate(flops=4 * 10**9, bytes_accessed=10**7, transcendentals=2 * 10**5),
        name="middle",
    )(
        me,
        weights,
        mixed,
        rest,
        norm_gain.reshape(1, width),
        bias_slope,
        visible.reshape(total, 1),
        visible.reshape(1, total),
        to_order,
    )
    grad_resid = lax.all_gather(grad_resid, "space", axis=0)
    got, grad_time = lax.optimization_barrier((got, grad_time))
    grad_time = exchange(grad_time, both)
    probs = pl.pallas_call(
        probs_kernel,
        out_shape=shape((HEADS // 2, total, 2 * total), F32),
        in_specs=[VMEM],
        out_specs=VMEM,
        compiler_params=params(24),
        cost_estimate=pl.CostEstimate(flops=10**9, bytes_accessed=4 * 10**6, transcendentals=2 * 10**5),
        name="temporal_probs",
    )(got)

    back = pl.pallas_call(
        backward_kernel,
        out_shape=shape((tm, 3 * steps, inner), BF16),
        in_specs=[VMEM] * 3,
        out_specs=VMEM,
        scratch_shapes=[pltpu.VMEM((total, 6, 128), F32)],
        compiler_params=params(24),
        cost_estimate=pl.CostEstimate(flops=3 * 10**8, bytes_accessed=2 * 10**6, transcendentals=0),
        name="temporal_backward",
    )(got, probs, grad_time)
    back, grad_resid = lax.optimization_barrier((back, grad_resid))
    back = exchange(back, "tm")
    outs = pl.pallas_call(
        unpack_kernel,
        out_shape=(shape(time_query.shape, BF16),) * 3,
        in_specs=[VMEM, VMEM],
        out_specs=(VMEM,) * 3,
        compiler_params=params(24),
        name="unpack",
    )(back, to_steps)
    grad_resid = pl.pallas_call(
        slice_kernel,
        out_shape=shape(residual_in.shape, BF16),
        in_specs=[SMEM, HBM],
        out_specs=VMEM,
        scratch_shapes=[pltpu.SemaphoreType.DMA],
        compiler_params=params(56),
        cost_estimate=pl.CostEstimate(flops=10**9, bytes_accessed=4 * 10**6, transcendentals=0),
        name="slice",
    )(me, grad_resid)
    return (grad_resid, *outs)


def solution(mesh):
    token = P("dp", "tm", "space", None)
    row = P(("tm", "space"), None)
    in_specs = (token, token, token, token, row, P(), row, row, P(), P("dp", None), token)
    return jax.shard_map(
        body, mesh=mesh, in_specs=in_specs, out_specs=(token,) * 4, check_vma=False
    )
```
